32 devices in a mesh: dp: 16 (over z, x, core), seq: 2 (over y).
Axes of the slice: x: 2, y: 2, z: 4, core: 2. Of those that a mesh axis runs over, the one named last changes fastest.
Arguments:
- tokens: bfloat16 [32, 1024, 768], P('dp', 'seq'), may hold values from -6 to 6
- segments: int32 [32, 1024], P('dp', 'seq'), may hold values from 0 to 7, as said below
- cotangent: bfloat16 [32, 1024, 768], P('dp', 'seq'), may hold values from -21 to 21
- gain_attn: float32 [768], replicated, may hold values from 0.25 to 1.75
- w_qkv: bfloat16 [768, 2304], replicated, may hold values from -0.21875 to 0.21875
- w_out: bfloat16 [768, 768], replicated, may hold values from -2.5 to 2.5
- gain_ffn: float32 [768], replicated, may hold values from 0.25 to 1.75
- w_up: bfloat16 [768, 3072], replicated, may hold values from -0.21875 to 0.21875
- w_down: bfloat16 [3072, 768], replicated, may hold values from -0.109375 to 0.109375
Outputs:
- outputs: bfloat16 [32, 1024, 768], P('dp', 'seq')
- grad_tokens: bfloat16 [32, 1024, 768], P('dp', 'seq')
- grad_w_qkv: float32 [768, 2304], P(('dp', 'seq'))
- grad_w_out: float32 [768, 768], P(('dp', 'seq'))
- grad_w_up: float32 [768, 3072], P(('dp', 'seq'))
- grad_w_down: float32 [3072, 768], P(('dp', 'seq'))
- grad_gain_attn: float32 [768], P(('dp', 'seq'))
- grad_gain_ffn: float32 [768], P(('dp', 'seq'))
The draws below stay inside these ranges and needn't reach their ends.
Inputs may be any that keep to these rules, and one draw needn't show every extreme that they name: `segments`: within each window the ids never fall, start at 0 at its first position and end at 7 at its last.
All inputs are finite; a program needn't handle non-finite values.
Results may differ from the reference program's by a relative error of at most 0.012.
Values may be sent and summed in bfloat16 or wider, within the bound.
No kernel may reach another device: no remote copies, remote signals or barrier semaphores. Data moves between devices by JAX's collectives and lax.ppermute only.
A program may use at most 384 MiB of HBM per device.

```python
import jax
import jax.numpy as jnp
from jax import lax

D = 768
HEADS = 24
HEAD_DIM = 32
FF = 3072
LEN = 1024
WINDOWS = 32


def draw_segments(key, part):
    key = jax.random.fold_in(key, 7)
    quarter = LEN // 4

    def one_window(subkey):
        early_key, late_key = jax.random.split(subkey)
        early_marks = jax.random.permutation(early_key, quarter - 1)[:4] + 1
        late_marks = jax.random.permutation(late_key, quarter)[:3] + 3 * quarter
        boundary = jnp.zeros((LEN,), jnp.int32).at[early_marks].set(1).at[late_marks].set(1)
        return jnp.cumsum(boundary).astype(jnp.int32)
    return jax.vmap(one_window)(jax.random.split(key, WINDOWS))


def draw_cotangent(key, part):
    key = jax.random.fold_in(key, 11)
    noise_key = jax.random.fold_in(key, 0)
    window_rise = 3.0 ** (jnp.arange(WINDOWS, dtype=jnp.float32) / max(WINDOWS - 1, 1))
    base_noise = jnp.clip(jax.random.normal(noise_key, (WINDOWS, LEN, D), jnp.float32), -4.0, 4.0)
    return (base_noise * window_rise[:, None, None]).astype(jnp.bfloat16)


def level_of(stream_key, extent, cuts, low, top_value):
    loudness = 1.0
    for dim, parts in cuts:
        heights = jax.random.uniform(jax.random.fold_in(jax.random.fold_in(stream_key, 6), dim), (parts,), jnp.float32, low / len(cuts), top_value / len(cuts))
        loudness = loudness * jnp.repeat(jnp.exp(heights), extent[dim] // parts).reshape((-1,) + (1,) * (len(extent) - 1 - dim))
    return loudness


def noise(key, dims, width, reach, pieces=(), kind=jnp.bfloat16):
    array = width * jax.random.normal(key, dims, jnp.float32)
    if pieces:
        array = array * level_of(key, dims, pieces, -0.22, 0.18)
    return jnp.clip(array, -reach, reach).astype(kind)


def setup_inputs(seed: int = 0) -> dict:
    splits = jax.random.split(jax.random.key(seed), 10)
    tokens = noise(splits[0], (WINDOWS, LEN, D), 1.0, 6.0, ((0, 16), (1, 2)))
    segments = draw_segments(jax.random.fold_in(splits[9], 71), 0)
    cotangent = draw_cotangent(jax.random.fold_in(splits[9], 71), 0)
    gain_attn = jnp.clip(1.0 + 0.15 * jax.random.normal(splits[3], (D,), jnp.float32), 0.25, 1.75)
    w_qkv = noise(splits[4], (D, 3 * D), D ** -0.5, 0.21875)
    w_out = noise(splits[5], (D, D), (D // 128) ** -0.5, 2.5)
    gain_ffn = jnp.clip(1.0 + 0.15 * jax.random.normal(splits[6], (D,), jnp.float32), 0.25, 1.75)
    w_up = noise(splits[7], (D, FF), D ** -0.5, 0.21875)
    w_down = noise(splits[8], (FF, D), FF ** -0.5, 0.109375)
    return dict(tokens=tokens, segments=segments, cotangent=cotangent, gain_attn=gain_attn, w_qkv=w_qkv, w_out=w_out, gain_ffn=gain_ffn, w_up=w_up, w_down=w_down)


@jax.custom_vjp
def low(v):
    return lax.optimization_barrier(v.astype(jnp.bfloat16)).astype(jnp.float32)

@jax.custom_vjp
def low_back(v):
    return v

def low_keep(v):
    return (low(v), None)

def low_pass(kept, grad):
    return (grad,)

def back_keep(v):
    return (v, None)

def back_low(kept, grad):
    return (low(grad),)
low.defvjp(low_keep, low_pass)
low_back.defvjp(back_keep, back_low)
epsilon = 1e-05
masked_score = -1e+30
highest = lax.Precision.HIGHEST

def norm_gain(values, gain_vector):
    row_mean = lax.optimization_barrier(jnp.mean(values, axis=-1, keepdims=True))
    centred = values - row_mean
    variance = lax.optimization_barrier(jnp.mean(centred * centred, axis=-1, keepdims=True))
    return centred * lax.rsqrt(variance + epsilon) * gain_vector

def window_layer(weights, packed):
    inputs, segment_ids = packed
    gain_attn, w_qkv, w_out, gain_ffn, w_up, w_down = weights
    normed_one = low(norm_gain(inputs, gain_attn))
    project = low_back(low(jnp.dot(normed_one, w_qkv, precision=highest)))
    queries = project[:, :D].reshape(LEN, HEADS, HEAD_DIM)
    keys_all = project[:, D:2 * D].reshape(LEN, HEADS, HEAD_DIM)
    values_all = project[:, 2 * D:].reshape(LEN, HEADS, HEAD_DIM)
    scores = jnp.einsum('qhd,khd->hqk', queries, keys_all, precision=highest) * HEAD_DIM ** (-0.5)
    positions = jnp.arange(LEN)
    allowed = (positions[None, :] <= positions[:, None]) & (segment_ids[:, None] == segment_ids[None, :])
    scores = low_back(jnp.where(allowed[None], scores, masked_score))
    row_max = lax.optimization_barrier(jnp.max(scores, axis=-1, keepdims=True))
    exponent = jnp.exp(scores - row_max)
    soft_weights = low(exponent / lax.optimization_barrier(jnp.sum(exponent, axis=-1, keepdims=True)))
    mixture = jnp.einsum('hqk,khd->qhd', soft_weights, values_all, precision=highest).reshape(LEN, D)
    mixture = low_back(low(mixture))
    middle = inputs + low_back(jnp.dot(mixture, w_out, precision=highest))
    normed_two = low(norm_gain(middle, gain_ffn))
    up_proj = low_back(jnp.dot(normed_two, w_up, precision=highest))
    activated = low(jax.nn.gelu(up_proj))
    return middle + low_back(jnp.dot(activated, w_down, precision=highest))

def reference(tokens, segments, cotangent, gain_attn, w_qkv, w_out, gain_ffn, w_up, w_down):
    checked_layer = jax.checkpoint(window_layer)

    def forward(inputs, gain_one, weight_qkv, weight_out, gain_two, weight_up, weight_down):
        weights = (gain_one, weight_qkv, weight_out, gain_two, weight_up, weight_down)
        return lax.map(lambda packed: checked_layer(weights, packed), (inputs, segments))
    floats = (tokens.astype(jnp.float32), gain_attn.astype(jnp.float32), w_qkv.astype(jnp.float32), w_out.astype(jnp.float32), gain_ffn.astype(jnp.float32), w_up.astype(jnp.float32), w_down.astype(jnp.float32))
    outputs, pullback = jax.vjp(forward, *floats)
    gradients = pullback(cotangent.astype(jnp.float32))
    return (outputs.astype(jnp.bfloat16), gradients[0].astype(jnp.bfloat16), gradients[2], gradients[3], gradients[5], gradients[6], gradients[1], gradients[4])
```

```python
import functools

import jax
import jax.numpy as jnp
from jax import lax
from jax.experimental import pallas as pl
from jax.experimental.pallas import tpu as pltpu
from jax.sharding import PartitionSpec as P

HEAD_DIM = 32
GROUP = 8
LANES = GROUP * HEAD_DIM
GRAIN = 128
masked_score = -1e30
SCALE = HEAD_DIM ** (-0.5)
SCALE2 = SCALE * 1.4426950408889634
NT = (((1,), (1,)), ((), ()))
NN = (((1,), (0,)), ((), ()))


def mm(a, b, dims=NN):
    return lax.dot_general(a, b, dims, preferred_element_type=jnp.float32)


def attend_kernel(first, seg_ref, q_ref, k_ref, v_ref, o_ref, lse_ref, bias, total, *, bq, unroll):
    i, g = pl.program_id(0), pl.program_id(1)
    length = k_ref.shape[0]
    start = first[i]
    lane = lax.div(lax.broadcasted_iota(jnp.int32, (1, LANES), 1), HEAD_DIM)
    lane_head = lax.broadcasted_iota(jnp.int32, (1, 128), 1)

    def span(width):
        begin = pl.multiple_of(start * GRAIN, GRAIN)

        @pl.when(g == 0)
        def _():
            seg_q = jnp.transpose(jnp.broadcast_to(seg_ref[0:1, pl.ds(pl.multiple_of(i * bq, bq), bq)], (128, bq)))[:, 0:1]
            place_q = i * bq + lax.broadcasted_iota(jnp.int32, (bq, width), 0)
            place_k = begin + lax.broadcasted_iota(jnp.int32, (bq, width), 1)
            allowed = (place_k <= place_q) & (seg_q == seg_ref[0:1, pl.ds(begin, width)])
            bias[:, :width] = jnp.where(allowed, 0.0, masked_score)

        total[...] = jnp.zeros_like(total)

        def head(h, logs):
            query = jnp.where(lane == h, q_ref[...], jnp.zeros((), jnp.bfloat16))
            s = mm(query, k_ref[pl.ds(begin, width), :], NT) * SCALE2 + bias[:, :width]
            top = jnp.max(s, axis=-1, keepdims=True)
            e = jnp.exp2(s - top)
            row = jnp.sum(e, axis=-1, keepdims=True)
            out = mm(e.astype(jnp.bfloat16), v_ref[pl.ds(begin, width), :])
            total[...] = jnp.where(lane == h, out / row, total[...])
            return jnp.where(lane_head == h, top + jnp.log2(row), logs)

        logs = lax.fori_loop(0, GROUP, head, jnp.zeros((bq, 128), jnp.float32), unroll=unroll)
        o_ref[...] = total[...].astype(o_ref.dtype)
        lse_ref[...] = jnp.transpose(logs)[:GROUP]

    blocks = (i + 1) * (bq // GRAIN) - start
    for count in range(bq // GRAIN, length // GRAIN + 1):
        pl.when(blocks == count)(functools.partial(span, count * GRAIN))


def attend(first, seg, proj, bq=256, unroll=2):
    length, width = proj.shape
    groups = width // 3 // LANES
    grid_spec = pltpu.PrefetchScalarGridSpec(
        num_scalar_prefetch=1,
        grid=(length // bq, groups),
        in_specs=[
            pl.BlockSpec((1, length), lambda i, g, *_: (0, 0)),
            pl.BlockSpec((bq, LANES), lambda i, g, *_: (i, g)),
            pl.BlockSpec((length, LANES), lambda i, g, *_: (0, groups + g)),
            pl.BlockSpec((length, LANES), lambda i, g, *_: (0, 2 * groups + g)),
        ],
        out_specs=[
            pl.BlockSpec((bq, LANES), lambda i, g, *_: (i, g)),
            pl.BlockSpec((GROUP, bq), lambda i, g, *_: (g, i)),
        ],
        scratch_shapes=[pltpu.VMEM((bq, length), jnp.float32), pltpu.VMEM((bq, LANES), jnp.float32)],
    )
    return pl.pallas_call(
        functools.partial(attend_kernel, bq=bq, unroll=unroll),
        grid_spec=grid_spec,
        out_shape=[
            jax.ShapeDtypeStruct((length, width // 3), jnp.bfloat16),
            jax.ShapeDtypeStruct((groups * GROUP, length), jnp.float32),
        ],
        compiler_params=pltpu.CompilerParams(vmem_limit_bytes=48 << 20),
        name="attend",
    )(first, seg, proj, proj, proj)


def attend_back_kernel(last, seg_ref, q_ref, k_ref, v_ref, up_ref, o_ref, lse_ref, gq_ref, gk_ref, gv_ref,
                       bias, inner, logs, key_t, gq_t, gk, gv, *, bk, unroll):
    g, j = pl.program_id(0), pl.program_id(1)
    length = q_ref.shape[0]
    lane = lax.div(lax.broadcasted_iota(jnp.int32, (1, LANES), 1), HEAD_DIM)

    @pl.when(j == 0)
    def _():
        gq_t[...] = jnp.zeros_like(gq_t)
        pick = (lax.div(lax.broadcasted_iota(jnp.int32, (GROUP, LANES), 1), HEAD_DIM)
                == lax.broadcasted_iota(jnp.int32, (GROUP, LANES), 0)).astype(jnp.float32)
        product = up_ref[...].astype(jnp.float32) * o_ref[...].astype(jnp.float32)
        totals = lax.dot_general(pick, product, NT, precision=lax.Precision.HIGHEST,
                                 preferred_element_type=jnp.float32)
        for h in range(GROUP):
            inner[h] = totals[h:h + 1]
            logs[h] = lse_ref[h:h + 1]

    key_t[...] = jnp.transpose(k_ref[...])

    def span(width):
        begin = pl.multiple_of(j * bk, bk)
        here = pl.ds(begin, width)
        seg_k = jnp.transpose(jnp.broadcast_to(seg_ref[0:1, pl.ds(begin, bk)], (128, bk)))[:, 0:1]
        place_k = lax.broadcasted_iota(jnp.int32, (bk, width), 0)
        place_q = lax.broadcasted_iota(jnp.int32, (bk, width), 1)
        allowed = (place_k <= place_q) & (seg_k == seg_ref[0:1, here])
        bias[:, :width] = jnp.where(allowed, 0.0, masked_score)

        def head(h, carry):
            zero = jnp.zeros((), jnp.bfloat16)
            key = jnp.where(lane == h, k_ref[...], zero)
            value = jnp.where(lane == h, v_ref[...], zero)
            s = mm(key, q_ref[here, :], NT) * SCALE2 + (bias[:, :width] - logs[h, :, here])
            p = jnp.exp2(s)
            dp = mm(value, up_ref[here, :], NT)
            ds = (p * (dp - inner[h, :, here])).astype(jnp.bfloat16)
            gv[...] = jnp.where(lane == h, mm(p.astype(jnp.bfloat16), up_ref[here, :]), gv[...])
            gk[...] = jnp.where(lane == h, mm(ds, q_ref[here, :]), gk[...])
            rows = pl.ds(pl.multiple_of(h * HEAD_DIM, HEAD_DIM), HEAD_DIM)
            gq_t[rows, here] += mm(key_t[rows, :], ds)
            return carry

        lax.fori_loop(0, GROUP, head, 0, unroll=unroll)

    blocks = last[j] - j * (bk // GRAIN)
    for count in range(bk // GRAIN, length // GRAIN + 1):
        pl.when(blocks == count)(functools.partial(span, count * GRAIN))

    gk_ref[...] = (gk[...] * SCALE).astype(gk_ref.dtype)
    gv_ref[...] = gv[...].astype(gv_ref.dtype)

    @pl.when(j == pl.num_programs(1) - 1)
    def _():
        gq_ref[...] = jnp.transpose((gq_t[...] * SCALE).astype(gq_ref.dtype))


def attend_back(last, seg, proj, up, o, lse, bk=256, unroll=2):
    length, width = proj.shape
    groups = width // 3 // LANES
    whole = lambda at: pl.BlockSpec((length, LANES), lambda g, j, *_: (0, at(g)))
    block = lambda at: pl.BlockSpec((bk, LANES), lambda g, j, *_: (j, at(g)))
    grid_spec = pltpu.PrefetchScalarGridSpec(
        num_scalar_prefetch=1,
        grid=(groups, length // bk),
        in_specs=[
            pl.BlockSpec((1, length), lambda g, j, *_: (0, 0)),
            whole(lambda g: g),
            block(lambda g: groups + g),
            block(lambda g: 2 * groups + g),
            whole(lambda g: g),
            whole(lambda g: g),
            pl.BlockSpec((GROUP, length), lambda g, j, *_: (g, 0)),
        ],
        out_specs=[whole(lambda g: g), block(lambda g: g), block(lambda g: g)],
        scratch_shapes=[
            pltpu.VMEM((bk, length), jnp.float32),
            pltpu.VMEM((GROUP, 1, length), jnp.float32),
            pltpu.VMEM((GROUP, 1, length), jnp.float32),
            pltpu.VMEM((LANES, bk), jnp.bfloat16),
            pltpu.VMEM((LANES, length), jnp.float32),
            pltpu.VMEM((bk, LANES), jnp.float32),
            pltpu.VMEM((bk, LANES), jnp.float32),
        ],
    )
    out = jax.ShapeDtypeStruct((length, width // 3), jnp.bfloat16)
    return pl.pallas_call(
        functools.partial(attend_back_kernel, bk=bk, unroll=unroll),
        grid_spec=grid_spec,
        out_shape=[out, out, out],
        compiler_params=pltpu.CompilerParams(vmem_limit_bytes=48 << 20),
        name="attend_back",
    )(last, seg, proj, proj, proj, up, o, lse)


def bounds(seg, bq, bk):
    length = seg.shape[1]
    row = seg[0]
    first = jnp.sum(row[None, :] < row[::bq][:, None], axis=1) // GRAIN
    last = (jnp.sum(row[None, :] <= row[bk - 1::bk][:, None], axis=1) + GRAIN - 1) // GRAIN
    return first.astype(jnp.int32), last.astype(jnp.int32)

epsilon = 1e-05


def norm_gain(values, gain_vector):
    row_mean = jnp.mean(values, axis=-1, keepdims=True)
    centred = values - row_mean
    variance = jnp.mean(centred * centred, axis=-1, keepdims=True)
    return centred * lax.rsqrt(variance + epsilon) * gain_vector


def swapped(block):
    return lax.ppermute(block, "seq", [(0, 1), (1, 0)])


def gather_window(block):
    place = lax.axis_index("seq")
    kept = lax.dynamic_index_in_dim(block, place, 0, keepdims=False)
    other = swapped(lax.dynamic_index_in_dim(block, 1 - place, 0, keepdims=False))
    return jnp.where(place == 0, jnp.concatenate([kept, other]), jnp.concatenate([other, kept]))


def spread_window(rows):
    place = lax.axis_index("seq")
    halves = rows.reshape(2, rows.shape[0] // 2, rows.shape[1])
    kept = lax.dynamic_index_in_dim(halves, place, 0, keepdims=False)
    other = swapped(lax.dynamic_index_in_dim(halves, 1 - place, 0, keepdims=False))
    return jnp.where(place == 0, jnp.stack([kept, other]), jnp.stack([other, kept]))


def body(tokens, segments, cotangent, gain_attn, w_qkv, w_out, gain_ffn, w_up, w_down):
    bf16 = jnp.bfloat16
    inputs = gather_window(tokens).astype(jnp.float32)
    seg = gather_window(segments)[None]
    upstream = gather_window(cotangent)
    first, last = bounds(seg, 256, 256)
    normed_one, norm_one_pull = jax.vjp(norm_gain, inputs, gain_attn)
    low_one = normed_one.astype(bf16)
    proj = mm(low_one, w_qkv).astype(bf16)
    mixture, lse = attend(first, seg, proj, bq=256, unroll=8)
    middle = inputs + mm(mixture, w_out)
    normed_two, norm_two_pull = jax.vjp(norm_gain, middle, gain_ffn)
    low_two = normed_two.astype(bf16)
    up_proj = mm(low_two, w_up)
    activated, gelu_pull = jax.vjp(jax.nn.gelu, up_proj)
    low_three = activated.astype(bf16)
    outputs = (middle + mm(low_three, w_down)).astype(bf16)
    grad_w_down = mm(low_three.T, upstream)
    grad_active = mm(upstream, w_down.T)
    grad_up = gelu_pull(grad_active)[0].astype(bf16)
    grad_w_up = mm(low_two.T, grad_up)
    grad_norm_two = mm(grad_up, w_up.T)
    grad_middle_norm, grad_gain_ffn = norm_two_pull(grad_norm_two)
    grad_middle = upstream.astype(jnp.float32) + grad_middle_norm
    grad_branch = grad_middle.astype(bf16)
    grad_w_out = mm(mixture.T, grad_branch)
    grad_mixture = mm(grad_branch, w_out.T).astype(bf16)
    grad_project = jnp.concatenate(
        attend_back(last, seg, proj, grad_mixture, mixture, lse, bk=256, unroll=4), axis=1
    )
    grad_w_qkv = mm(low_one.T, grad_project)
    grad_norm_one = mm(grad_project, w_qkv.T)
    grad_input_norm, grad_gain_attn = norm_one_pull(grad_norm_one)
    grad_inputs = (grad_middle + grad_input_norm).astype(bf16)
    summed = [
        lax.psum_scatter(grad, ("dp", "seq"), scatter_dimension=0, tiled=True)
        for grad in (grad_w_qkv, grad_w_out, grad_w_up, grad_w_down, grad_gain_attn, grad_gain_ffn)
    ]
    return (spread_window(outputs), spread_window(grad_inputs), *summed)


def solution(mesh):
    placed = (
        P("dp", "seq", None),
        P("dp", "seq"),
        P("dp", "seq", None),
        P(),
        P(),
        P(),
        P(),
        P(),
        P(),
    )
    return jax.shard_map(
        body,
        mesh=mesh,
        in_specs=placed,
        out_specs=(
            P("dp", "seq", None),
            P("dp", "seq", None),
            P(("dp", "seq"), None),
            P(("dp", "seq"), None),
            P(("dp", "seq"), None),
            P(("dp", "seq"), None),
            P(("dp", "seq")),
            P(("dp", "seq")),
        ),
        check_vma=False,
    )
```

```python
import functools

import jax
import jax.numpy as jnp
from jax import lax
from jax.experimental import pallas as pl
from jax.experimental.pallas import tpu as pltpu
from jax.sharding import PartitionSpec as P

HEAD_DIM = 32
GROUP = 8
LANES = GROUP * HEAD_DIM
SMALL = 128
PART = 3 * SMALL
GRAIN = 128
masked_score = -1e30
epsilon = 1e-05
SCALE = HEAD_DIM ** (-0.5)
SCALE2 = SCALE * 1.4426950408889634
NT = (((1,), (1,)), ((), ()))
NN = (((1,), (0,)), ((), ()))


def mm(a, b, dims=NN):
    return lax.dot_general(a, b, dims, preferred_element_type=jnp.float32)


def attend_kernel(first, seg_ref, q_ref, k_ref, v_ref, o_ref, lse_ref, bias, total, *, bq, unroll):
    i, g = pl.program_id(0), pl.program_id(1)
    length = k_ref.shape[0]
    start = first[i]
    lane = lax.div(lax.broadcasted_iota(jnp.int32, (1, LANES), 1), HEAD_DIM)
    lane_head = lax.broadcasted_iota(jnp.int32, (1, 128), 1)

    def span(width):
        begin = pl.multiple_of(start * GRAIN, GRAIN)

        @pl.when(g == 0)
        def _():
            seg_q = jnp.transpose(jnp.broadcast_to(seg_ref[0:1, pl.ds(pl.multiple_of(i * bq, bq), bq)], (128, bq)))[:, 0:1]
            place_q = i * bq + lax.broadcasted_iota(jnp.int32, (bq, width), 0)
            place_k = begin + lax.broadcasted_iota(jnp.int32, (bq, width), 1)
            allowed = (place_k <= place_q) & (seg_q == seg_ref[0:1, pl.ds(begin, width)])
            bias[:, :width] = jnp.where(allowed, 0.0, masked_score)

        total[...] = jnp.zeros_like(total)

        def head(h, logs):
            query = jnp.where(lane == h, q_ref[...], jnp.zeros((), jnp.bfloat16))
            s = mm(query, k_ref[pl.ds(begin, width), :], NT) * SCALE2 + bias[:, :width]
            top = jnp.max(s, axis=-1, keepdims=True)
            e = jnp.exp2(s - top)
            row = jnp.sum(e, axis=-1, keepdims=True)
            out = mm(e.astype(jnp.bfloat16), v_ref[pl.ds(begin, width), :])
            total[...] = jnp.where(lane == h, out / row, total[...])
            place = jnp.where(h < GROUP // 2, h, h + GROUP // 2)
            return jnp.where(lane_head == place, top + jnp.log2(row), logs)

        logs = lax.fori_loop(0, GROUP, head, jnp.zeros((bq, 128), jnp.float32), unroll=unroll)
        o_ref[...] = total[...].astype(o_ref.dtype)
        lse_ref[...] = jnp.transpose(logs)[:2 * GROUP]

    blocks = (i + 1) * (bq // GRAIN) - start
    for count in range(bq // GRAIN, length // GRAIN + 1):
        pl.when(blocks == count)(functools.partial(span, count * GRAIN))


def attend(first, seg, proj, bq=256, unroll=8):
    length, width = proj.shape
    groups = width // 3 // LANES
    grid_spec = pltpu.PrefetchScalarGridSpec(
        num_scalar_prefetch=1,
        grid=(length // bq, groups),
        in_specs=[
            pl.BlockSpec((1, length), lambda i, g, *_: (0, 0)),
            pl.BlockSpec((bq, LANES), lambda i, g, *_: (i, g)),
            pl.BlockSpec((length, LANES), lambda i, g, *_: (0, groups + g)),
            pl.BlockSpec((length, LANES), lambda i, g, *_: (0, 2 * groups + g)),
        ],
        out_specs=[
            pl.BlockSpec((bq, LANES), lambda i, g, *_: (i, g)),
            pl.BlockSpec((2 * GROUP, bq), lambda i, g, *_: (g, i)),
        ],
        scratch_shapes=[pltpu.VMEM((bq, length), jnp.float32), pltpu.VMEM((bq, LANES), jnp.float32)],
    )
    return pl.pallas_call(
        functools.partial(attend_kernel, bq=bq, unroll=unroll),
        grid_spec=grid_spec,
        out_shape=[
            jax.ShapeDtypeStruct((length, width // 3), jnp.bfloat16),
            jax.ShapeDtypeStruct((groups * 2 * GROUP, length), jnp.float32),
        ],
        compiler_params=pltpu.CompilerParams(vmem_limit_bytes=60 << 20),
        cost_estimate=pl.CostEstimate(flops=28 << 30, bytes_accessed=8 << 20, transcendentals=24 * length * length),
        name="attend",
    )(first, seg, proj, proj, proj)


def attend_back_kernel(last, seg_ref, q_ref, k_ref, v_ref, up_ref, o_ref, lse_ref, low_t_ref, *refs, bk):
    *riders, gq_ref, gk_ref, gv_ref, keep_ref, send_ref, bias, inner, key_t, value_t, q_t, up_t, gq_t, gk, gv = refs
    g, j = pl.program_id(0), pl.program_id(1)
    length, lanes = q_ref.shape
    heads = lanes // HEAD_DIM
    lane = lax.div(lax.broadcasted_iota(jnp.int32, (1, lanes), 1), HEAD_DIM)

    @pl.when(j == 0)
    def _():
        gq_t[...] = jnp.zeros_like(gq_t)
        q_t[...] = jnp.transpose(q_ref[...])
        up_t[...] = jnp.transpose(up_ref[...])
        pick = (lax.div(lax.broadcasted_iota(jnp.int32, (8, lanes), 1), HEAD_DIM)
                == lax.broadcasted_iota(jnp.int32, (8, lanes), 0)).astype(jnp.float32)
        product = up_ref[...].astype(jnp.float32) * o_ref[...].astype(jnp.float32)
        inner[...] = lax.dot_general(pick, product, NT, precision=lax.Precision.HIGHEST,
                                     preferred_element_type=jnp.float32)

    key_t[...] = jnp.transpose(k_ref[...])
    value_t[...] = jnp.transpose(v_ref[...])

    def span(width):
        begin = pl.multiple_of(j * bk, bk)
        here = pl.ds(begin, width)
        seg_k = jnp.transpose(jnp.broadcast_to(seg_ref[0:1, pl.ds(begin, bk)], (128, bk)))[:, 0:1]
        place_k = lax.broadcasted_iota(jnp.int32, (bk, width), 0)
        place_q = lax.broadcasted_iota(jnp.int32, (bk, width), 1)
        allowed = (place_k <= place_q) & (seg_k == seg_ref[0:1, here])
        bias[:, :width] = jnp.where(allowed, 0.0, masked_score)
        for h in range(heads):
            rows = slice(h * HEAD_DIM, (h + 1) * HEAD_DIM)
            key, value = jnp.transpose(key_t[rows, :]), jnp.transpose(value_t[rows, :])
            s = mm(key, q_t[rows, here]) * SCALE2 + (bias[:, :width] - lse_ref[h:h + 1, here])
            p = jnp.exp2(s)
            dp = mm(value, up_t[rows, here])
            ds = (p * (dp - inner[h:h + 1, here])).astype(jnp.bfloat16)
            grad_v = mm(p.astype(jnp.bfloat16), up_ref[here, :])
            grad_k = mm(ds, q_ref[here, :])
            gv[...] = jnp.where(lane == h, grad_v, gv[...]) if h else grad_v
            gk[...] = jnp.where(lane == h, grad_k, gk[...]) if h else grad_k
            gq_t[rows, here] += mm(key_t[rows, :], ds)

    blocks = last[j] - j * (bk // GRAIN)
    for count in range(bk // GRAIN, length // GRAIN + 1):
        pl.when(blocks == count)(functools.partial(span, count * GRAIN))

    here = pl.ds(pl.multiple_of(j * bk, bk), bk)
    gk_ref[here, :] = (gk[...] * SCALE).astype(gk_ref.dtype)
    gv_ref[here, :] = gv[...].astype(gv_ref.dtype)

    @pl.when(j == pl.num_programs(1) - 1)
    def _():
        gq_ref[...] = jnp.transpose((gq_t[...] * SCALE).astype(gq_ref.dtype))
        joined = jnp.concatenate([gq_ref[...], gk_ref[...], gv_ref[...]], axis=1)
        cut(mm(low_t_ref[...], joined), keep_ref, send_ref, g)

    if riders:
        @pl.when((g == 0) & (j == 0))
        def _():
            extra = riders[0].shape[0]
            for rider, target in zip(riders, (keep_ref, send_ref)):
                target[-extra:] = rider[...]


def attend_back(begin, count, last, seg, proj, up, o, lse, low_t, shards, riders=(), bk=256):
    length, width = proj.shape
    groups = width // 3 // SMALL
    half = width // 6
    group = lambda g: g + begin
    whole = lambda offset: pl.BlockSpec((length, SMALL), lambda g, j, *_: (0, offset + group(g)))
    block = lambda offset: pl.BlockSpec((bk, SMALL), lambda g, j, *_: (j, offset + group(g)))
    fixed = lambda *shape: pl.BlockSpec(shape, lambda g, j, *_: (0, 0), pipeline_mode=pl.Buffered(1))
    out = pl.BlockSpec((length, SMALL), lambda g, j, *_: (0, g))
    rows = 2 * half // shards
    piece = (half, PART) if rows % 8 else (shards // 2, rows, PART)
    lead = count + (riders[0].shape[0] if riders else 0)
    all_of = lambda *size: pl.BlockSpec(size, lambda g, j, *_: (0,) * len(size), pipeline_mode=pl.Buffered(1))
    split = all_of(lead, *piece)
    grid_spec = pltpu.PrefetchScalarGridSpec(
        num_scalar_prefetch=1,
        grid=(count, length // bk),
        in_specs=[
            fixed(1, length),
            whole(0),
            block(groups),
            block(2 * groups),
            whole(0),
            whole(0),
            pl.BlockSpec((8, length), lambda g, j, *_: (group(g), 0)),
            fixed(2 * half, length),
            *[all_of(*rider.shape) for rider in riders],
        ],
        out_specs=[out, out, out, split, split],
        scratch_shapes=[
            pltpu.VMEM((bk, length), jnp.float32),
            pltpu.VMEM((8, length), jnp.float32),
            pltpu.VMEM((SMALL, bk), jnp.bfloat16),
            pltpu.VMEM((SMALL, bk), jnp.bfloat16),
            pltpu.VMEM((SMALL, length), jnp.bfloat16),
            pltpu.VMEM((SMALL, length), jnp.bfloat16),
            pltpu.VMEM((SMALL, length), jnp.float32),
            pltpu.VMEM((bk, SMALL), jnp.float32),
            pltpu.VMEM((bk, SMALL), jnp.float32),
        ],
    )
    heads = jax.ShapeDtypeStruct((length, count * SMALL), jnp.bfloat16)
    parts = jax.ShapeDtypeStruct((lead, *piece), jnp.bfloat16)
    return pl.pallas_call(
        functools.partial(attend_back_kernel, bk=bk),
        grid_spec=grid_spec,
        out_shape=[heads, heads, heads, parts, parts],
        compiler_params=pltpu.CompilerParams(vmem_limit_bytes=60 << 20),
        cost_estimate=pl.CostEstimate(flops=(count * 10) << 30, bytes_accessed=8 << 20, transcendentals=count * 4 * length * length),
        name="attend_back",
    )(last, seg, proj, proj, proj, up, o, lse, low_t, *riders)


def bounds(seg, bq, bk):
    row = seg[0]
    first = jnp.sum(row[None, :] < row[::bq][:, None], axis=1) // GRAIN
    last = (jnp.sum(row[None, :] <= row[bk - 1::bk][:, None], axis=1) + GRAIN - 1) // GRAIN
    return first.astype(jnp.int32), last.astype(jnp.int32)


def gelu_pair(u):
    c = 0.7978845608028654
    square = u * u
    t = jnp.tanh(u * (c + (c * 0.044715) * square))
    half = 0.5 * t + 0.5
    slope = half + (0.5 * u) * (1.0 - t * t) * (c + (3 * c * 0.044715) * square)
    return u * half, slope


def row_stats(values):
    mean = jnp.mean(values, axis=-1, keepdims=True)
    centred = values - mean
    return mean, lax.rsqrt(jnp.mean(centred * centred, axis=-1, keepdims=True) + epsilon)


def norm_back(values, gain, upstream):
    mean, rate = row_stats(values)
    unit = (values - mean) * rate
    inner = upstream * gain
    level = jnp.mean(inner, axis=-1, keepdims=True)
    along = jnp.mean(inner * unit, axis=-1, keepdims=True)
    return rate * (inner - level - unit * along)


def shard_at(place, core_rel, q_rel):
    core, q = place[0] ^ core_rel, place[1] ^ q_rel
    return ((q >> 1) * 2 + core) * 2 + (q & 1)


def arranged(place, rows, source, target, shards):
    if rows % 8:
        target[...] = source[...].astype(target.dtype)
        return
    chips = shards // 2
    for at in range(0, shards, 2):
        pair = [
            source[pl.ds(pl.multiple_of(shard_at(place, b // chips, b % chips) * rows, 8), rows), :]
            for b in (at, at + 1)
        ]
        target[at * rows:(at + 2) * rows, :] = jnp.concatenate(pair).astype(target.dtype)


def cut(grad, keep, send, first):
    half = grad.shape[0] // 2
    for at in range(grad.shape[1] // PART):
        block = grad[:, at * PART:(at + 1) * PART]
        if len(keep.shape) == 3:
            keep[first + at] = block[:half].astype(keep.dtype)
            send[first + at] = block[half:].astype(send.dtype)
        else:
            chips, rows = keep.shape[1:3]
            for q in range(chips):
                keep[first + at, q] = block[q * rows:(q + 1) * rows].astype(keep.dtype)
                send[first + at, q] = block[half + q * rows:half + (q + 1) * rows].astype(send.dtype)


def before_kernel(place, x_ref, gain_ref, w_ref, *refs, shards, block):
    proj_ref, low_t_ref, low, flat = refs[-4:]
    length, width = x_ref.shape

    @pl.when(pl.program_id(0) == 0)
    def _():
        for at in range(0, length, block):
            at = slice(at, at + block)
            values = x_ref[at, :].astype(jnp.float32)
            mean, rate = row_stats(values)
            normed = (values - mean) * rate * gain_ref[...]
            low[at, :] = normed.astype(jnp.bfloat16)
            flat[:, at] = jnp.transpose(normed)
        arranged(place, width // shards, flat, low_t_ref, shards)

    proj_ref[...] = mm(low[...], w_ref[...]).astype(jnp.bfloat16)


def before(place, x, gain, w, shards, so_far=(), chunk=768, block=256):
    length, width = x.shape
    columns = w.shape[1]
    whole = lambda *shape: pl.BlockSpec(shape, lambda c, *_: (0, 0), pipeline_mode=pl.Buffered(1))
    grid_spec = pltpu.PrefetchScalarGridSpec(
        num_scalar_prefetch=1,
        grid=(columns // chunk,),
        in_specs=[whole(length, width), whole(1, width), pl.BlockSpec((width, chunk), lambda c, *_: (0, c))]
        + [pl.BlockSpec(memory_space=pl.ANY)] * len(so_far),
        out_specs=[
            pl.BlockSpec((length, chunk), lambda c, place: (place[2], c)),
            pl.BlockSpec((width, length), lambda c, place: (0, place[2])),
        ],
        scratch_shapes=[pltpu.VMEM((length, width), jnp.bfloat16), pltpu.VMEM((width, length), jnp.float32)],
    )
    return pl.pallas_call(
        functools.partial(before_kernel, shards=shards, block=block),
        grid_spec=grid_spec,
        out_shape=[
            jax.ShapeDtypeStruct((2 * length, columns), jnp.bfloat16),
            jax.ShapeDtypeStruct((width, 2 * length), jnp.bfloat16),
        ],
        input_output_aliases={4 + at: at for at in range(len(so_far))},
        compiler_params=pltpu.CompilerParams(vmem_limit_bytes=60 << 20),
        cost_estimate=pl.CostEstimate(flops=2 * length * width * columns, bytes_accessed=12 << 20, transcendentals=length),
        name="before",
    )(place, x, gain, w, *so_far)


def middle_kernel(place, x_kept, x_other, o_ref, gy_kept, gy_other, w_out_ref, gain_ref, w_up_ref, w_down_ref,
                  out_kept, out_other, gx_ref, go_ref, keep_up, send_up, keep_down, send_down, keep_out, send_out,
                  gy, x1, low, low_t, total, back, flat, part, *, shards, block):
    c = pl.program_id(0)
    length, width = o_ref.shape
    chunk = w_down_ref.shape[0]
    pieces = [slice(at, at + block) for at in range(0, length, block)]
    rows = width // shards
    half, window = width // 2, length // 2
    kept = pl.ds(pl.multiple_of(place[2] * window, window), window)
    other = pl.ds(pl.multiple_of((1 - place[2]) * window, window), window)

    @pl.when(c == 0)
    def _():
        gy[kept, :] = gy_kept[...]
        gy[other, :] = gy_other[...]
        x1[kept, :] = x_kept[...].astype(jnp.float32)
        x1[other, :] = x_other[...].astype(jnp.float32)
        for at in pieces:
            values = x1[at, :] + mm(o_ref[at, :], w_out_ref[...])
            x1[at, :] = values
            mean, rate = row_stats(values)
            normed = (values - mean) * rate * gain_ref[...]
            low[at, :] = normed.astype(jnp.bfloat16)
            flat[:, at] = jnp.transpose(normed)
            total[at, :] = values
            back[at, :] = jnp.zeros_like(values)
        arranged(place, rows, flat, low_t, shards)

    lifted, slopes = [], []
    for at in pieces:
        a, slope = gelu_pair(mm(low[at, :], w_up_ref[...]))
        a = a.astype(jnp.bfloat16)
        gu = (mm(gy[at, :], w_down_ref[...], NT) * slope).astype(jnp.bfloat16)
        total[at, :] += mm(a, w_down_ref[...])
        back[at, :] += mm(gu, w_up_ref[...], NT)
        lifted.append(jnp.transpose(a))
        slopes.append(gu)
    cut(mm(low_t[...], jnp.concatenate(slopes, axis=0)), keep_up, send_up, 0)
    grad_down = mm(jnp.concatenate(lifted, axis=1), gy[...])
    if rows % 8:
        for at in range(width // PART):
            for target, begin in ((keep_down, 0), (send_down, chunk // 2)):
                piece = grad_down[begin:begin + chunk // 2, at * PART:(at + 1) * PART]
                target[at] = piece.astype(jnp.bfloat16)
    else:
        part[...] = grad_down
        for rel, target in enumerate((keep_down, send_down)):
            for q_rel in range(4):
                q = (place[1] ^ q_rel) & 3
                source = (((q >> 1) * 2 + (place[0] ^ rel)) * 2 + (q & 1)) * 4 * rows
                for sub in range(4):
                    source_rows = pl.ds(pl.multiple_of(source + sub * rows, 8), rows)
                    for at in range(width // PART):
                        piece = part[source_rows, at * PART:(at + 1) * PART]
                        target[4 * at + sub, q_rel] = piece.astype(jnp.bfloat16)

    @pl.when(c == pl.num_programs(0) - 1)
    def _():
        branch = []
        out_kept[...] = total[kept, :].astype(jnp.bfloat16)
        out_other[...] = total[other, :].astype(jnp.bfloat16)
        for at in pieces:
            grad = gy[at, :].astype(jnp.float32) + norm_back(x1[at, :], gain_ref[...], back[at, :])
            gx_ref[at, :] = grad
            grad = grad.astype(jnp.bfloat16)
            branch.append(grad)
            go_ref[at, :] = mm(grad, w_out_ref[...], NT).astype(jnp.bfloat16)
            flat[:, at] = jnp.transpose(o_ref[at, :].astype(jnp.float32))
        arranged(place, rows, flat, low_t, shards)
        cut(mm(low_t[...], jnp.concatenate(branch, axis=0)), keep_out, send_out, 0)


def middle(place, x, o, gy, w_out, gain, w_up, w_down, shards, block=256):
    length, width = o.shape
    lift = w_up.shape[1]
    steps = 4
    chunk = lift // steps
    half, window = width // 2, length // 2
    at = (lambda c, place: c) if (width // shards) % 8 else (lambda c, place: c ^ (place[1] >> 2))
    whole = lambda *shape: pl.BlockSpec(shape, lambda c, *_: (0, 0), pipeline_mode=pl.Buffered(1))
    out = lambda *shape: pl.BlockSpec(shape, lambda c, *_: (0,) * len(shape), pipeline_mode=pl.Buffered(1))
    shape = jax.ShapeDtypeStruct
    rows = width // shards
    if rows % 8:
        up_shape, down_shape, out_shape = (lift // PART, half, PART), (width // PART, lift // 2, PART), (width // PART, half, PART)
        up = pl.BlockSpec((chunk // PART, half, PART), lambda c, place: (at(c, place), 0, 0))
        down = pl.BlockSpec((width // PART, chunk // 2, PART), lambda c, place: (0, c, 0))
    else:
        piece = (shards // 2, rows, PART)
        up_shape, down_shape, out_shape = (lift // PART, *piece), (lift // PART, *piece), (width // PART, *piece)
        up = pl.BlockSpec((chunk // PART, *piece), lambda c, place: (at(c, place), 0, 0, 0))
        down = pl.BlockSpec((lift // PART, 4, rows, PART), lambda c, place: (0, c, 0, 0))
    bf16 = jnp.bfloat16
    grid_spec = pltpu.PrefetchScalarGridSpec(
        num_scalar_prefetch=1,
        grid=(steps,),
        in_specs=[
            whole(window, width), whole(window, width), whole(length, width), whole(window, width),
            whole(window, width), whole(width, width), whole(1, width),
            pl.BlockSpec((width, chunk), lambda c, place: (0, at(c, place))),
            pl.BlockSpec((chunk, width), lambda c, place: (at(c, place), 0)),
        ],
        out_specs=[
            out(window, width), out(window, width), out(length, width), out(length, width), up, up, down, down,
            out(*out_shape), out(*out_shape),
        ],
        scratch_shapes=[
            pltpu.VMEM((length, width), bf16),
            pltpu.VMEM((length, width), jnp.float32),
            pltpu.VMEM((length, width), bf16),
            pltpu.VMEM((width, length), bf16),
            pltpu.VMEM((length, width), jnp.float32),
            pltpu.VMEM((length, width), jnp.float32),
            pltpu.VMEM((width, length), jnp.float32),
            pltpu.VMEM((chunk, width), jnp.float32),
        ],
    )
    return pl.pallas_call(
        functools.partial(middle_kernel, shards=shards, block=block),
        grid_spec=grid_spec,
        out_shape=[
            shape((window, width), bf16), shape((window, width), bf16),
            shape((length, width), jnp.float32), shape((length, width), bf16),
            *[shape(size, bf16) for size in (up_shape, up_shape, down_shape, down_shape, out_shape, out_shape)],
        ],
        compiler_params=pltpu.CompilerParams(vmem_limit_bytes=60 << 20),
        cost_estimate=pl.CostEstimate(flops=12 * length * width * lift, bytes_accessed=40 << 20, transcendentals=length * lift),
        name="middle",
    )(place, *x, o, *gy, w_out, gain, w_up, w_down)


def after_kernel(place, x_ref, gain_ref, gx_ref, w_ref, *refs):
    out_ref = refs[-1]
    width = x_ref.shape[1]
    back = jnp.zeros(gx_ref.shape, jnp.float32)
    at = 0
    for names in zip(*[iter(refs[:-1])] * 3):
        columns = names[0].shape[1]
        for third, ref in enumerate(names):
            begin = third * width + at
            back += mm(ref[...], w_ref[:, begin:begin + columns], NT)
        at += columns
    values = x_ref[...].astype(jnp.float32)
    out_ref[...] = (gx_ref[...] + norm_back(values, gain_ref[...], back)).astype(out_ref.dtype)


def after(place, x, gain, gx, w, pieces, block=256):
    length, width = x.shape
    steps = length // block
    rows = lambda columns: pl.BlockSpec((block, columns), lambda i, place: (place[2] * steps + i, 0))
    own = pl.BlockSpec((block, width), lambda i, place: (i, 0))
    whole = lambda *shape: pl.BlockSpec(shape, lambda i, place: (0, 0), pipeline_mode=pl.Buffered(1))
    grid_spec = pltpu.PrefetchScalarGridSpec(
        num_scalar_prefetch=1,
        grid=(steps,),
        in_specs=[own, whole(1, width), rows(width), whole(width, w.shape[1])] + [rows(piece.shape[1]) for piece in pieces],
        out_specs=own,
    )
    return pl.pallas_call(
        after_kernel,
        grid_spec=grid_spec,
        out_shape=jax.ShapeDtypeStruct((length, width), jnp.bfloat16),
        compiler_params=pltpu.CompilerParams(vmem_limit_bytes=60 << 20),
        cost_estimate=pl.CostEstimate(flops=6 * length * width * width, bytes_accessed=16 << 20, transcendentals=length),
        name="after",
    )(place, x, gain, gx, w, *pieces)


def swapped(block):
    return lax.ppermute(block, "seq", [(0, 1), (1, 0)])


def split_window(block):
    place = lax.axis_index("seq")
    take = lambda at: lax.dynamic_index_in_dim(block, at, 0, keepdims=False)
    return take(place), take(1 - place)


def joined(kept, other):
    place = lax.axis_index("seq")
    return jnp.where(place == 0, jnp.stack([kept, other]), jnp.stack([other, kept]))


def crossed(block, bits):
    if 0 in bits:
        block = swapped(block)
    step = sum(1 << abs(bit) if bit > 0 else 1 for bit in bits if bit)
    if step:
        block = lax.ppermute(block, "dp", [(i, i ^ step) for i in range(lax.axis_size("dp"))])
    return block


def picks(left, bits, mask):
    rest = [bit for bit in left if bit not in bits]
    found = []
    for number in range(1 << len(rest)):
        value = {bit: (number >> (len(rest) - 1 - at)) & 1 for at, bit in enumerate(rest)}
        value.update({bit: int(bit in mask) for bit in bits})
        found.append(sum(value[bit] << (len(left) - 1 - at) for at, bit in enumerate(left)))
    return found


def masks_of(bits):
    return [tuple(bit for e, bit in enumerate(bits) if number >> e & 1) for number in range(1, 1 << len(bits))]


def combine_kernel(*refs, work, steps):
    for lead, cut_up, terms, targets in work:
        def one(index, carry):
            for count, sources, places, target, offset in targets:
                for at, source in enumerate(sources):
                    total = None
                    for ref, begin in terms:
                        value = refs[ref][begin + index * places + source].astype(jnp.float32)
                        total = value if total is None else total + value
                    refs[target][offset + index * count + at] = total.astype(refs[target].dtype)
            return carry

        if cut_up:
            one(0, 0)
        elif steps > 1:
            @pl.when(pl.program_id(0) == 0)
            def _():
                lax.fori_loop(0, lead, one, 0)
        else:
            lax.fori_loop(0, lead, one, 0)


class Flow:
    def __init__(self, place, keep, send, chips, plan, blocks=0):
        if keep.ndim == 3:
            index = jnp.stack([shard_at(place, rel, q) for rel in range(2) for q in range(chips)])
            lead, half, columns = keep.shape
            both = jnp.stack([array.reshape(lead, max(blocks, 1), -1, columns) for array in (keep, send)], axis=2)
            parts = max(blocks, 1)
            both = both.reshape(lead, 2 * chips, parts, -1, columns)[:, index].transpose(0, 2, 1, 3, 4)
            both = both.reshape(lead * parts, 2 * chips, -1, columns)
            keep, send = both[:, :chips], both[:, chips:]
        self.lead, _, self.rows, self.columns = keep.shape
        self.left = list(reversed(range(chips.bit_length() - 1)))
        self.plan = list(plan)
        self.terms = [(keep.reshape(-1, self.rows, self.columns), 0)]
        self.first = send.reshape(-1, self.rows, self.columns)


def combine(flows, steps):
    inputs, in_specs, out_shapes, out_specs, work, sends = [], [], [], [], [], {}

    def spec(array, per):
        if per:
            return pl.BlockSpec((per, *array.shape[1:]), lambda i: (i, 0, 0))
        return pl.BlockSpec(array.shape, lambda i: (0, 0, 0), pipeline_mode=pl.Buffered(1))

    def place_of(array, per):
        for at, seen in enumerate(inputs):
            if seen is array:
                return at
        inputs.append(array)
        in_specs.append(spec(array, per))
        return len(inputs) - 1

    plans = []
    for flow in flows:
        bits = flow.plan.pop(0)
        places = 1 << len(flow.left)
        count = places >> len(bits)
        cut_up = steps > 1 and flow.lead == steps
        terms = [(place_of(array, cut_up and places), offset) for array, offset in flow.terms]
        kept = picks(flow.left, bits, ())
        plans.append((flow, bits, places, count, cut_up, terms, kept))
    sizes = {}
    for flow, bits, places, count, cut_up, terms, kept in plans:
        for mask in masks_of(bits):
            key = mask if steps == 1 else (mask, id(flow))
            sizes.setdefault(key, []).append((flow, flow.lead * count, cut_up and count, mask))
    outputs = []
    for flow, bits, places, count, cut_up, terms, kept in plans:
        shape = (flow.lead * count, flow.rows, flow.columns)
        outputs.append(jax.ShapeDtypeStruct(shape, jnp.bfloat16 if count > 4 else jnp.float32))
        out_specs.append(spec(outputs[-1], cut_up and count))
    for key, members in sizes.items():
        shape = (sum(size for _, size, _, _ in members), members[0][0].rows, members[0][0].columns)
        outputs.append(jax.ShapeDtypeStruct(shape, jnp.bfloat16))
        out_specs.append(spec(outputs[-1], members[0][2]))
    base = len(inputs)
    for at, (flow, bits, places, count, cut_up, terms, kept) in enumerate(plans):
        targets = [(count, kept, places, base + at, 0)]
        for number, (key, members) in enumerate(sizes.items()):
            offset = 0
            for member, size, _, mask in members:
                if member is flow:
                    targets.append((count, picks(flow.left, bits, mask), places, base + len(plans) + number, offset))
                offset += size
        work.append((flow.lead, cut_up, terms, targets))
    results = pl.pallas_call(
        functools.partial(combine_kernel, work=work, steps=steps),
        grid=(steps,),
        in_specs=in_specs,
        out_specs=out_specs,
        out_shape=outputs,
        compiler_params=pltpu.CompilerParams(vmem_limit_bytes=60 << 20),
        cost_estimate=pl.CostEstimate(flops=1 << 20, bytes_accessed=8 << 20, transcendentals=0),
        name="combine",
    )(*inputs)
    for (flow, bits, *_), kept in zip(plans, results):
        flow.terms = [(kept, 0)]
        flow.left = [bit for bit in flow.left if bit not in bits]
    return [
        (members[0][3], array, [(flow, size) for flow, size, _, _ in members])
        for members, array in zip(sizes.values(), results[len(plans):])
    ]


def leave(flows, value=None, steps=1):
    starting = [flow for flow in flows if flow.plan and flow.first is not None]
    going = [flow for flow in flows if flow.plan and flow.first is None]
    sent = [((-1,), flow.first, [(flow, flow.first.shape[0])]) for flow in starting]
    for flow in starting:
        flow.plan.pop(0)
        flow.first = None
    if going:
        sent = combine(going, steps) + sent
    value, arrays = lax.optimization_barrier((value, [array for _, array, _ in sent]))
    return value, [(crossed(array, mask), members) for array, (mask, _, members) in zip(arrays, sent)]


def arrive(transfers, value=None):
    moved, value = lax.optimization_barrier(([array for array, _ in transfers], value))
    for array, (_, members) in zip(moved, transfers):
        at = 0
        for flow, size in members:
            flow.terms.append((array, at))
            at += size
    return value


def finish_kernel(*refs, work, count):
    inputs, outputs = refs[:count], refs[count:]
    for terms, targets in work:
        for lead, (target, row, column, width, parts) in enumerate(targets):
            total = sum(inputs[ref][offset + lead].astype(jnp.float32) for ref, offset in terms)
            for part in range(parts):
                piece = slice(part * width, (part + 1) * width)
                begin = column + part * (outputs[target].shape[1] // parts if parts > 1 else 0)
                outputs[target][row:row + total.shape[0], begin:begin + width] = total[:, piece]
    for number, source in enumerate((0, 2)):
        weight, gain = inputs[count - 4 + 2 * number], inputs[count - 3 + 2 * number]
        outputs[4 + number][...] = jnp.sum(weight[...] * outputs[source][...], axis=1, keepdims=True) / gain[...]


def finish(up, down, out_and_one, two, three, out_lead, weights):
    inputs, work = [], []

    def place_of(array):
        for at, seen in enumerate(inputs):
            if seen is array:
                return at
        inputs.append(array)
        return len(inputs) - 1

    rows = up.rows
    heads = iter(range(6))
    third = lambda: (0, 0, next(heads) * SMALL, SMALL, 3)
    plans = (
        (up, [(2, 0, lead * PART, PART, 1) for lead in range(up.lead)]),
        (down, [(3, (lead % 4) * rows, (lead // 4) * PART, PART, 1) for lead in range(down.lead)]),
        (out_and_one, [third() for _ in range(out_and_one.lead - out_lead)]
         + [(1, 0, lead * PART, PART, 1) for lead in range(out_lead)]),
        (two, [third() for _ in range(two.lead)]),
        (three, [third() for _ in range(three.lead)]),
    )
    for flow, targets in plans:
        work.append(([(place_of(array), offset) for array, offset in flow.terms], targets))
    inputs += weights
    width = out_lead * PART
    shape = lambda *size: jax.ShapeDtypeStruct(size, jnp.float32)
    return pl.pallas_call(
        functools.partial(finish_kernel, work=work, count=len(inputs)),
        out_shape=[shape(rows, 3 * width), shape(rows, width), shape(rows, up.lead * PART), shape(4 * rows, width),
                   shape(rows, 1), shape(rows, 1)],
        compiler_params=pltpu.CompilerParams(vmem_limit_bytes=60 << 20),
        cost_estimate=pl.CostEstimate(flops=1 << 20, bytes_accessed=4 << 20, transcendentals=0),
        name="finish",
    )(*inputs)


def body(tokens, segments, cotangent, gain_attn, w_qkv, w_out, gain_ffn, w_up, w_down):
    chips = lax.axis_size("dp")
    shards = 2 * chips
    dp, seq = lax.axis_index("dp"), lax.axis_index("seq")
    here = jnp.stack([dp & 1, (dp >> 1) * 2 + seq, seq]).astype(jnp.int32)
    there = jnp.stack([dp & 1, (dp >> 1) * 2 + seq, 1 - seq]).astype(jnp.int32)
    far = tuple(range(2, chips.bit_length() - 1))
    wide = [far[at:at + 2] for at in range(0, len(far), 2)]

    x_kept, x_sent = split_window(tokens)
    seg_kept, seg_sent = split_window(segments)
    gy_kept, gy_sent = split_window(cotangent)
    x_other, seg_other, gy_other = swapped(x_sent), swapped(seg_sent), swapped(gy_sent)
    seg = jnp.where(seq == 0, jnp.concatenate([seg_kept, seg_other]), jnp.concatenate([seg_other, seg_kept]))[None]
    first, last = bounds(seg, 256, 256)
    gain_one, gain_two = gain_attn[None], gain_ffn[None]
    early = before(here, x_kept, gain_one, w_qkv, shards)
    proj, low_t = before(there, x_other, gain_one, w_qkv, shards, early)
    mixture, lse = attend(first, seg, proj)
    out_kept, out_sent, gx, go, keep_up, send_up, keep_down, send_down, keep_out, send_out = middle(
        here, (x_kept, x_other), mixture, (gy_kept, gy_other), w_out, gain_two, w_up, w_down, shards
    )

    core = (-1,)
    later = [(bit,) for bit in far[1:]]
    up = Flow(here, keep_up, send_up, chips, [core, (1,), (0,), *wide])
    down = Flow(here, keep_down, send_down, chips, [core, far[:1], (1,), (0,), *later], 4)
    heads = []

    def heads_back(begin, count, plan, riders=()):
        *grads, keep, send = attend_back(begin, count, last, seg, proj, go, mixture, lse, low_t, shards, riders)
        heads.append(grads)
        return Flow(here, keep, send, chips, [core, *plan])

    (go, out_sent), moving = leave([up, down], (go, out_sent))
    out_other = swapped(out_sent)
    one = heads_back(0, 2, [far[:1], (1,), *later, (0,)], (keep_out, send_out))
    out_other = arrive(moving, out_other)
    (go, out_other), moving = leave([up, down, one], (go, out_other), up.lead)
    two = heads_back(2, 3, [(0,), (1,), *wide])
    arrive(moving)
    go, moving = leave([up, down, one, two], go, up.lead)
    three = heads_back(5, 1, [(0, 1), *wide])
    arrive(moving)
    flows = [up, down, one, two, three]
    gx, moving = leave(flows, gx)
    pieces = [piece for grads in heads for piece in grads]
    other_rows = after(there, x_other, gain_one, gx, w_qkv, pieces)
    other_rows = arrive(moving, other_rows)
    rows_back = swapped(other_rows)
    gx, moving = leave(flows, gx)
    kept_rows = after(here, x_kept, gain_one, gx, w_qkv, pieces)
    while True:
        kept_rows = arrive(moving, kept_rows)
        if not any(flow.plan for flow in flows):
            break
        _, moving = leave(flows)
    begin = shard_at(here, 0, 0) * up.rows
    shard_of = lambda array: lax.dynamic_slice_in_dim(array, begin, up.rows, 0).astype(jnp.float32)
    weights = [shard_of(w_qkv), shard_of(gain_attn)[:, None], shard_of(w_up), shard_of(gain_ffn)[:, None]]
    grad_qkv, grad_out, grad_up, grad_down, grad_gain_attn, grad_gain_ffn = finish(
        up, down, one, two, three, w_out.shape[1] // PART, weights
    )
    return (
        joined(out_kept, out_other),
        joined(kept_rows, rows_back),
        grad_qkv,
        grad_out,
        grad_up,
        grad_down,
        grad_gain_attn[:, 0],
        grad_gain_ffn[:, 0],
    )


def solution(mesh):
    placed = (
        P("dp", "seq", None),
        P("dp", "seq"),
        P("dp", "seq", None),
        P(),
        P(),
        P(),
        P(),
        P(),
        P(),
    )
    return jax.shard_map(
        body,
        mesh=mesh,
        in_specs=placed,
        out_specs=(
            P("dp", "seq", None),
            P("dp", "seq", None),
            P(("dp", "seq"), None),
            P(("dp", "seq"), None),
            P(("dp", "seq"), None),
            P(("dp", "seq"), None),
            P(("dp", "seq")),
            P(("dp", "seq")),
        ),
        check_vma=False,
    )
```

```python
import functools

import jax
import jax.numpy as jnp
from jax import lax
from jax.experimental import pallas as pl
from jax.experimental.pallas import tpu as pltpu
from jax.sharding import PartitionSpec as P

HEAD_DIM = 32
GROUP = 8
LANES = GROUP * HEAD_DIM
SMALL = 128
PART = 3 * SMALL
GRAIN = 128
masked_score = -1e30
epsilon = 1e-05
SCALE = HEAD_DIM ** (-0.5)
SCALE2 = SCALE * 1.4426950408889634
NT = (((1,), (1,)), ((), ()))
NN = (((1,), (0,)), ((), ()))


def mm(a, b, dims=NN):
    return lax.dot_general(a, b, dims, preferred_element_type=jnp.float32)


def attend_kernel(first, seg_ref, q_ref, k_ref, v_ref, o_ref, lse_ref, bias, total, *, bq, unroll):
    i, g = pl.program_id(0), pl.program_id(1)
    length = k_ref.shape[0]
    start = first[i]
    lane = lax.div(lax.broadcasted_iota(jnp.int32, (1, LANES), 1), HEAD_DIM)
    lane_head = lax.broadcasted_iota(jnp.int32, (1, 128), 1)

    def span(width):
        begin = pl.multiple_of(start * GRAIN, GRAIN)

        @pl.when(g == 0)
        def _():
            seg_q = jnp.transpose(jnp.broadcast_to(seg_ref[0:1, pl.ds(pl.multiple_of(i * bq, bq), bq)], (128, bq)))[:, 0:1]
            place_q = i * bq + lax.broadcasted_iota(jnp.int32, (bq, width), 0)
            place_k = begin + lax.broadcasted_iota(jnp.int32, (bq, width), 1)
            allowed = (place_k <= place_q) & (seg_q == seg_ref[0:1, pl.ds(begin, width)])
            bias[:, :width] = jnp.where(allowed, 0.0, masked_score)

        total[...] = jnp.zeros_like(total)

        def head(h, logs):
            query = jnp.where(lane == h, q_ref[...], jnp.zeros((), jnp.bfloat16))
            s = mm(query, k_ref[pl.ds(begin, width), :], NT) * SCALE2 + bias[:, :width]
            top = jnp.max(s, axis=-1, keepdims=True)
            e = jnp.exp2(s - top)
            row = jnp.sum(e, axis=-1, keepdims=True)
            out = mm(e.astype(jnp.bfloat16), v_ref[pl.ds(begin, width), :])
            total[...] = jnp.where(lane == h, out / row, total[...])
            place = jnp.where(h < GROUP // 2, h, h + GROUP // 2)
            return jnp.where(lane_head == place, top + jnp.log2(row), logs)

        logs = lax.fori_loop(0, GROUP, head, jnp.zeros((bq, 128), jnp.float32), unroll=unroll)
        o_ref[...] = total[...].astype(o_ref.dtype)
        lse_ref[...] = jnp.transpose(logs)[:2 * GROUP]

    blocks = (i + 1) * (bq // GRAIN) - start
    for count in range(bq // GRAIN, length // GRAIN + 1):
        pl.when(blocks == count)(functools.partial(span, count * GRAIN))


def attend(first, seg, proj, bq=256, unroll=8):
    length, width = proj.shape
    groups = width // 3 // LANES
    grid_spec = pltpu.PrefetchScalarGridSpec(
        num_scalar_prefetch=1,
        grid=(length // bq, groups),
        in_specs=[
            pl.BlockSpec((1, length), lambda i, g, *_: (0, 0)),
            pl.BlockSpec((bq, LANES), lambda i, g, *_: (i, g)),
            pl.BlockSpec((length, LANES), lambda i, g, *_: (0, groups + g)),
            pl.BlockSpec((length, LANES), lambda i, g, *_: (0, 2 * groups + g)),
        ],
        out_specs=[
            pl.BlockSpec((bq, LANES), lambda i, g, *_: (i, g)),
            pl.BlockSpec((2 * GROUP, bq), lambda i, g, *_: (g, i)),
        ],
        scratch_shapes=[pltpu.VMEM((bq, length), jnp.float32), pltpu.VMEM((bq, LANES), jnp.float32)],
    )
    return pl.pallas_call(
        functools.partial(attend_kernel, bq=bq, unroll=unroll),
        grid_spec=grid_spec,
        out_shape=[
            jax.ShapeDtypeStruct((length, width // 3), jnp.bfloat16),
            jax.ShapeDtypeStruct((groups * 2 * GROUP, length), jnp.float32),
        ],
        compiler_params=pltpu.CompilerParams(vmem_limit_bytes=60 << 20),
        cost_estimate=pl.CostEstimate(flops=28 << 30, bytes_accessed=8 << 20, transcendentals=24 * length * length),
        name="attend",
    )(first, seg, proj, proj, proj)


def attend_back_kernel(last, seg_ref, q_ref, k_ref, v_ref, up_ref, o_ref, lse_ref, low_t_ref, *refs, bk):
    *riders, gq_ref, gk_ref, gv_ref, keep_ref, send_ref, bias, inner, key_t, value_t, q_t, up_t, gq_t, gk, gv = refs
    g, j = pl.program_id(0), pl.program_id(1)
    length, lanes = q_ref.shape
    heads = lanes // HEAD_DIM
    lane = lax.div(lax.broadcasted_iota(jnp.int32, (1, lanes), 1), HEAD_DIM)

    @pl.when(j == 0)
    def _():
        gq_t[...] = jnp.zeros_like(gq_t)
        q_t[...] = jnp.transpose(q_ref[...])
        up_t[...] = jnp.transpose(up_ref[...])
        pick = (lax.div(lax.broadcasted_iota(jnp.int32, (8, lanes), 1), HEAD_DIM)
                == lax.broadcasted_iota(jnp.int32, (8, lanes), 0)).astype(jnp.float32)
        product = up_ref[...].astype(jnp.float32) * o_ref[...].astype(jnp.float32)
        inner[...] = lax.dot_general(pick, product, NT, precision=lax.Precision.HIGHEST,
                                     preferred_element_type=jnp.float32)

    key_t[...] = jnp.transpose(k_ref[...])
    value_t[...] = jnp.transpose(v_ref[...])

    def span(width):
        begin = pl.multiple_of(j * bk, bk)
        here = pl.ds(begin, width)
        seg_k = jnp.transpose(jnp.broadcast_to(seg_ref[0:1, pl.ds(begin, bk)], (128, bk)))[:, 0:1]
        place_k = lax.broadcasted_iota(jnp.int32, (bk, width), 0)
        place_q = lax.broadcasted_iota(jnp.int32, (bk, width), 1)
        allowed = (place_k <= place_q) & (seg_k == seg_ref[0:1, here])
        bias[:, :width] = jnp.where(allowed, 0.0, masked_score)
        for h in range(heads):
            rows = slice(h * HEAD_DIM, (h + 1) * HEAD_DIM)
            key, value = jnp.transpose(key_t[rows, :]), jnp.transpose(value_t[rows, :])
            s = mm(key, q_t[rows, here]) * SCALE2 + (bias[:, :width] - lse_ref[h:h + 1, here])
            p = jnp.exp2(s)
            dp = mm(value, up_t[rows, here])
            ds = (p * (dp - inner[h:h + 1, here])).astype(jnp.bfloat16)
            grad_v = mm(p.astype(jnp.bfloat16), up_ref[here, :])
            grad_k = mm(ds, q_ref[here, :])
            gv[...] = jnp.where(lane == h, grad_v, gv[...]) if h else grad_v
            gk[...] = jnp.where(lane == h, grad_k, gk[...]) if h else grad_k
            gq_t[rows, here] += mm(key_t[rows, :], ds)

    blocks = last[j] - j * (bk // GRAIN)
    for count in range(bk // GRAIN, length // GRAIN + 1):
        pl.when(blocks == count)(functools.partial(span, count * GRAIN))

    here = pl.ds(pl.multiple_of(j * bk, bk), bk)
    gk_ref[here, :] = (gk[...] * SCALE).astype(gk_ref.dtype)
    gv_ref[here, :] = gv[...].astype(gv_ref.dtype)

    @pl.when(j == pl.num_programs(1) - 1)
    def _():
        gq_ref[...] = jnp.transpose((gq_t[...] * SCALE).astype(gq_ref.dtype))
        joined = jnp.concatenate([gq_ref[...], gk_ref[...], gv_ref[...]], axis=1)
        cut(mm(low_t_ref[...], joined), keep_ref, send_ref, g)

    if riders:
        @pl.when((g == 0) & (j == 0))
        def _():
            extra = riders[0].shape[0]
            for rider, target in zip(riders, (keep_ref, send_ref)):
                target[-extra:] = rider[...]


def attend_back(begin, count, last, seg, proj, up, o, lse, low_t, shards, riders=(), bk=256):
    length, width = proj.shape
    groups = width // 3 // SMALL
    half = width // 6
    group = lambda g: g + begin
    whole = lambda offset: pl.BlockSpec((length, SMALL), lambda g, j, *_: (0, offset + group(g)))
    block = lambda offset: pl.BlockSpec((bk, SMALL), lambda g, j, *_: (j, offset + group(g)))
    fixed = lambda *shape: pl.BlockSpec(shape, lambda g, j, *_: (0, 0), pipeline_mode=pl.Buffered(1))
    out = pl.BlockSpec((length, SMALL), lambda g, j, *_: (0, g))
    rows = 2 * half // shards
    piece = (half, PART) if rows % 8 else (shards // 2, rows, PART)
    lead = count + (riders[0].shape[0] if riders else 0)
    all_of = lambda *size: pl.BlockSpec(size, lambda g, j, *_: (0,) * len(size), pipeline_mode=pl.Buffered(1))
    split = all_of(lead, *piece)
    grid_spec = pltpu.PrefetchScalarGridSpec(
        num_scalar_prefetch=1,
        grid=(count, length // bk),
        in_specs=[
            fixed(1, length),
            whole(0),
            block(groups),
            block(2 * groups),
            whole(0),
            whole(0),
            pl.BlockSpec((8, length), lambda g, j, *_: (group(g), 0)),
            fixed(2 * half, length),
            *[all_of(*rider.shape) for rider in riders],
        ],
        out_specs=[out, out, out, split, split],
        scratch_shapes=[
            pltpu.VMEM((bk, length), jnp.float32),
            pltpu.VMEM((8, length), jnp.float32),
            pltpu.VMEM((SMALL, bk), jnp.bfloat16),
            pltpu.VMEM((SMALL, bk), jnp.bfloat16),
            pltpu.VMEM((SMALL, length), jnp.bfloat16),
            pltpu.VMEM((SMALL, length), jnp.bfloat16),
            pltpu.VMEM((SMALL, length), jnp.float32),
            pltpu.VMEM((bk, SMALL), jnp.float32),
            pltpu.VMEM((bk, SMALL), jnp.float32),
        ],
    )
    heads = jax.ShapeDtypeStruct((length, count * SMALL), jnp.bfloat16)
    parts = jax.ShapeDtypeStruct((lead, *piece), jnp.bfloat16)
    return pl.pallas_call(
        functools.partial(attend_back_kernel, bk=bk),
        grid_spec=grid_spec,
        out_shape=[heads, heads, heads, parts, parts],
        compiler_params=pltpu.CompilerParams(vmem_limit_bytes=60 << 20),
        cost_estimate=pl.CostEstimate(flops=(count * 10) << 30, bytes_accessed=8 << 20, transcendentals=count * 4 * length * length),
        name="attend_back",
    )(last, seg, proj, proj, proj, up, o, lse, low_t, *riders)


def bounds(seg, bq, bk):
    row = seg[0]
    first = jnp.sum(row[None, :] < row[::bq][:, None], axis=1) // GRAIN
    last = (jnp.sum(row[None, :] <= row[bk - 1::bk][:, None], axis=1) + GRAIN - 1) // GRAIN
    return first.astype(jnp.int32), last.astype(jnp.int32)


def gelu_pair(u):
    c = 0.7978845608028654
    square = u * u
    t = jnp.tanh(u * (c + (c * 0.044715) * square))
    half = 0.5 * t + 0.5
    slope = half + (0.5 * u) * (1.0 - t * t) * (c + (3 * c * 0.044715) * square)
    return u * half, slope


def row_stats(values):
    mean = jnp.mean(values, axis=-1, keepdims=True)
    centred = values - mean
    return mean, lax.rsqrt(jnp.mean(centred * centred, axis=-1, keepdims=True) + epsilon)


def norm_back(values, gain, upstream):
    mean, rate = row_stats(values)
    unit = (values - mean) * rate
    inner = upstream * gain
    level = jnp.mean(inner, axis=-1, keepdims=True)
    along = jnp.mean(inner * unit, axis=-1, keepdims=True)
    return rate * (inner - level - unit * along)


def shard_at(place, core_rel, q_rel):
    core, q = place[0] ^ core_rel, place[1] ^ q_rel
    return ((q >> 1) * 2 + core) * 2 + (q & 1)


def arranged(place, rows, source, target, shards):
    if rows % 8:
        target[...] = source[...].astype(target.dtype)
        return
    chips = shards // 2
    for at in range(0, shards, 2):
        pair = [
            source[pl.ds(pl.multiple_of(shard_at(place, b // chips, b % chips) * rows, 8), rows), :]
            for b in (at, at + 1)
        ]
        target[at * rows:(at + 2) * rows, :] = jnp.concatenate(pair).astype(target.dtype)


def cut(grad, keep, send, first):
    half = grad.shape[0] // 2
    for at in range(grad.shape[1] // PART):
        block = grad[:, at * PART:(at + 1) * PART]
        if len(keep.shape) == 3:
            keep[first + at] = block[:half].astype(keep.dtype)
            send[first + at] = block[half:].astype(send.dtype)
        else:
            chips, rows = keep.shape[1:3]
            for q in range(chips):
                keep[first + at, q] = block[q * rows:(q + 1) * rows].astype(keep.dtype)
                send[first + at, q] = block[half + q * rows:half + (q + 1) * rows].astype(send.dtype)


def before_kernel(place, x_ref, gain_ref, w_ref, *refs, shards, block):
    proj_ref, low_t_ref, low, flat = refs[-4:]
    length, width = x_ref.shape

    @pl.when(pl.program_id(0) == 0)
    def _():
        for at in range(0, length, block):
            at = slice(at, at + block)
            values = x_ref[at, :].astype(jnp.float32)
            mean, rate = row_stats(values)
            normed = (values - mean) * rate * gain_ref[...]
            low[at, :] = normed.astype(jnp.bfloat16)
            flat[:, at] = jnp.transpose(normed)
        arranged(place, width // shards, flat, low_t_ref, shards)

    proj_ref[...] = mm(low[...], w_ref[...]).astype(jnp.bfloat16)


def before(place, x, gain, w, shards, so_far=(), chunk=768, block=256):
    length, width = x.shape
    columns = w.shape[1]
    whole = lambda *shape: pl.BlockSpec(shape, lambda c, *_: (0, 0), pipeline_mode=pl.Buffered(1))
    grid_spec = pltpu.PrefetchScalarGridSpec(
        num_scalar_prefetch=1,
        grid=(columns // chunk,),
        in_specs=[whole(length, width), whole(1, width), pl.BlockSpec((width, chunk), lambda c, *_: (0, c))]
        + [pl.BlockSpec(memory_space=pl.ANY)] * len(so_far),
        out_specs=[
            pl.BlockSpec((length, chunk), lambda c, place: (place[2], c)),
            pl.BlockSpec((width, length), lambda c, place: (0, place[2])),
        ],
        scratch_shapes=[pltpu.VMEM((length, width), jnp.bfloat16), pltpu.VMEM((width, length), jnp.float32)],
    )
    return pl.pallas_call(
        functools.partial(before_kernel, shards=shards, block=block),
        grid_spec=grid_spec,
        out_shape=[
            jax.ShapeDtypeStruct((2 * length, columns), jnp.bfloat16),
            jax.ShapeDtypeStruct((width, 2 * length), jnp.bfloat16),
        ],
        input_output_aliases={4 + at: at for at in range(len(so_far))},
        compiler_params=pltpu.CompilerParams(vmem_limit_bytes=60 << 20),
        cost_estimate=pl.CostEstimate(flops=2 * length * width * columns, bytes_accessed=12 << 20, transcendentals=length),
        name="before",
    )(place, x, gain, w, *so_far)


def middle_kernel(place, x_kept, x_other, o_ref, gy_kept, gy_other, w_out_ref, gain_ref, w_up_ref, w_down_ref,
                  out_kept, out_other, gx_ref, go_ref, keep_up, send_up, keep_down, send_down, keep_out, send_out,
                  gy, x1, low, low_t, total, back, flat, part, *, shards, block):
    c = pl.program_id(0)
    length, width = o_ref.shape
    chunk = w_down_ref.shape[0]
    pieces = [slice(at, at + block) for at in range(0, length, block)]
    rows = width // shards
    half, window = width // 2, length // 2
    kept = pl.ds(pl.multiple_of(place[2] * window, window), window)
    other = pl.ds(pl.multiple_of((1 - place[2]) * window, window), window)

    @pl.when(c == 0)
    def _():
        gy[kept, :] = gy_kept[...]
        gy[other, :] = gy_other[...]
        x1[kept, :] = x_kept[...].astype(jnp.float32)
        x1[other, :] = x_other[...].astype(jnp.float32)
        for at in pieces:
            values = x1[at, :] + mm(o_ref[at, :], w_out_ref[...])
            x1[at, :] = values
            mean, rate = row_stats(values)
            normed = (values - mean) * rate * gain_ref[...]
            low[at, :] = normed.astype(jnp.bfloat16)
            flat[:, at] = jnp.transpose(normed)
            total[at, :] = values
            back[at, :] = jnp.zeros_like(values)
        arranged(place, rows, flat, low_t, shards)

    lifted, slopes = [], []
    for at in pieces:
        a, slope = gelu_pair(mm(low[at, :], w_up_ref[...]))
        a = a.astype(jnp.bfloat16)
        gu = (mm(gy[at, :], w_down_ref[...], NT) * slope).astype(jnp.bfloat16)
        total[at, :] += mm(a, w_down_ref[...])
        back[at, :] += mm(gu, w_up_ref[...], NT)
        lifted.append(jnp.transpose(a))
        slopes.append(gu)
    cut(mm(low_t[...], jnp.concatenate(slopes, axis=0)), keep_up, send_up, 0)
    grad_down = mm(jnp.concatenate(lifted, axis=1), gy[...])
    if rows % 8:
        for at in range(width // PART):
            for target, begin in ((keep_down, 0), (send_down, chunk // 2)):
                piece = grad_down[begin:begin + chunk // 2, at * PART:(at + 1) * PART]
                target[at] = piece.astype(jnp.bfloat16)
    else:
        part[...] = grad_down
        for rel, target in enumerate((keep_down, send_down)):
            for q_rel in range(4):
                q = (place[1] ^ q_rel) & 3
                source = (((q >> 1) * 2 + (place[0] ^ rel)) * 2 + (q & 1)) * 4 * rows
                for sub in range(4):
                    source_rows = pl.ds(pl.multiple_of(source + sub * rows, 8), rows)
                    for at in range(width // PART):
                        piece = part[source_rows, at * PART:(at + 1) * PART]
                        target[4 * at + sub, q_rel] = piece.astype(jnp.bfloat16)

    @pl.when(c == pl.num_programs(0) - 1)
    def _():
        branch = []
        out_kept[...] = total[kept, :].astype(jnp.bfloat16)
        out_other[...] = total[other, :].astype(jnp.bfloat16)
        for at in pieces:
            grad = gy[at, :].astype(jnp.float32) + norm_back(x1[at, :], gain_ref[...], back[at, :])
            gx_ref[at, :] = grad
            grad = grad.astype(jnp.bfloat16)
            branch.append(grad)
            go_ref[at, :] = mm(grad, w_out_ref[...], NT).astype(jnp.bfloat16)
            flat[:, at] = jnp.transpose(o_ref[at, :].astype(jnp.float32))
        arranged(place, rows, flat, low_t, shards)
        cut(mm(low_t[...], jnp.concatenate(branch, axis=0)), keep_out, send_out, 0)


def middle(place, x, o, gy, w_out, gain, w_up, w_down, shards, block=256):
    length, width = o.shape
    lift = w_up.shape[1]
    steps = 4
    chunk = lift // steps
    half, window = width // 2, length // 2
    at = (lambda c, place: c) if (width // shards) % 8 else (lambda c, place: c ^ (place[1] >> 2))
    whole = lambda *shape: pl.BlockSpec(shape, lambda c, *_: (0, 0), pipeline_mode=pl.Buffered(1))
    out = lambda *shape: pl.BlockSpec(shape, lambda c, *_: (0,) * len(shape), pipeline_mode=pl.Buffered(1))
    shape = jax.ShapeDtypeStruct
    rows = width // shards
    if rows % 8:
        up_shape, down_shape, out_shape = (lift // PART, half, PART), (width // PART, lift // 2, PART), (width // PART, half, PART)
        up = pl.BlockSpec((chunk // PART, half, PART), lambda c, place: (at(c, place), 0, 0))
        down = pl.BlockSpec((width // PART, chunk // 2, PART), lambda c, place: (0, c, 0))
    else:
        piece = (shards // 2, rows, PART)
        up_shape, down_shape, out_shape = (lift // PART, *piece), (lift // PART, *piece), (width // PART, *piece)
        up = pl.BlockSpec((chunk // PART, *piece), lambda c, place: (at(c, place), 0, 0, 0))
        down = pl.BlockSpec((lift // PART, 4, rows, PART), lambda c, place: (0, c, 0, 0))
    bf16 = jnp.bfloat16
    grid_spec = pltpu.PrefetchScalarGridSpec(
        num_scalar_prefetch=1,
        grid=(steps,),
        in_specs=[
            whole(window, width), whole(window, width), whole(length, width), whole(window, width),
            whole(window, width), whole(width, width), whole(1, width),
            pl.BlockSpec((width, chunk), lambda c, place: (0, at(c, place))),
            pl.BlockSpec((chunk, width), lambda c, place: (at(c, place), 0)),
        ],
        out_specs=[
            out(window, width), out(window, width), out(length, width), out(length, width), up, up, down, down,
            out(*out_shape), out(*out_shape),
        ],
        scratch_shapes=[
            pltpu.VMEM((length, width), bf16),
            pltpu.VMEM((length, width), jnp.float32),
            pltpu.VMEM((length, width), bf16),
            pltpu.VMEM((width, length), bf16),
            pltpu.VMEM((length, width), jnp.float32),
            pltpu.VMEM((length, width), jnp.float32),
            pltpu.VMEM((width, length), jnp.float32),
            pltpu.VMEM((chunk, width), jnp.float32),
        ],
    )
    return pl.pallas_call(
        functools.partial(middle_kernel, shards=shards, block=block),
        grid_spec=grid_spec,
        out_shape=[
            shape((window, width), bf16), shape((window, width), bf16),
            shape((length, width), jnp.float32), shape((length, width), bf16),
            *[shape(size, bf16) for size in (up_shape, up_shape, down_shape, down_shape, out_shape, out_shape)],
        ],
        compiler_params=pltpu.CompilerParams(vmem_limit_bytes=60 << 20),
        cost_estimate=pl.CostEstimate(flops=12 * length * width * lift, bytes_accessed=40 << 20, transcendentals=length * lift),
        name="middle",
    )(place, *x, o, *gy, w_out, gain, w_up, w_down)


def after_kernel(place, x_ref, gain_ref, gx_ref, w_ref, *refs):
    out_ref = refs[-1]
    width = x_ref.shape[1]
    back = jnp.zeros(gx_ref.shape, jnp.float32)
    at = 0
    for names in zip(*[iter(refs[:-1])] * 3):
        columns = names[0].shape[1]
        for third, ref in enumerate(names):
            begin = third * width + at
            back += mm(ref[...], w_ref[:, begin:begin + columns], NT)
        at += columns
    values = x_ref[...].astype(jnp.float32)
    out_ref[...] = (gx_ref[...] + norm_back(values, gain_ref[...], back)).astype(out_ref.dtype)


def after(place, x, gain, gx, w, pieces, block=256):
    length, width = x.shape
    steps = length // block
    rows = lambda columns: pl.BlockSpec((block, columns), lambda i, place: (place[2] * steps + i, 0))
    own = pl.BlockSpec((block, width), lambda i, place: (i, 0))
    whole = lambda *shape: pl.BlockSpec(shape, lambda i, place: (0, 0), pipeline_mode=pl.Buffered(1))
    grid_spec = pltpu.PrefetchScalarGridSpec(
        num_scalar_prefetch=1,
        grid=(steps,),
        in_specs=[own, whole(1, width), rows(width), whole(width, w.shape[1])] + [rows(piece.shape[1]) for piece in pieces],
        out_specs=own,
    )
    return pl.pallas_call(
        after_kernel,
        grid_spec=grid_spec,
        out_shape=jax.ShapeDtypeStruct((length, width), jnp.bfloat16),
        compiler_params=pltpu.CompilerParams(vmem_limit_bytes=60 << 20),
        cost_estimate=pl.CostEstimate(flops=6 * length * width * width, bytes_accessed=16 << 20, transcendentals=length),
        name="after",
    )(place, x, gain, gx, w, *pieces)


def swapped(block):
    return lax.ppermute(block, "seq", [(0, 1), (1, 0)])


def split_window(block):
    place = lax.axis_index("seq")
    take = lambda at: lax.dynamic_index_in_dim(block, at, 0, keepdims=False)
    return take(place), take(1 - place)


def joined(kept, other):
    place = lax.axis_index("seq")
    return jnp.where(place == 0, jnp.stack([kept, other]), jnp.stack([other, kept]))


def crossed(block, bits):
    step = sum(1 if bit == 0 else 2 if bit == -1 else 2 << bit for bit in bits)
    count = 2 * lax.axis_size("dp")
    return lax.ppermute(block, ("dp", "seq"), [(i, i ^ step) for i in range(count)])


def masks_of(bits):
    return [tuple(bit for e, bit in enumerate(bits) if number >> e & 1) for number in range(1, 1 << len(bits))]


def combine_kernel(*refs, work, steps):
    for lead, cut_up, targets in work:
        def one(index, carry):
            for target, offset, count, sources in targets:
                for at, terms in enumerate(sources):
                    total = None
                    for ref, begin, per, place in terms:
                        where = (index, *place) if per is None else (begin + index * per + place,)
                        value = refs[ref][where].astype(jnp.float32)
                        total = value if total is None else total + value
                    refs[target][offset + index * count + at] = total.astype(refs[target].dtype)
            return carry

        if cut_up:
            lax.fori_loop(0, lead // steps, one, 0)
        elif steps > 1:
            @pl.when(pl.program_id(0) == 0)
            def _():
                lax.fori_loop(0, lead, one, 0)
        else:
            lax.fori_loop(0, lead, one, 0)


class Flow:
    def __init__(self, place, keep, send, chips, plan, blocks=0):
        if keep.ndim == 3:
            index = jnp.stack([shard_at(place, rel, q) for rel in range(2) for q in range(chips)])
            lead, half, columns = keep.shape
            both = jnp.stack([array.reshape(lead, max(blocks, 1), -1, columns) for array in (keep, send)], axis=2)
            parts = max(blocks, 1)
            both = both.reshape(lead, 2 * chips, parts, -1, columns)[:, index].transpose(0, 2, 1, 3, 4)
            both = both.reshape(lead * parts, 2 * chips, -1, columns)
            keep, send = both[:, :chips], both[:, chips:]
        self.lead, _, self.rows, self.columns = keep.shape
        self.left = list(reversed(range(chips.bit_length() - 1)))
        self.plan = list(plan)
        self.terms = [(keep.reshape(-1, self.rows, self.columns), list(self.left), None)]
        self.first = send.reshape(-1, self.rows, self.columns)


class Operands:
    def __init__(self):
        self.arrays, self.specs, self.seen = [], [], {}

    def add(self, array, spec):
        self.arrays.append(array)
        self.specs.append(spec)
        return len(self.arrays) - 1

    def finder(self, flow, term, fixed, cut_up):
        array, bits, offset = term
        if offset is not None:
            if id(array) not in self.seen:
                self.seen[id(array)] = self.add(array, pl.BlockSpec(array.shape, lambda i: (0, 0, 0), pipeline_mode=pl.Buffered(1)))
            ref, per = self.seen[id(array)], 1 << len(bits)
            return lambda value: (ref, offset, per, sum(value[bit] << (len(bits) - 1 - at) for at, bit in enumerate(bits)))
        view = array.reshape(flow.lead, *(2,) * len(bits), flow.rows, flow.columns)
        block = (flow.lead // cut_up if cut_up else flow.lead, *[1 if bit in fixed else 2 for bit in bits], flow.rows, flow.columns)
        index = tuple(fixed.get(bit, 0) for bit in bits)
        mode = {} if cut_up else dict(pipeline_mode=pl.Buffered(1))
        ref = self.add(view, pl.BlockSpec(block, lambda i: (i if cut_up else 0, *index, 0, 0), **mode))
        return lambda value: (ref, 0, None, tuple(0 if bit in fixed else value[bit] for bit in bits))


def combine(flows, steps):
    operands, plans, sizes = Operands(), [], {}
    for flow in flows:
        bits = flow.plan.pop(0)
        rest = [bit for bit in flow.left if bit not in bits]
        cut_up = steps if steps > 1 and flow.lead % steps == 0 else 0
        gone = {bit: 0 for bit in range(64) if bit not in flow.left}
        fixed = {**gone, bits[0]: 1} if len(bits) == 1 else gone
        finders = [operands.finder(flow, term, fixed, cut_up) for term in flow.terms]
        plans.append((flow, bits, rest, cut_up, gone, finders))
        for mask in masks_of(bits):
            size = flow.lead << len(rest)
            key = mask if steps == 1 else (mask, id(flow))
            sizes.setdefault(key, []).append((flow, size, cut_up and size // cut_up, mask))
    outputs, out_specs = [], []
    for members in sizes.values():
        shape = (sum(size for _, size, _, _ in members), members[0][0].rows, members[0][0].columns)
        outputs.append(jax.ShapeDtypeStruct(shape, jnp.bfloat16))
        cut = members[0][2]
        out_specs.append(
            pl.BlockSpec((cut, *shape[1:]), lambda i: (i, 0, 0)) if cut
            else pl.BlockSpec(shape, lambda i: (0, 0, 0), pipeline_mode=pl.Buffered(1))
        )
    work = []
    for flow, bits, rest, cut_up, gone, finders in plans:
        targets = []
        for number, members in enumerate(sizes.values()):
            offset = 0
            for member, size, _, mask in members:
                if member is flow:
                    sources = []
                    for at in range(1 << len(rest)):
                        value = {bit: (at >> (len(rest) - 1 - e)) & 1 for e, bit in enumerate(rest)}
                        value.update(gone)
                        value.update({bit: int(bit in mask) for bit in bits})
                        sources.append([find(value) for find in finders])
                    targets.append((len(operands.arrays) + number, offset, 1 << len(rest), sources))
                offset += size
        work.append((flow.lead, cut_up, targets))
        flow.left = rest
    results = pl.pallas_call(
        functools.partial(combine_kernel, work=work, steps=steps),
        grid=(steps,),
        in_specs=operands.specs,
        out_specs=out_specs,
        out_shape=outputs,
        compiler_params=pltpu.CompilerParams(vmem_limit_bytes=60 << 20),
        cost_estimate=pl.CostEstimate(flops=1 << 20, bytes_accessed=8 << 20, transcendentals=0),
        name="combine",
    )(*operands.arrays)
    return [
        (members[0][3], array, [(flow, size) for flow, size, _, _ in members])
        for members, array in zip(sizes.values(), results)
    ]


def leave(flows, value=None, steps=1):
    flows = [flow for flow in flows if flow.plan]
    starting = [flow for flow in flows if flow.plan[0] == (-1,)]
    waiting = [flow for flow in flows if flow.plan[0] == ()]
    going = [flow for flow in flows if flow not in starting and flow not in waiting]
    for flow in starting + waiting:
        flow.plan.pop(0)
    sent = combine(going, steps) if going else []
    sent += [((-1,), flow.first, [(flow, flow.first.shape[0])]) for flow in starting]
    value, arrays = lax.optimization_barrier((value, [array for _, array, _ in sent]))
    return value, [(crossed(array, mask), members) for array, (mask, _, members) in zip(arrays, sent)]


def arrive(transfers, value=None):
    moved, value = lax.optimization_barrier(([array for array, _ in transfers], value))
    for array, (_, members) in zip(moved, transfers):
        at = 0
        for flow, size in members:
            flow.terms.append((array, list(flow.left), at if len(members) > 1 else None))
            at += size
    return value


def finish_kernel(*refs, work, count):
    inputs, outputs = refs[:count], refs[count:]
    for terms, targets in work:
        for lead, (target, row, column, width, parts) in enumerate(targets):
            total = None
            for ref, begin, per, place in terms:
                where = (lead, *place) if per is None else (begin + lead * per + place,)
                value = inputs[ref][where].astype(jnp.float32)
                total = value if total is None else total + value
            for part in range(parts):
                piece = slice(part * width, (part + 1) * width)
                begin = column + part * (outputs[target].shape[1] // parts if parts > 1 else 0)
                outputs[target][row:row + total.shape[0], begin:begin + width] = total[:, piece]
    for number, source in enumerate((0, 2)):
        weight, gain = inputs[count - 4 + 2 * number], inputs[count - 3 + 2 * number]
        ones = jnp.ones((8, weight.shape[1]), jnp.float32)
        sums = lax.dot_general(ones, weight[...] * outputs[source][...], NT, precision=lax.Precision.HIGHEST,
                               preferred_element_type=jnp.float32)
        outputs[4 + number][...] = sums[:1] / gain[...]


def finish(up, down, out_and_one, others, out_lead, weights):
    operands, work = Operands(), []
    rows = up.rows
    heads = iter(range(64))
    third = lambda: (0, 0, next(heads) * SMALL, SMALL, 3)
    plans = [
        (up, [(2, 0, lead * PART, PART, 1) for lead in range(up.lead)]),
        (down, [(3, (lead % 4) * rows, (lead // 4) * PART, PART, 1) for lead in range(down.lead)]),
        (out_and_one, [third() for _ in range(out_and_one.lead - out_lead)]
         + [(1, 0, lead * PART, PART, 1) for lead in range(out_lead)]),
    ]
    plans += [(flow, [third() for _ in range(flow.lead)]) for flow in others]
    gone = {bit: 0 for bit in range(64)}
    for flow, targets in plans:
        finders = [operands.finder(flow, term, gone, False) for term in flow.terms]
        work.append(([find(gone) for find in finders], targets))
    for weight in weights:
        operands.add(weight, pl.BlockSpec(weight.shape, lambda i: (0, 0), pipeline_mode=pl.Buffered(1)))
    width = out_lead * PART
    sizes = [(rows, 3 * width), (rows, width), (rows, up.lead * PART), (4 * rows, width), (1, rows), (1, rows)]
    return pl.pallas_call(
        functools.partial(finish_kernel, work=work, count=len(operands.arrays)),
        grid=(1,),
        in_specs=operands.specs,
        out_specs=[pl.BlockSpec(size, lambda i: (0, 0), pipeline_mode=pl.Buffered(1)) for size in sizes],
        out_shape=[jax.ShapeDtypeStruct(size, jnp.float32) for size in sizes],
        compiler_params=pltpu.CompilerParams(vmem_limit_bytes=60 << 20),
        cost_estimate=pl.CostEstimate(flops=1 << 20, bytes_accessed=4 << 20, transcendentals=0),
        name="finish",
    )(*operands.arrays)


def body(tokens, segments, cotangent, gain_attn, w_qkv, w_out, gain_ffn, w_up, w_down):
    chips = lax.axis_size("dp")
    shards = 2 * chips
    dp, seq = lax.axis_index("dp"), lax.axis_index("seq")
    here = jnp.stack([dp & 1, (dp >> 1) * 2 + seq, seq]).astype(jnp.int32)
    there = jnp.stack([dp & 1, (dp >> 1) * 2 + seq, 1 - seq]).astype(jnp.int32)
    far = tuple(range(2, chips.bit_length() - 1))
    wide = [far[at:at + 2] for at in range(0, len(far), 2)]

    x_kept, x_sent = split_window(tokens)
    segments, cotangent, x_sent = lax.optimization_barrier((segments, cotangent, x_sent))
    seg_kept, seg_sent = split_window(segments)
    gy_kept, gy_sent = split_window(cotangent)
    x_other, seg_other, gy_other = swapped(x_sent), swapped(seg_sent), swapped(gy_sent)
    seg = jnp.where(seq == 0, jnp.concatenate([seg_kept, seg_other]), jnp.concatenate([seg_other, seg_kept]))[None]
    first, last = bounds(seg, 256, 256)
    gain_one, gain_two = gain_attn[None], gain_ffn[None]
    begin = shard_at(here, 0, 0) * (w_out.shape[0] // shards)
    shard_of = lambda array: lax.dynamic_slice_in_dim(array, begin, w_out.shape[0] // shards, 0).astype(jnp.float32)
    weights = [shard_of(w_qkv), shard_of(gain_attn)[None], shard_of(w_up), shard_of(gain_ffn)[None]]
    x_other, weights = lax.optimization_barrier((x_other, weights))
    early = before(here, x_kept, gain_one, w_qkv, shards)
    proj, low_t = before(there, x_other, gain_one, w_qkv, shards, early)
    mixture, lse = attend(first, seg, proj)
    out_kept, out_sent, gx, go, keep_up, send_up, keep_down, send_down, keep_out, send_out = middle(
        here, (x_kept, x_other), mixture, (gy_kept, gy_other), w_out, gain_two, w_up, w_down, shards
    )

    core, near = (-1,), [(bit,) for bit in far]
    up = Flow(here, keep_up, send_up, chips, [core, (1,), (0,), *near])
    down = Flow(here, keep_down, send_down, chips, [core, *near[:1], (1,), (0,), *near[1:]], 4)
    heads = []

    def heads_back(begin, count, plan, riders=()):
        *grads, keep, send = attend_back(begin, count, last, seg, proj, go, mixture, lse, low_t, shards, riders)
        heads.append(grads)
        return Flow(here, keep, send, chips, [core, *plan])

    (go, out_sent), moving = leave([up, down], (go, out_sent))
    out_other = swapped(out_sent)
    one = heads_back(0, 2, [*near[:1], (0,), (1,), *near[1:]], (keep_out, send_out))
    out_other = arrive(moving, out_other)
    (go, out_other), moving = leave([up, down, one], (go, out_other), 2)
    two = heads_back(2, 3, [(1,), (0,), *wide])
    arrive(moving)
    go, moving = leave([up, down, one, two], go, 2)
    three = heads_back(5, 1, [(0, 1), *wide])
    arrive(moving)
    flows = [up, down, one, two, three]
    gx, moving = leave(flows, gx)
    pieces = [piece for grads in heads for piece in grads]
    other_rows = after(there, x_other, gain_one, gx, w_qkv, pieces)
    other_rows = arrive(moving, other_rows)
    rows_back = swapped(other_rows)
    gx, moving = leave(flows, gx)
    kept_rows = after(here, x_kept, gain_one, gx, w_qkv, pieces)
    while True:
        kept_rows = arrive(moving, kept_rows)
        if not any(flow.plan for flow in flows):
            break
        _, moving = leave(flows)
    grad_qkv, grad_out, grad_up, grad_down, grad_gain_attn, grad_gain_ffn = finish(
        up, down, one, [two, three], w_out.shape[1] // PART, weights
    )
    return (
        joined(out_kept, out_other),
        joined(kept_rows, rows_back),
        grad_qkv,
        grad_out,
        grad_up,
        grad_down,
        grad_gain_attn[0],
        grad_gain_ffn[0],
    )


def solution(mesh):
    placed = (
        P("dp", "seq", None),
        P("dp", "seq"),
        P("dp", "seq", None),
        P(),
        P(),
        P(),
        P(),
        P(),
        P(),
    )
    return jax.shard_map(
        body,
        mesh=mesh,
        in_specs=placed,
        out_specs=(
            P("dp", "seq", None),
            P("dp", "seq", None),
            P(("dp", "seq"), None),
            P(("dp", "seq"), None),
            P(("dp", "seq"), None),
            P(("dp", "seq"), None),
            P(("dp", "seq")),
            P(("dp", "seq")),
        ),
        check_vma=False,
    )
```

```python
import functools

import jax
import jax.numpy as jnp
from jax import lax
from jax.experimental import pallas as pl
from jax.experimental.pallas import tpu as pltpu
from jax.sharding import PartitionSpec as P

HEAD_DIM = 32
GROUP = 8
LANES = GROUP * HEAD_DIM
SMALL = 128
PART = 3 * SMALL
GRAIN = 128
masked_score = -1e30
epsilon = 1e-05
SCALE = HEAD_DIM ** (-0.5)
SCALE2 = SCALE * 1.4426950408889634
NT = (((1,), (1,)), ((), ()))
NN = (((1,), (0,)), ((), ()))


def mm(a, b, dims=NN):
    return lax.dot_general(a, b, dims, preferred_element_type=jnp.float32)


def attend_kernel(first, seg_ref, q_ref, k_ref, v_ref, o_ref, lse_ref, bias, total, *, bq, unroll):
    i, g = pl.program_id(0), pl.program_id(1)
    length = k_ref.shape[0]
    start = first[i]
    lane = lax.div(lax.broadcasted_iota(jnp.int32, (1, LANES), 1), HEAD_DIM)
    lane_head = lax.broadcasted_iota(jnp.int32, (1, 128), 1)

    def span(width):
        begin = pl.multiple_of(start * GRAIN, GRAIN)

        @pl.when(g == 0)
        def _():
            seg_q = jnp.transpose(jnp.broadcast_to(seg_ref[0:1, pl.ds(pl.multiple_of(i * bq, bq), bq)], (128, bq)))[:, 0:1]
            place_q = i * bq + lax.broadcasted_iota(jnp.int32, (bq, width), 0)
            place_k = begin + lax.broadcasted_iota(jnp.int32, (bq, width), 1)
            allowed = (place_k <= place_q) & (seg_q == seg_ref[0:1, pl.ds(begin, width)])
            bias[:, :width] = jnp.where(allowed, 0.0, masked_score)

        total[...] = jnp.zeros_like(total)

        def head(h, logs):
            query = jnp.where(lane == h, q_ref[...], jnp.zeros((), jnp.bfloat16))
            s = mm(query, k_ref[pl.ds(begin, width), :], NT) * SCALE2 + bias[:, :width]
            top = jnp.max(s, axis=-1, keepdims=True)
            e = jnp.exp2(s - top)
            row = jnp.sum(e, axis=-1, keepdims=True)
            out = mm(e.astype(jnp.bfloat16), v_ref[pl.ds(begin, width), :])
            total[...] = jnp.where(lane == h, out * (1.0 / row), total[...])
            place = jnp.where(h < GROUP // 2, h, h + GROUP // 2)
            return jnp.where(lane_head == place, top + jnp.log2(row), logs)

        logs = lax.fori_loop(0, GROUP, head, jnp.zeros((bq, 128), jnp.float32), unroll=unroll)
        o_ref[...] = total[...].astype(o_ref.dtype)
        lse_ref[...] = jnp.transpose(logs)[:2 * GROUP]

    blocks = (i + 1) * (bq // GRAIN) - start
    for count in range(bq // GRAIN, length // GRAIN + 1):
        pl.when(blocks == count)(functools.partial(span, count * GRAIN))


def attend(first, seg, proj, bq=256, unroll=8):
    length, width = proj.shape
    groups = width // 3 // LANES
    grid_spec = pltpu.PrefetchScalarGridSpec(
        num_scalar_prefetch=1,
        grid=(length // bq, groups),
        in_specs=[
            pl.BlockSpec((1, length), lambda i, g, *_: (0, 0)),
            pl.BlockSpec((bq, LANES), lambda i, g, *_: (i, g)),
            pl.BlockSpec((length, LANES), lambda i, g, *_: (0, groups + g)),
            pl.BlockSpec((length, LANES), lambda i, g, *_: (0, 2 * groups + g)),
        ],
        out_specs=[
            pl.BlockSpec((bq, LANES), lambda i, g, *_: (i, g)),
            pl.BlockSpec((2 * GROUP, bq), lambda i, g, *_: (g, i)),
        ],
        scratch_shapes=[pltpu.VMEM((bq, length), jnp.float32), pltpu.VMEM((bq, LANES), jnp.float32)],
    )
    return pl.pallas_call(
        functools.partial(attend_kernel, bq=bq, unroll=unroll),
        grid_spec=grid_spec,
        out_shape=[
            jax.ShapeDtypeStruct((length, width // 3), jnp.bfloat16),
            jax.ShapeDtypeStruct((groups * 2 * GROUP, length), jnp.float32),
        ],
        compiler_params=pltpu.CompilerParams(vmem_limit_bytes=60 << 20),
        cost_estimate=pl.CostEstimate(flops=28 << 30, bytes_accessed=8 << 20, transcendentals=24 * length * length),
        name="attend",
    )(first, seg, proj, proj, proj)


def attend_back_kernel(last, seg_ref, q_ref, k_ref, v_ref, up_ref, o_ref, lse_ref, low_t_ref, *refs, bk):
    *riders, gq_ref, gk_ref, gv_ref, keep_ref, send_ref, bias, inner, key_t, value_t, q_t, up_t, gq_t, gk, gv = refs
    g, j = pl.program_id(0), pl.program_id(1)
    length, lanes = q_ref.shape
    heads = lanes // HEAD_DIM
    lane = lax.div(lax.broadcasted_iota(jnp.int32, (1, lanes), 1), HEAD_DIM)

    @pl.when(j == 0)
    def _():
        gq_t[...] = jnp.zeros_like(gq_t)
        q_t[...] = jnp.transpose(q_ref[...])
        up_t[...] = jnp.transpose(up_ref[...])
        product = up_t[...].astype(jnp.float32) * jnp.transpose(o_ref[...]).astype(jnp.float32)
        for h in range(heads):
            rows = slice(h * HEAD_DIM, (h + 1) * HEAD_DIM)
            inner[h:h + 1, :] = jnp.sum(product[rows], axis=0, keepdims=True)

    key_t[...] = jnp.transpose(k_ref[...])
    value_t[...] = jnp.transpose(v_ref[...])

    def span(width):
        begin = pl.multiple_of(j * bk, bk)
        here = pl.ds(begin, width)

        @pl.when(g == 0)
        def _():
            seg_k = jnp.transpose(jnp.broadcast_to(seg_ref[0:1, pl.ds(begin, bk)], (128, bk)))[:, 0:1]
            place_k = lax.broadcasted_iota(jnp.int32, (bk, width), 0)
            place_q = lax.broadcasted_iota(jnp.int32, (bk, width), 1)
            allowed = (place_k <= place_q) & (seg_k == seg_ref[0:1, here])
            bias[j, :, :width] = jnp.where(allowed, 0.0, masked_score)

        for h in range(heads):
            rows = slice(h * HEAD_DIM, (h + 1) * HEAD_DIM)
            key, value = jnp.transpose(key_t[rows, :]), jnp.transpose(value_t[rows, :])
            s = mm(key, q_t[rows, here]) * SCALE2 + (bias[j, :, :width] - lse_ref[h:h + 1, here])
            p = jnp.exp2(s)
            dp = mm(value, up_t[rows, here])
            ds = (p * (dp - inner[h:h + 1, here])).astype(jnp.bfloat16)
            grad_v = mm(p.astype(jnp.bfloat16), up_ref[here, :])
            grad_k = mm(ds, q_ref[here, :])
            gv[...] = jnp.where(lane == h, grad_v, gv[...]) if h else grad_v
            gk[...] = jnp.where(lane == h, grad_k, gk[...]) if h else grad_k
            gq_t[rows, here] += mm(key_t[rows, :], ds)

    blocks = last[j] - j * (bk // GRAIN)
    for count in range(bk // GRAIN, length // GRAIN + 1):
        pl.when(blocks == count)(functools.partial(span, count * GRAIN))

    here = pl.ds(pl.multiple_of(j * bk, bk), bk)
    gk_ref[here, :] = (gk[...] * SCALE).astype(gk_ref.dtype)
    gv_ref[here, :] = gv[...].astype(gv_ref.dtype)

    @pl.when(j == pl.num_programs(1) - 1)
    def _():
        gq_ref[...] = jnp.transpose((gq_t[...] * SCALE).astype(gq_ref.dtype))
        joined = jnp.concatenate([gq_ref[...], gk_ref[...], gv_ref[...]], axis=1)
        cut(mm(low_t_ref[...], joined), keep_ref, send_ref, g)

    if riders:
        @pl.when((g == 0) & (j == 0))
        def _():
            extra = riders[0].shape[0]
            for rider, target in zip(riders, (keep_ref, send_ref)):
                target[-extra:] = rider[...]


def attend_back(begin, count, last, seg, proj, up, o, lse, low_t, shards, riders=(), bk=256):
    length, width = proj.shape
    groups = width // 3 // SMALL
    half = width // 6
    group = lambda g: g + begin
    whole = lambda offset: pl.BlockSpec((length, SMALL), lambda g, j, *_: (0, offset + group(g)))
    block = lambda offset: pl.BlockSpec((bk, SMALL), lambda g, j, *_: (j, offset + group(g)))
    fixed = lambda *shape: pl.BlockSpec(shape, lambda g, j, *_: (0, 0), pipeline_mode=pl.Buffered(1))
    out = pl.BlockSpec((length, SMALL), lambda g, j, *_: (0, g))
    rows = 2 * half // shards
    piece = (half, PART) if rows % 8 else (shards // 2, rows, PART)
    lead = count + (riders[0].shape[0] if riders else 0)
    all_of = lambda *size: pl.BlockSpec(size, lambda g, j, *_: (0,) * len(size), pipeline_mode=pl.Buffered(1))
    split = all_of(lead, *piece)
    grid_spec = pltpu.PrefetchScalarGridSpec(
        num_scalar_prefetch=1,
        grid=(count, length // bk),
        in_specs=[
            fixed(1, length),
            whole(0),
            block(groups),
            block(2 * groups),
            whole(0),
            whole(0),
            pl.BlockSpec((8, length), lambda g, j, *_: (group(g), 0)),
            fixed(2 * half, length),
            *[all_of(*rider.shape) for rider in riders],
        ],
        out_specs=[out, out, out, split, split],
        scratch_shapes=[
            pltpu.VMEM((length // bk, bk, length), jnp.float32),
            pltpu.VMEM((8, length), jnp.float32),
            pltpu.VMEM((SMALL, bk), jnp.bfloat16),
            pltpu.VMEM((SMALL, bk), jnp.bfloat16),
            pltpu.VMEM((SMALL, length), jnp.bfloat16),
            pltpu.VMEM((SMALL, length), jnp.bfloat16),
            pltpu.VMEM((SMALL, length), jnp.float32),
            pltpu.VMEM((bk, SMALL), jnp.float32),
            pltpu.VMEM((bk, SMALL), jnp.float32),
        ],
    )
    heads = jax.ShapeDtypeStruct((length, count * SMALL), jnp.bfloat16)
    parts = jax.ShapeDtypeStruct((lead, *piece), jnp.bfloat16)
    return pl.pallas_call(
        functools.partial(attend_back_kernel, bk=bk),
        grid_spec=grid_spec,
        out_shape=[heads, heads, heads, parts, parts],
        compiler_params=pltpu.CompilerParams(vmem_limit_bytes=60 << 20),
        cost_estimate=pl.CostEstimate(flops=(count * 10) << 30, bytes_accessed=8 << 20, transcendentals=count * 4 * length * length),
        name="attend_back",
    )(last, seg, proj, proj, proj, up, o, lse, low_t, *riders)


def bounds(seg, bq, bk):
    row = seg[0]
    first = jnp.sum(row[None, :] < row[::bq][:, None], axis=1) // GRAIN
    last = (jnp.sum(row[None, :] <= row[bk - 1::bk][:, None], axis=1) + GRAIN - 1) // GRAIN
    return first.astype(jnp.int32), last.astype(jnp.int32)


def gelu_pair(u):
    c = 0.7978845608028654
    square = u * u
    t = jnp.tanh(u * (c + (c * 0.044715) * square))
    half = 0.5 * t + 0.5
    slope = half + (0.5 * u) * (1.0 - t * t) * (c + (3 * c * 0.044715) * square)
    return u * half, slope


def row_stats(values):
    mean = jnp.mean(values, axis=-1, keepdims=True)
    centred = values - mean
    return mean, lax.rsqrt(jnp.mean(centred * centred, axis=-1, keepdims=True) + epsilon)


def norm_back(values, gain, upstream):
    mean, rate = row_stats(values)
    unit = (values - mean) * rate
    inner = upstream * gain
    level = jnp.mean(inner, axis=-1, keepdims=True)
    along = jnp.mean(inner * unit, axis=-1, keepdims=True)
    return rate * (inner - level - unit * along)


def shard_at(place, core_rel, q_rel):
    core, q = place[0] ^ core_rel, place[1] ^ q_rel
    return ((q >> 1) * 2 + core) * 2 + (q & 1)


def arranged(place, rows, source, target, shards):
    if rows % 8:
        target[...] = source[...].astype(target.dtype)
        return
    chips = shards // 2
    for at in range(0, shards, 2):
        pair = [
            source[pl.ds(pl.multiple_of(shard_at(place, b // chips, b % chips) * rows, 8), rows), :]
            for b in (at, at + 1)
        ]
        target[at * rows:(at + 2) * rows, :] = jnp.concatenate(pair).astype(target.dtype)


def cut(grad, keep, send, first):
    half = grad.shape[0] // 2
    for at in range(grad.shape[1] // PART):
        block = grad[:, at * PART:(at + 1) * PART]
        if len(keep.shape) == 3:
            keep[first + at] = block[:half].astype(keep.dtype)
            send[first + at] = block[half:].astype(send.dtype)
        else:
            chips, rows = keep.shape[1:3]
            for q in range(chips):
                keep[first + at, q] = block[q * rows:(q + 1) * rows].astype(keep.dtype)
                send[first + at, q] = block[half + q * rows:half + (q + 1) * rows].astype(send.dtype)


def before_kernel(place, x_ref, gain_ref, w_ref, *refs, shards, block):
    proj_ref, low_t_ref, low, flat = refs[-4:]
    length, width = x_ref.shape

    @pl.when(pl.program_id(0) == 0)
    def _():
        for at in range(0, length, block):
            at = slice(at, at + block)
            values = x_ref[at, :].astype(jnp.float32)
            mean, rate = row_stats(values)
            normed = (values - mean) * rate * gain_ref[...]
            low[at, :] = normed.astype(jnp.bfloat16)
            flat[:, at] = jnp.transpose(normed)
        arranged(place, width // shards, flat, low_t_ref, shards)

    proj_ref[...] = mm(low[...], w_ref[...]).astype(jnp.bfloat16)


def before(place, x, gain, w, shards, so_far=(), chunk=768, block=256):
    length, width = x.shape
    columns = w.shape[1]
    whole = lambda *shape: pl.BlockSpec(shape, lambda c, *_: (0, 0), pipeline_mode=pl.Buffered(1))
    grid_spec = pltpu.PrefetchScalarGridSpec(
        num_scalar_prefetch=1,
        grid=(columns // chunk,),
        in_specs=[whole(length, width), whole(1, width), pl.BlockSpec((width, chunk), lambda c, *_: (0, c))]
        + [pl.BlockSpec(memory_space=pl.ANY)] * len(so_far),
        out_specs=[
            pl.BlockSpec((length, chunk), lambda c, place: (place[2], c)),
            pl.BlockSpec((width, length), lambda c, place: (0, place[2])),
        ],
        scratch_shapes=[pltpu.VMEM((length, width), jnp.bfloat16), pltpu.VMEM((width, length), jnp.float32)],
    )
    return pl.pallas_call(
        functools.partial(before_kernel, shards=shards, block=block),
        grid_spec=grid_spec,
        out_shape=[
            jax.ShapeDtypeStruct((2 * length, columns), jnp.bfloat16),
            jax.ShapeDtypeStruct((width, 2 * length), jnp.bfloat16),
        ],
        input_output_aliases={4 + at: at for at in range(len(so_far))},
        compiler_params=pltpu.CompilerParams(vmem_limit_bytes=60 << 20),
        cost_estimate=pl.CostEstimate(flops=2 * length * width * columns, bytes_accessed=12 << 20, transcendentals=length),
        name="before",
    )(place, x, gain, w, *so_far)


def middle_kernel(place, x_kept, x_other, o_ref, gy_kept, gy_other, w_out_ref, gain_ref, w_up_ref, w_down_ref,
                  out_kept, out_other, gx_ref, go_ref, keep_up, send_up, keep_down, send_down, keep_out, send_out,
                  gy, x1, low, low_t, total, back, flat, part, *, shards, block):
    c = pl.program_id(0)
    length, width = o_ref.shape
    chunk = w_down_ref.shape[0]
    pieces = [slice(at, at + block) for at in range(0, length, block)]
    rows = width // shards
    half, window = width // 2, length // 2
    kept = pl.ds(pl.multiple_of(place[2] * window, window), window)
    other = pl.ds(pl.multiple_of((1 - place[2]) * window, window), window)

    @pl.when(c == 0)
    def _():
        gy[kept, :] = gy_kept[...]
        gy[other, :] = gy_other[...]
        x1[kept, :] = x_kept[...].astype(jnp.float32)
        x1[other, :] = x_other[...].astype(jnp.float32)
        for at in pieces:
            values = x1[at, :] + mm(o_ref[at, :], w_out_ref[...])
            x1[at, :] = values
            mean, rate = row_stats(values)
            normed = (values - mean) * rate * gain_ref[...]
            low[at, :] = normed.astype(jnp.bfloat16)
            flat[:, at] = jnp.transpose(normed)
            total[at, :] = values
            back[at, :] = jnp.zeros_like(values)
        arranged(place, rows, flat, low_t, shards)

    lifted, slopes = [], []
    for at in pieces:
        a, slope = gelu_pair(mm(low[at, :], w_up_ref[...]))
        a = a.astype(jnp.bfloat16)
        gu = (mm(gy[at, :], w_down_ref[...], NT) * slope).astype(jnp.bfloat16)
        total[at, :] += mm(a, w_down_ref[...])
        back[at, :] += mm(gu, w_up_ref[...], NT)
        lifted.append(jnp.transpose(a))
        slopes.append(gu)
    cut(mm(low_t[...], jnp.concatenate(slopes, axis=0)), keep_up, send_up, 0)
    grad_down = mm(jnp.concatenate(lifted, axis=1), gy[...])
    if rows % 8:
        for at in range(width // PART):
            for target, begin in ((keep_down, 0), (send_down, chunk // 2)):
                piece = grad_down[begin:begin + chunk // 2, at * PART:(at + 1) * PART]
                target[at] = piece.astype(jnp.bfloat16)
    else:
        part[...] = grad_down
        for rel, target in enumerate((keep_down, send_down)):
            for q_rel in range(4):
                q = (place[1] ^ q_rel) & 3
                source = (((q >> 1) * 2 + (place[0] ^ rel)) * 2 + (q & 1)) * 4 * rows
                for sub in range(4):
                    source_rows = pl.ds(pl.multiple_of(source + sub * rows, 8), rows)
                    for at in range(width // PART):
                        piece = part[source_rows, at * PART:(at + 1) * PART]
                        target[4 * at + sub, q_rel] = piece.astype(jnp.bfloat16)

    @pl.when(c == pl.num_programs(0) - 1)
    def _():
        branch = []
        out_kept[...] = total[kept, :].astype(jnp.bfloat16)
        out_other[...] = total[other, :].astype(jnp.bfloat16)
        for at in pieces:
            grad = gy[at, :].astype(jnp.float32) + norm_back(x1[at, :], gain_ref[...], back[at, :])
            grad = grad.astype(jnp.bfloat16)
            gx_ref[at, :] = grad
            branch.append(grad)
            go_ref[at, :] = mm(grad, w_out_ref[...], NT).astype(jnp.bfloat16)
            flat[:, at] = jnp.transpose(o_ref[at, :].astype(jnp.float32))
        arranged(place, rows, flat, low_t, shards)
        cut(mm(low_t[...], jnp.concatenate(branch, axis=0)), keep_out, send_out, 0)


def middle(place, x, o, gy, w_out, gain, w_up, w_down, shards, block=256):
    length, width = o.shape
    lift = w_up.shape[1]
    steps = 4
    chunk = lift // steps
    half, window = width // 2, length // 2
    at = (lambda c, place: c) if (width // shards) % 8 else (lambda c, place: c ^ (place[1] >> 2))
    whole = lambda *shape: pl.BlockSpec(shape, lambda c, *_: (0, 0), pipeline_mode=pl.Buffered(1))
    out = lambda *shape: pl.BlockSpec(shape, lambda c, *_: (0,) * len(shape), pipeline_mode=pl.Buffered(1))
    shape = jax.ShapeDtypeStruct
    rows = width // shards
    if rows % 8:
        up_shape, down_shape, out_shape = (lift // PART, half, PART), (width // PART, lift // 2, PART), (width // PART, half, PART)
        up = pl.BlockSpec((chunk // PART, half, PART), lambda c, place: (at(c, place), 0, 0))
        down = pl.BlockSpec((width // PART, chunk // 2, PART), lambda c, place: (0, c, 0))
    else:
        piece = (shards // 2, rows, PART)
        up_shape, down_shape, out_shape = (lift // PART, *piece), (lift // PART, *piece), (width // PART, *piece)
        up = pl.BlockSpec((chunk // PART, *piece), lambda c, place: (at(c, place), 0, 0, 0))
        down = pl.BlockSpec((lift // PART, 4, rows, PART), lambda c, place: (0, c, 0, 0))
    bf16 = jnp.bfloat16
    grid_spec = pltpu.PrefetchScalarGridSpec(
        num_scalar_prefetch=1,
        grid=(steps,),
        in_specs=[
            whole(window, width), whole(window, width), whole(length, width), whole(window, width),
            whole(window, width), whole(width, width), whole(1, width),
            pl.BlockSpec((width, chunk), lambda c, place: (0, at(c, place))),
            pl.BlockSpec((chunk, width), lambda c, place: (at(c, place), 0)),
        ],
        out_specs=[
            out(window, width), out(window, width), out(length, width), out(length, width), up, up, down, down,
            out(*out_shape), out(*out_shape),
        ],
        scratch_shapes=[
            pltpu.VMEM((length, width), bf16),
            pltpu.VMEM((length, width), jnp.float32),
            pltpu.VMEM((length, width), bf16),
            pltpu.VMEM((width, length), bf16),
            pltpu.VMEM((length, width), jnp.float32),
            pltpu.VMEM((length, width), jnp.float32),
            pltpu.VMEM((width, length), jnp.float32),
            pltpu.VMEM((chunk, width), jnp.float32),
        ],
    )
    return pl.pallas_call(
        functools.partial(middle_kernel, shards=shards, block=block),
        grid_spec=grid_spec,
        out_shape=[
            shape((window, width), bf16), shape((window, width), bf16),
            shape((length, width), bf16), shape((length, width), bf16),
            *[shape(size, bf16) for size in (up_shape, up_shape, down_shape, down_shape, out_shape, out_shape)],
        ],
        compiler_params=pltpu.CompilerParams(vmem_limit_bytes=60 << 20),
        cost_estimate=pl.CostEstimate(flops=12 * length * width * lift, bytes_accessed=40 << 20, transcendentals=length * lift),
        name="middle",
    )(place, *x, o, *gy, w_out, gain, w_up, w_down)


def after_kernel(place, x_ref, gain_ref, gx_ref, w_ref, *refs):
    out_ref = refs[-1]
    grads = jnp.concatenate([ref[...] for third in range(3) for ref in refs[third:-1:3]], axis=1)
    back = mm(grads, w_ref[...], NT)
    values = x_ref[...].astype(jnp.float32)
    out_ref[...] = (gx_ref[...].astype(jnp.float32) + norm_back(values, gain_ref[...], back)).astype(out_ref.dtype)


def after(place, x, gain, gx, w, pieces, block=256):
    length, width = x.shape
    steps = length // block
    rows = lambda columns: pl.BlockSpec((block, columns), lambda i, place: (place[2] * steps + i, 0))
    own = pl.BlockSpec((block, width), lambda i, place: (i, 0))
    whole = lambda *shape: pl.BlockSpec(shape, lambda i, place: (0, 0), pipeline_mode=pl.Buffered(1))
    grid_spec = pltpu.PrefetchScalarGridSpec(
        num_scalar_prefetch=1,
        grid=(steps,),
        in_specs=[own, whole(1, width), rows(width), whole(width, w.shape[1])] + [rows(piece.shape[1]) for piece in pieces],
        out_specs=own,
    )
    return pl.pallas_call(
        after_kernel,
        grid_spec=grid_spec,
        out_shape=jax.ShapeDtypeStruct((length, width), jnp.bfloat16),
        compiler_params=pltpu.CompilerParams(vmem_limit_bytes=60 << 20),
        cost_estimate=pl.CostEstimate(flops=6 * length * width * width, bytes_accessed=16 << 20, transcendentals=length),
        name="after",
    )(place, x, gain, gx, w, *pieces)


def swapped(block):
    return lax.ppermute(block, "seq", [(0, 1), (1, 0)])


def split_window(block):
    place = lax.axis_index("seq")
    take = lambda at: lax.dynamic_index_in_dim(block, at, 0, keepdims=False)
    return take(place), take(1 - place)


def joined(kept, other):
    place = lax.axis_index("seq")
    return jnp.where(place == 0, jnp.stack([kept, other]), jnp.stack([other, kept]))


def crossed(block, bits):
    step = sum(1 if bit == 0 else 2 if bit == -1 else 2 << bit for bit in bits)
    count = 2 * lax.axis_size("dp")
    return lax.ppermute(block, ("dp", "seq"), [(i, i ^ step) for i in range(count)])


def masks_of(bits):
    return [tuple(bit for e, bit in enumerate(bits) if number >> e & 1) for number in range(1, 1 << len(bits))]


def combine_kernel(*refs, work, steps):
    for lead, cut_up, targets in work:
        def one(index, carry):
            for target, offset, count, sources in targets:
                for at, terms in enumerate(sources):
                    total = None
                    for ref, begin, per, place in terms:
                        where = (index, *place) if per is None else (begin + index * per + place,)
                        value = refs[ref][where].astype(jnp.float32)
                        total = value if total is None else total + value
                    refs[target][offset + index * count + at] = total.astype(refs[target].dtype)
            return carry

        count = lead // steps if cut_up else lead

        def all_of(count=count, one=one):
            if sum(len(sources) for _, _, _, sources in targets) > 32:
                lax.fori_loop(0, count, one, 0)
            else:
                for index in range(count):
                    one(index, 0)

        if cut_up:
            all_of()
        elif steps > 1:
            @pl.when(pl.program_id(0) == 0)
            def _():
                all_of()
        else:
            all_of()


class Flow:
    def __init__(self, place, keep, send, chips, plan, blocks=0):
        if keep.ndim == 3:
            index = jnp.stack([shard_at(place, rel, q) for rel in range(2) for q in range(chips)])
            lead, half, columns = keep.shape
            both = jnp.stack([array.reshape(lead, max(blocks, 1), -1, columns) for array in (keep, send)], axis=2)
            parts = max(blocks, 1)
            both = both.reshape(lead, 2 * chips, parts, -1, columns)[:, index].transpose(0, 2, 1, 3, 4)
            both = both.reshape(lead * parts, 2 * chips, -1, columns)
            keep, send = both[:, :chips], both[:, chips:]
        self.lead, _, self.rows, self.columns = keep.shape
        self.left = list(reversed(range(chips.bit_length() - 1)))
        self.plan = list(plan)
        self.terms = [(keep.reshape(-1, self.rows, self.columns), list(self.left), None)]
        self.first = send.reshape(-1, self.rows, self.columns)


class Operands:
    def __init__(self):
        self.arrays, self.specs, self.seen = [], [], {}

    def add(self, array, spec):
        self.arrays.append(array)
        self.specs.append(spec)
        return len(self.arrays) - 1

    def finder(self, flow, term, fixed, cut_up):
        array, bits, offset = term
        if offset is not None:
            if id(array) not in self.seen:
                self.seen[id(array)] = self.add(array, pl.BlockSpec(array.shape, lambda i: (0, 0, 0), pipeline_mode=pl.Buffered(1)))
            ref, per = self.seen[id(array)], 1 << len(bits)
            return lambda value: (ref, offset, per, sum(value[bit] << (len(bits) - 1 - at) for at, bit in enumerate(bits)))
        view = array.reshape(flow.lead, *(2,) * len(bits), flow.rows, flow.columns)
        block = (flow.lead // cut_up if cut_up else flow.lead, *[1 if bit in fixed else 2 for bit in bits], flow.rows, flow.columns)
        index = tuple(fixed.get(bit, 0) for bit in bits)
        mode = {} if cut_up else dict(pipeline_mode=pl.Buffered(1))
        ref = self.add(view, pl.BlockSpec(block, lambda i: (i if cut_up else 0, *index, 0, 0), **mode))
        return lambda value: (ref, 0, None, tuple(0 if bit in fixed else value[bit] for bit in bits))


def combine(flows, steps):
    operands, plans, sizes = Operands(), [], {}
    for flow in flows:
        bits = flow.plan.pop(0)
        rest = [bit for bit in flow.left if bit not in bits]
        cut_up = steps if steps > 1 and flow.lead % steps == 0 else 0
        gone = {bit: 0 for bit in range(64) if bit not in flow.left}
        fixed = {**gone, bits[0]: 1} if len(bits) == 1 else gone
        finders = [operands.finder(flow, term, fixed, cut_up) for term in flow.terms]
        plans.append((flow, bits, rest, cut_up, gone, finders))
        for mask in masks_of(bits):
            size = flow.lead << len(rest)
            key = mask if steps == 1 else (mask, id(flow))
            sizes.setdefault(key, []).append((flow, size, cut_up and size // cut_up, mask))
    outputs, out_specs = [], []
    for members in sizes.values():
        shape = (sum(size for _, size, _, _ in members), members[0][0].rows, members[0][0].columns)
        outputs.append(jax.ShapeDtypeStruct(shape, jnp.bfloat16))
        cut = members[0][2]
        out_specs.append(
            pl.BlockSpec((cut, *shape[1:]), lambda i: (i, 0, 0)) if cut
            else pl.BlockSpec(shape, lambda i: (0, 0, 0), pipeline_mode=pl.Buffered(1))
        )
    work = []
    for flow, bits, rest, cut_up, gone, finders in plans:
        targets = []
        for number, members in enumerate(sizes.values()):
            offset = 0
            for member, size, _, mask in members:
                if member is flow:
                    sources = []
                    for at in range(1 << len(rest)):
                        value = {bit: (at >> (len(rest) - 1 - e)) & 1 for e, bit in enumerate(rest)}
                        value.update(gone)
                        value.update({bit: int(bit in mask) for bit in bits})
                        sources.append([find(value) for find in finders])
                    targets.append((len(operands.arrays) + number, offset, 1 << len(rest), sources))
                offset += size
        work.append((flow.lead, cut_up, targets))
        flow.left = rest
    results = pl.pallas_call(
        functools.partial(combine_kernel, work=work, steps=steps),
        grid=(steps,),
        in_specs=operands.specs,
        out_specs=out_specs,
        out_shape=outputs,
        compiler_params=pltpu.CompilerParams(vmem_limit_bytes=60 << 20),
        cost_estimate=pl.CostEstimate(flops=1 << 20, bytes_accessed=8 << 20, transcendentals=0),
        name="combine",
    )(*operands.arrays)
    return [
        (members[0][3], array, [(flow, size) for flow, size, _, _ in members])
        for members, array in zip(sizes.values(), results)
    ]


def leave(flows, value=None, steps=1):
    flows = [flow for flow in flows if flow.plan]
    starting = [flow for flow in flows if flow.plan[0] == (-1,)]
    waiting = [flow for flow in flows if flow.plan[0] == ()]
    going = [flow for flow in flows if flow not in starting and flow not in waiting]
    for flow in starting + waiting:
        flow.plan.pop(0)
    sent = combine(going, steps) if going else []
    sent += [((-1,), flow.first, [(flow, flow.first.shape[0])]) for flow in starting]
    value, arrays = lax.optimization_barrier((value, [array for _, array, _ in sent]))
    return value, [(crossed(array, mask), members) for array, (mask, _, members) in zip(arrays, sent)]


def arrive(transfers, value=None):
    moved, value = lax.optimization_barrier(([array for array, _ in transfers], value))
    for array, (_, members) in zip(moved, transfers):
        at = 0
        for flow, size in members:
            flow.terms.append((array, list(flow.left), at if len(members) > 1 else None))
            at += size
    return value


def finish_kernel(*refs, work, gains, count):
    inputs, outputs = refs[:count], refs[count:]
    for terms, targets in work:
        for lead, (target, row, column, width, parts) in enumerate(targets):
            total = None
            for ref, begin, per, place in terms:
                where = (lead, *place) if per is None else (begin + lead * per + place,)
                value = inputs[ref][where].astype(jnp.float32)
                total = value if total is None else total + value
            for part in range(parts):
                piece = slice(part * width, (part + 1) * width)
                begin = column + part * (outputs[target].shape[1] // parts if parts > 1 else 0)
                outputs[target][row:row + total.shape[0], begin:begin + width] = total[:, piece]
    for source, weight, gain, target in gains:
        product = inputs[weight][...] * outputs[source][...]
        sums = lax.dot_general(jnp.ones((8, product.shape[1]), jnp.float32), product, NT,
                               precision=lax.Precision.HIGHEST, preferred_element_type=jnp.float32)
        outputs[target][...] = sums[:1] / inputs[gain][...]


def finish(plans, sizes, gained):
    operands, work, gains = Operands(), [], []
    gone = {bit: 0 for bit in range(64)}
    for flow, targets in plans:
        finders = [operands.finder(flow, term, gone, False) for term in flow.terms]
        work.append(([find(gone) for find in finders], targets))
    sizes = list(sizes)
    for source, *arrays in gained:
        at = [operands.add(array, pl.BlockSpec(array.shape, lambda i: (0, 0), pipeline_mode=pl.Buffered(1))) for array in arrays]
        gains.append((source, *at, len(sizes)))
        sizes.append((1, sizes[source][0]))
    return pl.pallas_call(
        functools.partial(finish_kernel, work=work, gains=gains, count=len(operands.arrays)),
        grid=(1,),
        in_specs=operands.specs,
        out_specs=[pl.BlockSpec(size, lambda i: (0, 0), pipeline_mode=pl.Buffered(1)) for size in sizes],
        out_shape=[jax.ShapeDtypeStruct(size, jnp.float32) for size in sizes],
        compiler_params=pltpu.CompilerParams(vmem_limit_bytes=60 << 20),
        cost_estimate=pl.CostEstimate(flops=1 << 20, bytes_accessed=4 << 20, transcendentals=0),
        name="finish",
    )(*operands.arrays)


def body(tokens, segments, cotangent, gain_attn, w_qkv, w_out, gain_ffn, w_up, w_down):
    chips = lax.axis_size("dp")
    shards = 2 * chips
    dp, seq = lax.axis_index("dp"), lax.axis_index("seq")
    here = jnp.stack([dp & 1, (dp >> 1) * 2 + seq, seq]).astype(jnp.int32)
    there = jnp.stack([dp & 1, (dp >> 1) * 2 + seq, 1 - seq]).astype(jnp.int32)
    far = tuple(range(2, chips.bit_length() - 1))
    rest = [far[at:at + 2] for at in range(2, len(far), 2)]

    x_kept, x_sent = split_window(tokens)
    segments, cotangent, x_sent = lax.optimization_barrier((segments, cotangent, x_sent))
    seg_kept, seg_sent = split_window(segments)
    gy_kept, gy_sent = split_window(cotangent)
    x_other, seg_other, gy_other = swapped(x_sent), swapped(seg_sent), swapped(gy_sent)
    seg = jnp.where(seq == 0, jnp.concatenate([seg_kept, seg_other]), jnp.concatenate([seg_other, seg_kept]))[None]
    first, last = bounds(seg, 256, 256)
    gain_one, gain_two = gain_attn[None], gain_ffn[None]
    begin = shard_at(here, 0, 0) * (w_out.shape[0] // shards)
    shard_of = lambda array: lax.dynamic_slice_in_dim(array, begin, w_out.shape[0] // shards, 0).astype(jnp.float32)
    weights = [shard_of(w_qkv), shard_of(gain_attn)[None], shard_of(w_up), shard_of(gain_ffn)[None]]
    x_other, weights = lax.optimization_barrier((x_other, weights))
    early = before(here, x_kept, gain_one, w_qkv, shards)
    proj, low_t = before(there, x_other, gain_one, w_qkv, shards, early)
    mixture, lse = attend(first, seg, proj)
    out_kept, out_sent, gx, go, keep_up, send_up, keep_down, send_down, keep_out, send_out = middle(
        here, (x_kept, x_other), mixture, (gy_kept, gy_other), w_out, gain_two, w_up, w_down, shards
    )

    core, near = (-1,), [(bit,) for bit in far]
    up = Flow(here, keep_up, send_up, chips, [core, (1,), (0,), *near])
    down = Flow(here, keep_down, send_down, chips, [core, *near[:1], (1,), (0,), *near[1:]], 4)
    heads = []

    def heads_back(begin, count, plan, riders=()):
        *grads, keep, send = attend_back(begin, count, last, seg, proj, go, mixture, lse, low_t, shards, riders)
        heads.append(grads)
        return Flow(here, keep, send, chips, [core, *plan])

    (go, out_sent), moving = leave([up, down], (go, out_sent))
    out_other = swapped(out_sent)
    one = heads_back(0, 2, [*near[:1], (0,), (1,), *near[1:]], (keep_out, send_out))
    out_other = arrive(moving, out_other)
    (go, out_other), moving = leave([up, down, one], (go, out_other), 2)
    two = heads_back(2, 3, [(1,), *near[:1], (0, *far[1:2]), *rest])
    arrive(moving)
    go, moving = leave([up, down, one, two], go, 2)
    three = heads_back(5, 1, [(1, *far[:1]), (0, *far[1:2]), *rest])
    arrive(moving)
    flows = [up, down, one, two, three]
    gx, moving = leave(flows, gx)
    pieces = [piece for grads in heads for piece in grads]
    other_rows = after(there, x_other, gain_one, gx, w_qkv, pieces)
    other_rows = arrive(moving, other_rows)
    rows_back = swapped(other_rows)
    gx, moving = leave(flows, gx)
    kept_rows = after(here, x_kept, gain_one, gx, w_qkv, pieces)
    kept_rows, rows_back = arrive(moving, (kept_rows, rows_back))
    rows, width = up.rows, w_out.shape[1]
    w_qkv_rows, gain_one_rows, w_up_rows, gain_two_rows = weights

    def finish_ffn(w_rows):
        return finish([
            (up, [(0, 0, lead * PART, PART, 1) for lead in range(up.lead)]),
            (down, [(1, (lead % 4) * rows, (lead // 4) * PART, PART, 1) for lead in range(down.lead)]),
        ], [(rows, up.lead * PART), (4 * rows, width)], [(0, w_rows, gain_two_rows)])

    soon = not (up.plan or down.plan)
    (kept_rows, rows_back, w_up_rows), moving = leave(flows, (kept_rows, rows_back, w_up_rows))
    ffn_grads = finish_ffn(w_up_rows) if soon else None
    grad_tokens = joined(kept_rows, rows_back)
    while True:
        ffn_grads, grad_tokens = arrive(moving, (ffn_grads, grad_tokens))
        if not any(flow.plan for flow in flows):
            break
        _, moving = leave(flows)
    grad_up, grad_down, grad_gain_ffn = ffn_grads or finish_ffn(w_up_rows)
    out_lead, group = width // PART, iter(range(64))
    of_group = lambda flow, extra=0: [(0, 0, next(group) * SMALL, SMALL, 3) for _ in range(flow.lead - extra)]
    grad_qkv, grad_out, grad_gain_attn = finish([
        (one, of_group(one, out_lead) + [(1, 0, lead * PART, PART, 1) for lead in range(out_lead)]),
        (two, of_group(two)),
        (three, of_group(three)),
    ], [(rows, 3 * width), (rows, width)], [(0, w_qkv_rows, gain_one_rows)])
    return (
        joined(out_kept, out_other),
        grad_tokens,
        grad_qkv,
        grad_out,
        grad_up,
        grad_down,
        grad_gain_attn[0],
        grad_gain_ffn[0],
    )


def solution(mesh):
    placed = (
        P("dp", "seq", None),
        P("dp", "seq"),
        P("dp", "seq", None),
        P(),
        P(),
        P(),
        P(),
        P(),
        P(),
    )
    return jax.shard_map(
        body,
        mesh=mesh,
        in_specs=placed,
        out_specs=(
            P("dp", "seq", None),
            P("dp", "seq", None),
            P(("dp", "seq"), None),
            P(("dp", "seq"), None),
            P(("dp", "seq"), None),
            P(("dp", "seq"), None),
            P(("dp", "seq")),
            P(("dp", "seq")),
        ),
        check_vma=False,
    )
```

```python
import functools

import jax
import jax.numpy as jnp
from jax import lax
from jax.experimental import pallas as pl
from jax.experimental.pallas import tpu as pltpu
from jax.sharding import PartitionSpec as P

HEAD_DIM = 32
GROUP = 8
LANES = GROUP * HEAD_DIM
SMALL = 128
PART = 3 * SMALL
GRAIN = 128
masked_score = -1e30
epsilon = 1e-05
SCALE = HEAD_DIM ** (-0.5)
SCALE2 = SCALE * 1.4426950408889634
NT = (((1,), (1,)), ((), ()))
NN = (((1,), (0,)), ((), ()))


def mm(a, b, dims=NN):
    return lax.dot_general(a, b, dims, preferred_element_type=jnp.float32)


def attend_kernel(first, seg_ref, q_ref, k_ref, v_ref, o_ref, lse_ref, bias, total, *, bq, unroll):
    i, g = pl.program_id(0), pl.program_id(1)
    length = k_ref.shape[0]
    start = first[i]
    lane = lax.div(lax.broadcasted_iota(jnp.int32, (1, LANES), 1), HEAD_DIM)
    lane_head = lax.broadcasted_iota(jnp.int32, (1, 128), 1)

    def span(width):
        begin = pl.multiple_of(start * GRAIN, GRAIN)

        @pl.when(g == 0)
        def _():
            seg_q = jnp.transpose(jnp.broadcast_to(seg_ref[0:1, pl.ds(pl.multiple_of(i * bq, bq), bq)], (128, bq)))[:, 0:1]
            place_q = i * bq + lax.broadcasted_iota(jnp.int32, (bq, width), 0)
            place_k = begin + lax.broadcasted_iota(jnp.int32, (bq, width), 1)
            allowed = (place_k <= place_q) & (seg_q == seg_ref[0:1, pl.ds(begin, width)])
            bias[:, :width] = jnp.where(allowed, 0.0, masked_score)

        total[...] = jnp.zeros_like(total)

        def head(h, logs):
            query = jnp.where(lane == h, q_ref[...], jnp.zeros((), jnp.bfloat16))
            s = mm(query, k_ref[pl.ds(begin, width), :], NT) * SCALE2 + bias[:, :width]
            top = jnp.max(s, axis=-1, keepdims=True)
            e = jnp.exp2(s - top)
            row = jnp.sum(e, axis=-1, keepdims=True)
            out = mm(e.astype(jnp.bfloat16), v_ref[pl.ds(begin, width), :])
            total[...] = jnp.where(lane == h, out * (1.0 / row), total[...])
            place = jnp.where(h < GROUP // 2, h, h + GROUP // 2)
            return jnp.where(lane_head == place, top + jnp.log2(row), logs)

        logs = lax.fori_loop(0, GROUP, head, jnp.zeros((bq, 128), jnp.float32), unroll=unroll)
        o_ref[...] = total[...].astype(o_ref.dtype)
        lse_ref[...] = jnp.transpose(logs)[:2 * GROUP]

    blocks = (i + 1) * (bq // GRAIN) - start
    for count in range(bq // GRAIN, length // GRAIN + 1):
        pl.when(blocks == count)(functools.partial(span, count * GRAIN))


def attend(first, seg, proj, bq=256, unroll=8):
    length, width = proj.shape
    groups = width // 3 // LANES
    grid_spec = pltpu.PrefetchScalarGridSpec(
        num_scalar_prefetch=1,
        grid=(length // bq, groups),
        in_specs=[
            pl.BlockSpec((1, length), lambda i, g, *_: (0, 0)),
            pl.BlockSpec((bq, LANES), lambda i, g, *_: (i, g)),
            pl.BlockSpec((length, LANES), lambda i, g, *_: (0, groups + g)),
            pl.BlockSpec((length, LANES), lambda i, g, *_: (0, 2 * groups + g)),
        ],
        out_specs=[
            pl.BlockSpec((bq, LANES), lambda i, g, *_: (i, g)),
            pl.BlockSpec((2 * GROUP, bq), lambda i, g, *_: (g, i)),
        ],
        scratch_shapes=[pltpu.VMEM((bq, length), jnp.float32), pltpu.VMEM((bq, LANES), jnp.float32)],
    )
    return pl.pallas_call(
        functools.partial(attend_kernel, bq=bq, unroll=unroll),
        grid_spec=grid_spec,
        out_shape=[
            jax.ShapeDtypeStruct((length, width // 3), jnp.bfloat16),
            jax.ShapeDtypeStruct((groups * 2 * GROUP, length), jnp.float32),
        ],
        compiler_params=pltpu.CompilerParams(vmem_limit_bytes=48 << 20),
        cost_estimate=pl.CostEstimate(flops=28 << 30, bytes_accessed=8 << 20, transcendentals=24 * length * length),
        name="attend",
    )(first, seg, proj, proj, proj)


def attend_back_kernel(last, place, seg_ref, q_ref, k_ref, v_ref, up_ref, o_ref, lse_ref, low_t_ref, *refs, bk):
    *riders, gq_ref, gk_ref, gv_ref, keep_ref, send_ref, bias, inner, key_t, value_t, q_t, up_t, gq_t, gk, gv, grad = refs
    g, j = pl.program_id(0), pl.program_id(1)
    length, lanes = q_ref.shape
    heads = lanes // HEAD_DIM
    lane = lax.div(lax.broadcasted_iota(jnp.int32, (1, lanes), 1), HEAD_DIM)

    @pl.when(j == 0)
    def _():
        gq_t[...] = jnp.zeros_like(gq_t)
        q_t[...] = jnp.transpose(q_ref[...])
        up_t[...] = jnp.transpose(up_ref[...])
        product = up_t[...].astype(jnp.float32) * jnp.transpose(o_ref[...]).astype(jnp.float32)
        for h in range(heads):
            rows = slice(h * HEAD_DIM, (h + 1) * HEAD_DIM)
            inner[h:h + 1, :] = jnp.sum(product[rows], axis=0, keepdims=True)

    key_t[...] = jnp.transpose(k_ref[...])
    value_t[...] = jnp.transpose(v_ref[...])

    def span(width):
        begin = pl.multiple_of(j * bk, bk)
        here = pl.ds(begin, width)

        @pl.when(g == 0)
        def _():
            seg_k = jnp.transpose(jnp.broadcast_to(seg_ref[0:1, pl.ds(begin, bk)], (128, bk)))[:, 0:1]
            place_k = lax.broadcasted_iota(jnp.int32, (bk, width), 0)
            place_q = lax.broadcasted_iota(jnp.int32, (bk, width), 1)
            allowed = (place_k <= place_q) & (seg_k == seg_ref[0:1, here])
            bias[j, :, :width] = jnp.where(allowed, 0.0, masked_score)

        for h in range(heads):
            rows = slice(h * HEAD_DIM, (h + 1) * HEAD_DIM)
            key, value = jnp.transpose(key_t[rows, :]), jnp.transpose(value_t[rows, :])
            s = mm(key, q_t[rows, here]) * SCALE2 + (bias[j, :, :width] - lse_ref[h:h + 1, here])
            p = jnp.exp2(s)
            dp = mm(value, up_t[rows, here])
            ds = (p * (dp - inner[h:h + 1, here])).astype(jnp.bfloat16)
            grad_v = mm(p.astype(jnp.bfloat16), up_ref[here, :])
            grad_k = mm(ds, q_ref[here, :])
            gv[...] = jnp.where(lane == h, grad_v, gv[...]) if h else grad_v
            gk[...] = jnp.where(lane == h, grad_k, gk[...]) if h else grad_k
            gq_t[rows, here] += mm(key_t[rows, :], ds)

    blocks = last[j] - j * (bk // GRAIN)
    for count in range(bk // GRAIN, length // GRAIN + 1):
        pl.when(blocks == count)(functools.partial(span, count * GRAIN))

    here = pl.ds(pl.multiple_of(j * bk, bk), bk)
    gk_ref[here, :] = (gk[...] * SCALE).astype(gk_ref.dtype)
    gv_ref[here, :] = gv[...].astype(gv_ref.dtype)

    @pl.when(j == pl.num_programs(1) - 1)
    def _():
        gq_ref[...] = jnp.transpose((gq_t[...] * SCALE).astype(gq_ref.dtype))
        joined = jnp.concatenate([gq_ref[...], gk_ref[...], gv_ref[...]], axis=1)
        grad[...] = mm(low_t_ref[...], joined)
        cut(place, grad, keep_ref, send_ref, g)

    if riders:
        @pl.when((g == 0) & (j == 0))
        def _():
            extra = riders[0].shape[0]
            for rider, target in zip(riders, (keep_ref, send_ref)):
                target[-extra:] = rider[...]


def attend_back(begin, count, last, place, seg, proj, up, o, lse, low_t, shards, riders=(), bk=256):
    length, width = proj.shape
    groups = width // 3 // SMALL
    half = width // 6
    group = lambda g: g + begin
    whole = lambda offset: pl.BlockSpec((length, SMALL), lambda g, j, *_: (0, offset + group(g)))
    block = lambda offset: pl.BlockSpec((bk, SMALL), lambda g, j, *_: (j, offset + group(g)))
    fixed = lambda *shape: pl.BlockSpec(shape, lambda g, j, *_: (0, 0), pipeline_mode=pl.Buffered(1))
    out = pl.BlockSpec((length, SMALL), lambda g, j, *_: (0, g))
    rows = 2 * half // shards
    piece = (half, PART) if rows % 8 else (shards // 2, rows, PART)
    lead = count + (riders[0].shape[0] if riders else 0)
    all_of = lambda *size: pl.BlockSpec(size, lambda g, j, *_: (0,) * len(size), pipeline_mode=pl.Buffered(1))
    split = all_of(lead, *piece)
    grid_spec = pltpu.PrefetchScalarGridSpec(
        num_scalar_prefetch=2,
        grid=(count, length // bk),
        in_specs=[
            fixed(1, length),
            whole(0),
            block(groups),
            block(2 * groups),
            whole(0),
            whole(0),
            pl.BlockSpec((8, length), lambda g, j, *_: (group(g), 0)),
            fixed(2 * half, length),
            *[all_of(*rider.shape) for rider in riders],
        ],
        out_specs=[out, out, out, split, split],
        scratch_shapes=[
            pltpu.VMEM((length // bk, bk, length), jnp.float32),
            pltpu.VMEM((8, length), jnp.float32),
            pltpu.VMEM((SMALL, bk), jnp.bfloat16),
            pltpu.VMEM((SMALL, bk), jnp.bfloat16),
            pltpu.VMEM((SMALL, length), jnp.bfloat16),
            pltpu.VMEM((SMALL, length), jnp.bfloat16),
            pltpu.VMEM((SMALL, length), jnp.float32),
            pltpu.VMEM((bk, SMALL), jnp.float32),
            pltpu.VMEM((bk, SMALL), jnp.float32),
            pltpu.VMEM((2 * half, PART), jnp.float32),
        ],
    )
    heads = jax.ShapeDtypeStruct((length, count * SMALL), jnp.bfloat16)
    parts = jax.ShapeDtypeStruct((lead, *piece), jnp.bfloat16)
    return pl.pallas_call(
        functools.partial(attend_back_kernel, bk=bk),
        grid_spec=grid_spec,
        out_shape=[heads, heads, heads, parts, parts],
        compiler_params=pltpu.CompilerParams(vmem_limit_bytes=60 << 20),
        cost_estimate=pl.CostEstimate(flops=(count * 10) << 30, bytes_accessed=8 << 20, transcendentals=count * 4 * length * length),
        name="attend_back",
    )(last, place, seg, proj, proj, proj, up, o, lse, low_t, *riders)


def bounds(seg, bq, bk):
    row = seg[0]
    first = jnp.sum(row[None, :] < row[::bq][:, None], axis=1) // GRAIN
    last = (jnp.sum(row[None, :] <= row[bk - 1::bk][:, None], axis=1) + GRAIN - 1) // GRAIN
    return first.astype(jnp.int32), last.astype(jnp.int32)


def gelu_pair(u):
    c = 0.7978845608028654
    square = u * u
    t = jnp.tanh(u * (c + (c * 0.044715) * square))
    half = 0.5 * t + 0.5
    slope = half + (0.5 * u) * (1.0 - t * t) * (c + (3 * c * 0.044715) * square)
    return u * half, slope


def row_stats(values):
    mean = jnp.mean(values, axis=-1, keepdims=True)
    centred = values - mean
    return mean, lax.rsqrt(jnp.mean(centred * centred, axis=-1, keepdims=True) + epsilon)


def norm_back(values, gain, upstream):
    mean, rate = row_stats(values)
    unit = (values - mean) * rate
    inner = upstream * gain
    level = jnp.mean(inner, axis=-1, keepdims=True)
    along = jnp.mean(inner * unit, axis=-1, keepdims=True)
    return rate * (inner - level - unit * along)


def shard_at(place, core_rel, q_rel):
    core, q = place[0] ^ core_rel, place[1] ^ q_rel
    return ((q >> 1) * 2 + core) * 2 + (q & 1)


def cut(place, grad, keep, send, first):
    half = grad.shape[0] // 2
    for at in range(grad.shape[1] // PART):
        columns = slice(at * PART, (at + 1) * PART)
        if len(keep.shape) == 3:
            keep[first + at] = grad[:half, columns].astype(keep.dtype)
            send[first + at] = grad[half:, columns].astype(send.dtype)
        else:
            chips, rows = keep.shape[1:3]
            for rel, target in enumerate((keep, send)):
                for q in range(chips):
                    source = pl.ds(pl.multiple_of(shard_at(place, rel, q) * rows, 8), rows)
                    target[first + at, q] = grad[source, columns].astype(target.dtype)


def before_kernel(place, x_ref, gain_ref, w_ref, *refs, shards, block):
    proj_ref, low_t_ref, low = refs[-3:]
    length, width = x_ref.shape

    @pl.when(pl.program_id(0) == 0)
    def _():
        for at in range(0, length, block):
            at = slice(at, at + block)
            values = x_ref[at, :].astype(jnp.float32)
            mean, rate = row_stats(values)
            normed = ((values - mean) * rate * gain_ref[...]).astype(jnp.bfloat16)
            low[at, :] = normed
            low_t_ref[:, at] = jnp.transpose(normed)

    proj_ref[...] = mm(low[...], w_ref[...]).astype(jnp.bfloat16)


def before(place, x, gain, w, shards, so_far=(), chunk=768, block=256):
    length, width = x.shape
    columns = w.shape[1]
    whole = lambda *shape: pl.BlockSpec(shape, lambda c, *_: (0, 0), pipeline_mode=pl.Buffered(1))
    grid_spec = pltpu.PrefetchScalarGridSpec(
        num_scalar_prefetch=1,
        grid=(columns // chunk,),
        in_specs=[whole(length, width), whole(1, width), pl.BlockSpec((width, chunk), lambda c, *_: (0, c))]
        + [pl.BlockSpec(memory_space=pl.ANY)] * len(so_far),
        out_specs=[
            pl.BlockSpec((length, chunk), lambda c, place: (place[2], c)),
            pl.BlockSpec((width, length), lambda c, place: (0, place[2])),
        ],
        scratch_shapes=[pltpu.VMEM((length, width), jnp.bfloat16)],
    )
    return pl.pallas_call(
        functools.partial(before_kernel, shards=shards, block=block),
        grid_spec=grid_spec,
        out_shape=[
            jax.ShapeDtypeStruct((2 * length, columns), jnp.bfloat16),
            jax.ShapeDtypeStruct((width, 2 * length), jnp.bfloat16),
        ],
        input_output_aliases={4 + at: at for at in range(len(so_far))},
        compiler_params=pltpu.CompilerParams(vmem_limit_bytes=60 << 20),
        cost_estimate=pl.CostEstimate(flops=2 * length * width * columns, bytes_accessed=12 << 20, transcendentals=length),
        name="before",
    )(place, x, gain, w, *so_far)


def middle_kernel(place, x_kept, x_other, o_ref, gy_kept, gy_other, w_out_ref, gain_ref, w_up_ref, w_down_ref,
                  out_kept, out_other, gx_ref, go_ref, keep_up, send_up, keep_down, send_down, keep_out, send_out,
                  gy, x1, low, low_t, total, back, whole, part, *, shards, block):
    c = pl.program_id(0)
    length, width = o_ref.shape
    chunk = w_down_ref.shape[0]
    pieces = [slice(at, at + block) for at in range(0, length, block)]
    rows = width // shards
    half, window = width // 2, length // 2
    kept = pl.ds(pl.multiple_of(place[2] * window, window), window)
    other = pl.ds(pl.multiple_of((1 - place[2]) * window, window), window)

    @pl.when(c == 0)
    def _():
        gy[kept, :] = gy_kept[...]
        gy[other, :] = gy_other[...]
        x1[kept, :] = x_kept[...].astype(jnp.float32)
        x1[other, :] = x_other[...].astype(jnp.float32)
        for at in pieces:
            values = x1[at, :] + mm(o_ref[at, :], w_out_ref[...])
            x1[at, :] = values
            mean, rate = row_stats(values)
            normed = ((values - mean) * rate * gain_ref[...]).astype(jnp.bfloat16)
            low[at, :] = normed
            low_t[:, at] = jnp.transpose(normed)
            total[at, :] = values
            back[at, :] = jnp.zeros_like(values)

    lifted, slopes = [], []
    for at in pieces:
        a, slope = gelu_pair(mm(low[at, :], w_up_ref[...]))
        a = a.astype(jnp.bfloat16)
        gu = (mm(gy[at, :], w_down_ref[...], NT) * slope).astype(jnp.bfloat16)
        total[at, :] += mm(a, w_down_ref[...])
        back[at, :] += mm(gu, w_up_ref[...], NT)
        lifted.append(jnp.transpose(a))
        slopes.append(gu)
    whole[...] = mm(low_t[...], jnp.concatenate(slopes, axis=0))
    cut(place, whole, keep_up, send_up, 0)
    grad_down = mm(jnp.concatenate(lifted, axis=1), gy[...])
    if rows % 8:
        for at in range(width // PART):
            for target, begin in ((keep_down, 0), (send_down, chunk // 2)):
                piece = grad_down[begin:begin + chunk // 2, at * PART:(at + 1) * PART]
                target[at] = piece.astype(jnp.bfloat16)
    else:
        part[...] = grad_down
        for rel, target in enumerate((keep_down, send_down)):
            for q_rel in range(4):
                q = (place[1] ^ q_rel) & 3
                source = (((q >> 1) * 2 + (place[0] ^ rel)) * 2 + (q & 1)) * 4 * rows
                for sub in range(4):
                    source_rows = pl.ds(pl.multiple_of(source + sub * rows, 8), rows)
                    for at in range(width // PART):
                        piece = part[source_rows, at * PART:(at + 1) * PART]
                        target[4 * at + sub, q_rel] = piece.astype(jnp.bfloat16)

    @pl.when(c == pl.num_programs(0) - 1)
    def _():
        branch = []
        out_kept[...] = total[kept, :].astype(jnp.bfloat16)
        out_other[...] = total[other, :].astype(jnp.bfloat16)
        for at in pieces:
            grad = gy[at, :].astype(jnp.float32) + norm_back(x1[at, :], gain_ref[...], back[at, :])
            grad = grad.astype(jnp.bfloat16)
            gx_ref[at, :] = grad
            branch.append(grad)
            go_ref[at, :] = mm(grad, w_out_ref[...], NT).astype(jnp.bfloat16)
            low_t[:, at] = jnp.transpose(o_ref[at, :])
        whole[...] = mm(low_t[...], jnp.concatenate(branch, axis=0))
        cut(place, whole, keep_out, send_out, 0)


def middle(place, x, o, gy, w_out, gain, w_up, w_down, shards, block=512):
    length, width = o.shape
    lift = w_up.shape[1]
    steps = 4
    chunk = lift // steps
    half, window = width // 2, length // 2
    at = (lambda c, place: c) if (width // shards) % 8 else (lambda c, place: c ^ (place[1] >> 2))
    whole = lambda *shape: pl.BlockSpec(shape, lambda c, *_: (0, 0), pipeline_mode=pl.Buffered(1))
    out = lambda *shape: pl.BlockSpec(shape, lambda c, *_: (0,) * len(shape), pipeline_mode=pl.Buffered(1))
    shape = jax.ShapeDtypeStruct
    rows = width // shards
    if rows % 8:
        up_shape, down_shape, out_shape = (lift // PART, half, PART), (width // PART, lift // 2, PART), (width // PART, half, PART)
        up = pl.BlockSpec((chunk // PART, half, PART), lambda c, place: (at(c, place), 0, 0))
        down = pl.BlockSpec((width // PART, chunk // 2, PART), lambda c, place: (0, c, 0))
    else:
        piece = (shards // 2, rows, PART)
        up_shape, down_shape, out_shape = (lift // PART, *piece), (lift // PART, *piece), (width // PART, *piece)
        up = pl.BlockSpec((chunk // PART, *piece), lambda c, place: (at(c, place), 0, 0, 0))
        down = pl.BlockSpec((lift // PART, 4, rows, PART), lambda c, place: (0, c, 0, 0))
    bf16 = jnp.bfloat16
    grid_spec = pltpu.PrefetchScalarGridSpec(
        num_scalar_prefetch=1,
        grid=(steps,),
        in_specs=[
            whole(window, width), whole(window, width), whole(length, width), whole(window, width),
            whole(window, width), whole(width, width), whole(1, width),
            pl.BlockSpec((width, chunk), lambda c, place: (0, at(c, place))),
            pl.BlockSpec((chunk, width), lambda c, place: (at(c, place), 0)),
        ],
        out_specs=[
            out(window, width), out(window, width), out(length, width), out(length, width), up, up, down, down,
            out(*out_shape), out(*out_shape),
        ],
        scratch_shapes=[
            pltpu.VMEM((length, width), bf16),
            pltpu.VMEM((length, width), jnp.float32),
            pltpu.VMEM((length, width), bf16),
            pltpu.VMEM((width, length), bf16),
            pltpu.VMEM((length, width), jnp.float32),
            pltpu.VMEM((length, width), jnp.float32),
            pltpu.VMEM((width, width), jnp.float32),
            pltpu.VMEM((chunk, width), jnp.float32),
        ],
    )
    return pl.pallas_call(
        functools.partial(middle_kernel, shards=shards, block=block),
        grid_spec=grid_spec,
        out_shape=[
            shape((window, width), bf16), shape((window, width), bf16),
            shape((length, width), bf16), shape((length, width), bf16),
            *[shape(size, bf16) for size in (up_shape, up_shape, down_shape, down_shape, out_shape, out_shape)],
        ],
        compiler_params=pltpu.CompilerParams(vmem_limit_bytes=60 << 20),
        cost_estimate=pl.CostEstimate(flops=12 * length * width * lift, bytes_accessed=40 << 20, transcendentals=length * lift),
        name="middle",
    )(place, *x, o, *gy, w_out, gain, w_up, w_down)


def after_kernel(place, x_ref, gain_ref, gx_ref, w_ref, *refs):
    out_ref = refs[-1]
    grads = jnp.concatenate([ref[...] for third in range(3) for ref in refs[third:-1:3]], axis=1)
    back = mm(grads, w_ref[...], NT)
    values = x_ref[...].astype(jnp.float32)
    out_ref[...] = (gx_ref[...].astype(jnp.float32) + norm_back(values, gain_ref[...], back)).astype(out_ref.dtype)


def after(place, x, gain, gx, w, pieces, block=256):
    length, width = x.shape
    steps = length // block
    rows = lambda columns: pl.BlockSpec((block, columns), lambda i, place: (place[2] * steps + i, 0))
    own = pl.BlockSpec((block, width), lambda i, place: (i, 0))
    whole = lambda *shape: pl.BlockSpec(shape, lambda i, place: (0, 0), pipeline_mode=pl.Buffered(1))
    grid_spec = pltpu.PrefetchScalarGridSpec(
        num_scalar_prefetch=1,
        grid=(steps,),
        in_specs=[own, whole(1, width), rows(width), whole(width, w.shape[1])] + [rows(piece.shape[1]) for piece in pieces],
        out_specs=own,
    )
    return pl.pallas_call(
        after_kernel,
        grid_spec=grid_spec,
        out_shape=jax.ShapeDtypeStruct((length, width), jnp.bfloat16),
        compiler_params=pltpu.CompilerParams(vmem_limit_bytes=60 << 20),
        cost_estimate=pl.CostEstimate(flops=6 * length * width * width, bytes_accessed=16 << 20, transcendentals=length),
        name="after",
    )(place, x, gain, gx, w, *pieces)


def swapped(block):
    return lax.ppermute(block, "seq", [(0, 1), (1, 0)])


def split_window(block):
    place = lax.axis_index("seq")
    take = lambda at: lax.dynamic_index_in_dim(block, at, 0, keepdims=False)
    return take(place), take(1 - place)


def joined(kept, other):
    place = lax.axis_index("seq")
    return jnp.where(place == 0, jnp.stack([kept, other]), jnp.stack([other, kept]))


def crossed(block, bits):
    step = sum(1 if bit == 0 else 2 if bit == -1 else 2 << bit for bit in bits)
    count = 2 * lax.axis_size("dp")
    return lax.ppermute(block, ("dp", "seq"), [(i, i ^ step) for i in range(count)])


def masks_of(bits):
    return [tuple(bit for e, bit in enumerate(bits) if number >> e & 1) for number in range(1, 1 << len(bits))]


def combine_kernel(*refs, work, steps):
    for lead, cut_up, targets in work:
        def one(index, carry):
            for target, offset, count, sources in targets:
                for at, terms in enumerate(sources):
                    total = None
                    for ref, begin, per, place in terms:
                        where = (index, *place) if per is None else (begin + index * per + place,)
                        value = refs[ref][where].astype(jnp.float32)
                        total = value if total is None else total + value
                    refs[target][offset + index * count + at] = total.astype(refs[target].dtype)
            return carry

        count = lead // steps if cut_up else lead

        def all_of(count=count, one=one):
            if sum(len(sources) for _, _, _, sources in targets) > 32:
                lax.fori_loop(0, count, one, 0)
            else:
                for index in range(count):
                    one(index, 0)

        if cut_up:
            all_of()
        elif steps > 1:
            @pl.when(pl.program_id(0) == 0)
            def _():
                all_of()
        else:
            all_of()


class Flow:
    def __init__(self, place, keep, send, chips, plan, blocks=0):
        if keep.ndim == 3:
            index = jnp.stack([shard_at(place, rel, q) for rel in range(2) for q in range(chips)])
            lead, half, columns = keep.shape
            both = jnp.stack([array.reshape(lead, max(blocks, 1), -1, columns) for array in (keep, send)], axis=2)
            parts = max(blocks, 1)
            both = both.reshape(lead, 2 * chips, parts, -1, columns)[:, index].transpose(0, 2, 1, 3, 4)
            both = both.reshape(lead * parts, 2 * chips, -1, columns)
            keep, send = both[:, :chips], both[:, chips:]
        self.lead, _, self.rows, self.columns = keep.shape
        self.left = list(reversed(range(chips.bit_length() - 1)))
        self.plan = list(plan)
        self.terms = [(keep.reshape(-1, self.rows, self.columns), list(self.left), None)]
        self.first = send.reshape(-1, self.rows, self.columns)


class Operands:
    def __init__(self):
        self.arrays, self.specs, self.seen = [], [], {}

    def add(self, array, spec):
        self.arrays.append(array)
        self.specs.append(spec)
        return len(self.arrays) - 1

    def finder(self, flow, term, fixed, cut_up):
        array, bits, offset = term
        if offset is not None:
            if id(array) not in self.seen:
                self.seen[id(array)] = self.add(array, pl.BlockSpec(array.shape, lambda i: (0, 0, 0), pipeline_mode=pl.Buffered(1)))
            ref, per = self.seen[id(array)], 1 << len(bits)
            return lambda value: (ref, offset, per, sum(value[bit] << (len(bits) - 1 - at) for at, bit in enumerate(bits)))
        view = array.reshape(flow.lead, *(2,) * len(bits), flow.rows, flow.columns)
        block = (flow.lead // cut_up if cut_up else flow.lead, *[1 if bit in fixed else 2 for bit in bits], flow.rows, flow.columns)
        index = tuple(fixed.get(bit, 0) for bit in bits)
        mode = {} if cut_up else dict(pipeline_mode=pl.Buffered(1))
        ref = self.add(view, pl.BlockSpec(block, lambda i: (i if cut_up else 0, *index, 0, 0), **mode))
        return lambda value: (ref, 0, None, tuple(0 if bit in fixed else value[bit] for bit in bits))


def combine(flows, steps):
    operands, plans, sizes = Operands(), [], {}
    for flow in flows:
        bits = flow.plan.pop(0)
        rest = [bit for bit in flow.left if bit not in bits]
        cut_up = steps if steps > 1 and flow.lead % steps == 0 else 0
        gone = {bit: 0 for bit in range(64) if bit not in flow.left}
        fixed = {**gone, bits[0]: 1} if len(bits) == 1 else gone
        finders = [operands.finder(flow, term, fixed, cut_up) for term in flow.terms]
        plans.append((flow, bits, rest, cut_up, gone, finders))
        for mask in masks_of(bits):
            size = flow.lead << len(rest)
            key = mask if steps == 1 else (mask, id(flow))
            sizes.setdefault(key, []).append((flow, size, cut_up and size // cut_up, mask))
    outputs, out_specs = [], []
    for members in sizes.values():
        shape = (sum(size for _, size, _, _ in members), members[0][0].rows, members[0][0].columns)
        outputs.append(jax.ShapeDtypeStruct(shape, jnp.bfloat16))
        cut = members[0][2]
        out_specs.append(
            pl.BlockSpec((cut, *shape[1:]), lambda i: (i, 0, 0)) if cut
            else pl.BlockSpec(shape, lambda i: (0, 0, 0), pipeline_mode=pl.Buffered(1))
        )
    work = []
    for flow, bits, rest, cut_up, gone, finders in plans:
        targets = []
        for number, members in enumerate(sizes.values()):
            offset = 0
            for member, size, _, mask in members:
                if member is flow:
                    sources = []
                    for at in range(1 << len(rest)):
                        value = {bit: (at >> (len(rest) - 1 - e)) & 1 for e, bit in enumerate(rest)}
                        value.update(gone)
                        value.update({bit: int(bit in mask) for bit in bits})
                        sources.append([find(value) for find in finders])
                    targets.append((len(operands.arrays) + number, offset, 1 << len(rest), sources))
                offset += size
        work.append((flow.lead, cut_up, targets))
        flow.left = rest
    results = pl.pallas_call(
        functools.partial(combine_kernel, work=work, steps=steps),
        grid=(steps,),
        in_specs=operands.specs,
        out_specs=out_specs,
        out_shape=outputs,
        compiler_params=pltpu.CompilerParams(vmem_limit_bytes=60 << 20),
        cost_estimate=pl.CostEstimate(flops=1 << 20, bytes_accessed=8 << 20, transcendentals=0),
        name="combine",
    )(*operands.arrays)
    return [
        (members[0][3], array, [(flow, size) for flow, size, _, _ in members])
        for members, array in zip(sizes.values(), results)
    ]


def leave(flows, value=None, steps=1):
    flows = [flow for flow in flows if flow.plan]
    starting = [flow for flow in flows if flow.plan[0] == (-1,)]
    waiting = [flow for flow in flows if flow.plan[0] == ()]
    going = [flow for flow in flows if flow not in starting and flow not in waiting]
    for flow in starting + waiting:
        flow.plan.pop(0)
    sent = combine(going, steps) if going else []
    sent += [((-1,), flow.first, [(flow, flow.first.shape[0])]) for flow in starting]
    value, arrays = lax.optimization_barrier((value, [array for _, array, _ in sent]))
    return value, [(crossed(array, mask), members) for array, (mask, _, members) in zip(arrays, sent)]


def arrive(transfers, value=None):
    moved, value = lax.optimization_barrier(([array for array, _ in transfers], value))
    for array, (_, members) in zip(moved, transfers):
        at = 0
        for flow, size in members:
            flow.terms.append((array, list(flow.left), at if len(members) > 1 else None))
            at += size
    return value


def finish_kernel(*refs, work, gains, count):
    inputs, outputs = refs[:count], refs[count:]
    for terms, targets in work:
        for lead, (target, row, column, width, parts) in enumerate(targets):
            total = None
            for ref, begin, per, place in terms:
                where = (lead, *place) if per is None else (begin + lead * per + place,)
                value = inputs[ref][where].astype(jnp.float32)
                total = value if total is None else total + value
            for part in range(parts):
                piece = slice(part * width, (part + 1) * width)
                begin = column + part * (outputs[target].shape[1] // parts if parts > 1 else 0)
                outputs[target][row:row + total.shape[0], begin:begin + width] = total[:, piece]
    for source, weight, gain, target in gains:
        product = inputs[weight][...] * outputs[source][...]
        sums = lax.dot_general(jnp.ones((8, product.shape[1]), jnp.float32), product, NT,
                               precision=lax.Precision.HIGHEST, preferred_element_type=jnp.float32)
        outputs[target][...] = sums[:1] / inputs[gain][...]


def finish(plans, sizes, gained):
    operands, work, gains = Operands(), [], []
    gone = {bit: 0 for bit in range(64)}
    for flow, targets in plans:
        finders = [operands.finder(flow, term, gone, False) for term in flow.terms]
        work.append(([find(gone) for find in finders], targets))
    sizes = list(sizes)
    for source, *arrays in gained:
        at = [operands.add(array, pl.BlockSpec(array.shape, lambda i: (0, 0), pipeline_mode=pl.Buffered(1))) for array in arrays]
        gains.append((source, *at, len(sizes)))
        sizes.append((1, sizes[source][0]))
    return pl.pallas_call(
        functools.partial(finish_kernel, work=work, gains=gains, count=len(operands.arrays)),
        grid=(1,),
        in_specs=operands.specs,
        out_specs=[pl.BlockSpec(size, lambda i: (0, 0), pipeline_mode=pl.Buffered(1)) for size in sizes],
        out_shape=[jax.ShapeDtypeStruct(size, jnp.float32) for size in sizes],
        compiler_params=pltpu.CompilerParams(vmem_limit_bytes=60 << 20),
        cost_estimate=pl.CostEstimate(flops=1 << 20, bytes_accessed=4 << 20, transcendentals=0),
        name="finish",
    )(*operands.arrays)


def body(tokens, segments, cotangent, gain_attn, w_qkv, w_out, gain_ffn, w_up, w_down):
    chips = lax.axis_size("dp")
    shards = 2 * chips
    dp, seq = lax.axis_index("dp"), lax.axis_index("seq")
    here = jnp.stack([dp & 1, (dp >> 1) * 2 + seq, seq]).astype(jnp.int32)
    there = jnp.stack([dp & 1, (dp >> 1) * 2 + seq, 1 - seq]).astype(jnp.int32)
    far = tuple(range(2, chips.bit_length() - 1))
    rest = [far[at:at + 2] for at in range(2, len(far), 2)]

    x_kept, x_sent = split_window(tokens)
    segments, cotangent, x_sent = lax.optimization_barrier((segments, cotangent, x_sent))
    seg_kept, seg_sent = split_window(segments)
    gy_kept, gy_sent = split_window(cotangent)
    x_other, seg_other, gy_other = swapped(x_sent), swapped(seg_sent), swapped(gy_sent)
    seg = jnp.where(seq == 0, jnp.concatenate([seg_kept, seg_other]), jnp.concatenate([seg_other, seg_kept]))[None]
    first, last = bounds(seg, 256, 256)
    gain_one, gain_two = gain_attn[None], gain_ffn[None]
    begin = shard_at(here, 0, 0) * (w_out.shape[0] // shards)
    shard_of = lambda array: lax.dynamic_slice_in_dim(array, begin, w_out.shape[0] // shards, 0).astype(jnp.float32)
    weights = [shard_of(w_qkv), shard_of(gain_attn)[None], shard_of(w_up), shard_of(gain_ffn)[None]]
    x_other, weights = lax.optimization_barrier((x_other, weights))
    early = before(here, x_kept, gain_one, w_qkv, shards)
    proj, low_t = before(there, x_other, gain_one, w_qkv, shards, early)
    mixture, lse = attend(first, seg, proj)
    out_kept, out_sent, gx, go, keep_up, send_up, keep_down, send_down, keep_out, send_out = middle(
        here, (x_kept, x_other), mixture, (gy_kept, gy_other), w_out, gain_two, w_up, w_down, shards
    )

    core, near = (-1,), [(bit,) for bit in far]
    up = Flow(here, keep_up, send_up, chips, [core, (1,), (0,), *near])
    down = Flow(here, keep_down, send_down, chips, [core, *near[:1], (1,), (0,), *near[1:]], 4)
    heads = []

    def heads_back(begin, count, plan, riders=()):
        *grads, keep, send = attend_back(begin, count, last, here, seg, proj, go, mixture, lse, low_t, shards, riders)
        heads.append(grads)
        return Flow(here, keep, send, chips, [core, *plan])

    (go, out_sent), moving = leave([up, down], (go, out_sent))
    out_other = swapped(out_sent)
    one = heads_back(0, 2, [*near[:1], (0,), (1,), *near[1:]], (keep_out, send_out))
    out_other = arrive(moving, out_other)
    (go, out_other), moving = leave([up, down, one], (go, out_other), 2)
    two = heads_back(2, 3, [(1,), *near[:1], (0, *far[1:2]), *rest])
    arrive(moving)
    go, moving = leave([up, down, one, two], go, 2)
    three = heads_back(5, 1, [(1, *far[:1]), (0, *far[1:2]), *rest])
    arrive(moving)
    flows = [up, down, one, two, three]
    gx, moving = leave(flows, gx)
    pieces = [piece for grads in heads for piece in grads]
    other_rows = after(there, x_other, gain_one, gx, w_qkv, pieces)
    other_rows = arrive(moving, other_rows)
    rows_back = swapped(other_rows)
    gx, moving = leave(flows, gx)
    kept_rows = after(here, x_kept, gain_one, gx, w_qkv, pieces)
    kept_rows, rows_back = arrive(moving, (kept_rows, rows_back))
    rows, width = up.rows, w_out.shape[1]
    w_qkv_rows, gain_one_rows, w_up_rows, gain_two_rows = weights

    def finish_ffn(w_rows):
        return finish([
            (up, [(0, 0, lead * PART, PART, 1) for lead in range(up.lead)]),
            (down, [(1, (lead % 4) * rows, (lead // 4) * PART, PART, 1) for lead in range(down.lead)]),
        ], [(rows, up.lead * PART), (4 * rows, width)], [(0, w_rows, gain_two_rows)])

    soon = not (up.plan or down.plan)
    (kept_rows, rows_back, out_other, w_up_rows), moving = leave(flows, (kept_rows, rows_back, out_other, w_up_rows))
    ffn_grads = finish_ffn(w_up_rows) if soon else None
    grad_tokens, outputs = joined(kept_rows, rows_back), joined(out_kept, out_other)
    while True:
        ffn_grads, grad_tokens, outputs = arrive(moving, (ffn_grads, grad_tokens, outputs))
        if not any(flow.plan for flow in flows):
            break
        _, moving = leave(flows)
    grad_up, grad_down, grad_gain_ffn = ffn_grads or finish_ffn(w_up_rows)
    out_lead, group = width // PART, iter(range(64))
    of_group = lambda flow, extra=0: [(0, 0, next(group) * SMALL, SMALL, 3) for _ in range(flow.lead - extra)]
    grad_qkv, grad_out, grad_gain_attn = finish([
        (one, of_group(one, out_lead) + [(1, 0, lead * PART, PART, 1) for lead in range(out_lead)]),
        (two, of_group(two)),
        (three, of_group(three)),
    ], [(rows, 3 * width), (rows, width)], [(0, w_qkv_rows, gain_one_rows)])
    return (
        outputs,
        grad_tokens,
        grad_qkv,
        grad_out,
        grad_up,
        grad_down,
        grad_gain_attn[0],
        grad_gain_ffn[0],
    )


def solution(mesh):
    placed = (
        P("dp", "seq", None),
        P("dp", "seq"),
        P("dp", "seq", None),
        P(),
        P(),
        P(),
        P(),
        P(),
        P(),
    )
    return jax.shard_map(
        body,
        mesh=mesh,
        in_specs=placed,
        out_specs=(
            P("dp", "seq", None),
            P("dp", "seq", None),
            P(("dp", "seq"), None),
            P(("dp", "seq"), None),
            P(("dp", "seq"), None),
            P(("dp", "seq"), None),
            P(("dp", "seq")),
            P(("dp", "seq")),
        ),
        check_vma=False,
    )
```

```python
import functools

import jax
import jax.numpy as jnp
from jax import lax
from jax.experimental import pallas as pl
from jax.experimental.pallas import tpu as pltpu
from jax.sharding import PartitionSpec as P

HEAD_DIM = 32
GROUP = 8
LANES = GROUP * HEAD_DIM
SMALL = 128
PART = 3 * SMALL
GRAIN = 128
masked_score = -1e30
epsilon = 1e-05
SCALE = HEAD_DIM ** (-0.5)
SCALE2 = SCALE * 1.4426950408889634
NT = (((1,), (1,)), ((), ()))
NN = (((1,), (0,)), ((), ()))


def mm(a, b, dims=NN):
    return lax.dot_general(a, b, dims, preferred_element_type=jnp.float32)


def attend_kernel(first, seg_ref, q_ref, k_ref, v_ref, o_ref, lse_ref, bias, total, *, bq, unroll):
    i, g = pl.program_id(0), pl.program_id(1)
    length = k_ref.shape[0]
    start = first[i]
    lane = lax.div(lax.broadcasted_iota(jnp.int32, (1, LANES), 1), HEAD_DIM)
    lane_head = lax.broadcasted_iota(jnp.int32, (1, 128), 1)

    def span(width):
        begin = pl.multiple_of(start * GRAIN, GRAIN)

        @pl.when(g == 0)
        def _():
            seg_q = jnp.transpose(jnp.broadcast_to(seg_ref[0:1, pl.ds(pl.multiple_of(i * bq, bq), bq)], (128, bq)))[:, 0:1]
            place_q = i * bq + lax.broadcasted_iota(jnp.int32, (bq, width), 0)
            place_k = begin + lax.broadcasted_iota(jnp.int32, (bq, width), 1)
            allowed = (place_k <= place_q) & (seg_q == seg_ref[0:1, pl.ds(begin, width)])
            bias[:, :width] = jnp.where(allowed, 0.0, masked_score)

        total[...] = jnp.zeros_like(total)

        def head(h, logs):
            query = jnp.where(lane == h, q_ref[...], jnp.zeros((), jnp.bfloat16))
            s = mm(query, k_ref[pl.ds(begin, width), :], NT) * SCALE2 + bias[:, :width]
            top = jnp.max(s, axis=-1, keepdims=True)
            e = jnp.exp2(s - top)
            row = jnp.sum(e, axis=-1, keepdims=True)
            out = mm(e.astype(jnp.bfloat16), v_ref[pl.ds(begin, width), :])
            total[...] = jnp.where(lane == h, out * (1.0 / row), total[...])
            place = jnp.where(h < GROUP // 2, h, h + GROUP // 2)
            return jnp.where(lane_head == place, top + jnp.log2(row), logs)

        logs = lax.fori_loop(0, GROUP, head, jnp.zeros((bq, 128), jnp.float32), unroll=unroll)
        o_ref[...] = total[...].astype(o_ref.dtype)
        lse_ref[...] = jnp.transpose(logs)[:2 * GROUP]

    blocks = (i + 1) * (bq // GRAIN) - start
    for count in range(bq // GRAIN, length // GRAIN + 1):
        pl.when(blocks == count)(functools.partial(span, count * GRAIN))


def attend(first, seg, proj, bq=256, unroll=8):
    length, width = proj.shape
    groups = width // 3 // LANES
    grid_spec = pltpu.PrefetchScalarGridSpec(
        num_scalar_prefetch=1,
        grid=(length // bq, groups),
        in_specs=[
            pl.BlockSpec((1, length), lambda i, g, *_: (0, 0)),
            pl.BlockSpec((bq, LANES), lambda i, g, *_: (i, g)),
            pl.BlockSpec((length, LANES), lambda i, g, *_: (0, groups + g)),
            pl.BlockSpec((length, LANES), lambda i, g, *_: (0, 2 * groups + g)),
        ],
        out_specs=[
            pl.BlockSpec((bq, LANES), lambda i, g, *_: (i, g)),
            pl.BlockSpec((2 * GROUP, bq), lambda i, g, *_: (g, i)),
        ],
        scratch_shapes=[pltpu.VMEM((bq, length), jnp.float32), pltpu.VMEM((bq, LANES), jnp.float32)],
    )
    return pl.pallas_call(
        functools.partial(attend_kernel, bq=bq, unroll=unroll),
        grid_spec=grid_spec,
        out_shape=[
            jax.ShapeDtypeStruct((length, width // 3), jnp.bfloat16),
            jax.ShapeDtypeStruct((groups * 2 * GROUP, length), jnp.float32),
        ],
        compiler_params=pltpu.CompilerParams(vmem_limit_bytes=48 << 20),
        cost_estimate=pl.CostEstimate(flops=28 << 30, bytes_accessed=8 << 20, transcendentals=24 * length * length),
        name="attend",
    )(first, seg, proj, proj, proj)


def attend_back_kernel(last, place, seg_ref, q_ref, k_ref, v_ref, up_ref, o_ref, lse_ref, low_t_ref, *refs, bk):
    *riders, gq_ref, gk_ref, gv_ref, keep_ref, send_ref, bias, inner, key_t, value_t, q_t, up_t, gq_t, gk, gv, grad = refs
    g, j = pl.program_id(0), pl.program_id(1)
    length, lanes = q_ref.shape
    heads = lanes // HEAD_DIM
    lane = lax.div(lax.broadcasted_iota(jnp.int32, (1, lanes), 1), HEAD_DIM)

    @pl.when(j == 0)
    def _():
        gq_t[...] = jnp.zeros_like(gq_t)
        q_t[...] = jnp.transpose(q_ref[...])
        up_t[...] = jnp.transpose(up_ref[...])
        product = up_t[...].astype(jnp.float32) * jnp.transpose(o_ref[...]).astype(jnp.float32)
        for h in range(heads):
            rows = slice(h * HEAD_DIM, (h + 1) * HEAD_DIM)
            inner[h:h + 1, :] = jnp.sum(product[rows], axis=0, keepdims=True)

    key_t[...] = jnp.transpose(k_ref[...])
    value_t[...] = jnp.transpose(v_ref[...])

    def span(width):
        begin = pl.multiple_of(j * bk, bk)
        here = pl.ds(begin, width)

        @pl.when(g == 0)
        def _():
            seg_k = jnp.transpose(jnp.broadcast_to(seg_ref[0:1, pl.ds(begin, bk)], (128, bk)))[:, 0:1]
            place_k = lax.broadcasted_iota(jnp.int32, (bk, width), 0)
            place_q = lax.broadcasted_iota(jnp.int32, (bk, width), 1)
            allowed = (place_k <= place_q) & (seg_k == seg_ref[0:1, here])
            bias[j, :, :width] = jnp.where(allowed, 0.0, masked_score)

        for h in range(heads):
            rows = slice(h * HEAD_DIM, (h + 1) * HEAD_DIM)
            key, value = jnp.transpose(key_t[rows, :]), jnp.transpose(value_t[rows, :])
            s = mm(key, q_t[rows, here]) * SCALE2 + (bias[j, :, :width] - lse_ref[h:h + 1, here])
            p = jnp.exp2(s)
            dp = mm(value, up_t[rows, here])
            ds = (p * (dp - inner[h:h + 1, here])).astype(jnp.bfloat16)
            grad_v = mm(p.astype(jnp.bfloat16), up_ref[here, :])
            grad_k = mm(ds, q_ref[here, :])
            gv[...] = jnp.where(lane == h, grad_v, gv[...]) if h else grad_v
            gk[...] = jnp.where(lane == h, grad_k, gk[...]) if h else grad_k
            gq_t[rows, here] += mm(key_t[rows, :], ds)

    blocks = last[j] - j * (bk // GRAIN)
    for count in range(bk // GRAIN, length // GRAIN + 1):
        pl.when(blocks == count)(functools.partial(span, count * GRAIN))

    here = pl.ds(pl.multiple_of(j * bk, bk), bk)
    gk_ref[here, :] = (gk[...] * SCALE).astype(gk_ref.dtype)
    gv_ref[here, :] = gv[...].astype(gv_ref.dtype)

    @pl.when(j == pl.num_programs(1) - 1)
    def _():
        gq_ref[...] = jnp.transpose((gq_t[...] * SCALE).astype(gq_ref.dtype))
        joined = jnp.concatenate([gq_ref[...], gk_ref[...], gv_ref[...]], axis=1)
        grad[...] = mm(low_t_ref[...], joined)
        cut(place, grad, keep_ref, send_ref, g)

    if riders:
        @pl.when((g == 0) & (j == 0))
        def _():
            extra = riders[0].shape[0]
            for rider, target in zip(riders, (keep_ref, send_ref)):
                target[-extra:] = rider[...]


def attend_back(begin, count, last, place, seg, proj, up, o, lse, low_t, shards, riders=(), bk=256):
    length, width = proj.shape
    groups = width // 3 // SMALL
    half = width // 6
    group = lambda g: g + begin
    whole = lambda offset: pl.BlockSpec((length, SMALL), lambda g, j, *_: (0, offset + group(g)))
    block = lambda offset: pl.BlockSpec((bk, SMALL), lambda g, j, *_: (j, offset + group(g)))
    fixed = lambda *shape: pl.BlockSpec(shape, lambda g, j, *_: (0, 0), pipeline_mode=pl.Buffered(1))
    out = pl.BlockSpec((length, SMALL), lambda g, j, *_: (0, g))
    rows = 2 * half // shards
    piece = (half, PART) if rows % 8 else (shards // 2, rows, PART)
    lead = count + (riders[0].shape[0] if riders else 0)
    all_of = lambda *size: pl.BlockSpec(size, lambda g, j, *_: (0,) * len(size), pipeline_mode=pl.Buffered(1))
    split = all_of(lead, *piece)
    grid_spec = pltpu.PrefetchScalarGridSpec(
        num_scalar_prefetch=2,
        grid=(count, length // bk),
        in_specs=[
            fixed(1, length),
            whole(0),
            block(groups),
            block(2 * groups),
            whole(0),
            whole(0),
            pl.BlockSpec((8, length), lambda g, j, *_: (group(g), 0)),
            fixed(2 * half, length),
            *[all_of(*rider.shape) for rider in riders],
        ],
        out_specs=[out, out, out, split, split],
        scratch_shapes=[
            pltpu.VMEM((length // bk, bk, length), jnp.float32),
            pltpu.VMEM((8, length), jnp.float32),
            pltpu.VMEM((SMALL, bk), jnp.bfloat16),
            pltpu.VMEM((SMALL, bk), jnp.bfloat16),
            pltpu.VMEM((SMALL, length), jnp.bfloat16),
            pltpu.VMEM((SMALL, length), jnp.bfloat16),
            pltpu.VMEM((SMALL, length), jnp.float32),
            pltpu.VMEM((bk, SMALL), jnp.float32),
            pltpu.VMEM((bk, SMALL), jnp.float32),
            pltpu.VMEM((2 * half, PART), jnp.float32),
        ],
    )
    heads = jax.ShapeDtypeStruct((length, count * SMALL), jnp.bfloat16)
    parts = jax.ShapeDtypeStruct((lead, *piece), jnp.bfloat16)
    return pl.pallas_call(
        functools.partial(attend_back_kernel, bk=bk),
        grid_spec=grid_spec,
        out_shape=[heads, heads, heads, parts, parts],
        compiler_params=pltpu.CompilerParams(vmem_limit_bytes=60 << 20),
        cost_estimate=pl.CostEstimate(flops=(count * 10) << 30, bytes_accessed=8 << 20, transcendentals=count * 4 * length * length),
        name="attend_back",
    )(last, place, seg, proj, proj, proj, up, o, lse, low_t, *riders)


def bounds(seg, bq, bk):
    row = seg[0]
    first = jnp.sum(row[None, :] < row[::bq][:, None], axis=1) // GRAIN
    last = (jnp.sum(row[None, :] <= row[bk - 1::bk][:, None], axis=1) + GRAIN - 1) // GRAIN
    return first.astype(jnp.int32), last.astype(jnp.int32)


def gelu_pair(u):
    c = 0.7978845608028654
    square = u * u
    t = jnp.tanh(u * (c + (c * 0.044715) * square))
    half = 0.5 * t + 0.5
    slope = half + (0.5 * u) * (1.0 - t * t) * (c + (3 * c * 0.044715) * square)
    return u * half, slope


def row_stats(values):
    mean = jnp.mean(values, axis=-1, keepdims=True)
    centred = values - mean
    return mean, lax.rsqrt(jnp.mean(centred * centred, axis=-1, keepdims=True) + epsilon)


def norm_back(values, gain, upstream):
    mean, rate = row_stats(values)
    unit = (values - mean) * rate
    inner = upstream * gain
    level = jnp.mean(inner, axis=-1, keepdims=True)
    along = jnp.mean(inner * unit, axis=-1, keepdims=True)
    return rate * (inner - level - unit * along)


def shard_at(place, core_rel, q_rel):
    core, q = place[0] ^ core_rel, place[1] ^ q_rel
    return ((q >> 1) * 2 + core) * 2 + (q & 1)


def cut(place, grad, keep, send, first):
    half = grad.shape[0] // 2
    for at in range(grad.shape[1] // PART):
        columns = slice(at * PART, (at + 1) * PART)
        if len(keep.shape) == 3:
            keep[first + at] = grad[:half, columns].astype(keep.dtype)
            send[first + at] = grad[half:, columns].astype(send.dtype)
        else:
            chips, rows = keep.shape[1:3]
            for rel, target in enumerate((keep, send)):
                for q in range(chips):
                    source = pl.ds(pl.multiple_of(shard_at(place, rel, q) * rows, 8), rows)
                    target[first + at, q] = grad[source, columns].astype(target.dtype)


def before_kernel(place, x_ref, gain_ref, w_ref, *refs, shards, block):
    proj_ref, low_t_ref, low = refs[-3:]
    length, width = x_ref.shape

    @pl.when(pl.program_id(0) == 0)
    def _():
        for at in range(0, length, block):
            at = slice(at, at + block)
            values = x_ref[at, :].astype(jnp.float32)
            mean, rate = row_stats(values)
            normed = ((values - mean) * rate * gain_ref[...]).astype(jnp.bfloat16)
            low[at, :] = normed
            low_t_ref[:, at] = jnp.transpose(normed)

    proj_ref[...] = mm(low[...], w_ref[...]).astype(jnp.bfloat16)


def before(place, x, gain, w, shards, so_far=(), chunk=768, block=256):
    length, width = x.shape
    columns = w.shape[1]
    whole = lambda *shape: pl.BlockSpec(shape, lambda c, *_: (0, 0), pipeline_mode=pl.Buffered(1))
    grid_spec = pltpu.PrefetchScalarGridSpec(
        num_scalar_prefetch=1,
        grid=(columns // chunk,),
        in_specs=[whole(length, width), whole(1, width), pl.BlockSpec((width, chunk), lambda c, *_: (0, c))]
        + [pl.BlockSpec(memory_space=pl.ANY)] * len(so_far),
        out_specs=[
            pl.BlockSpec((length, chunk), lambda c, place: (place[2], c)),
            pl.BlockSpec((width, length), lambda c, place: (0, place[2])),
        ],
        scratch_shapes=[pltpu.VMEM((length, width), jnp.bfloat16)],
    )
    return pl.pallas_call(
        functools.partial(before_kernel, shards=shards, block=block),
        grid_spec=grid_spec,
        out_shape=[
            jax.ShapeDtypeStruct((2 * length, columns), jnp.bfloat16),
            jax.ShapeDtypeStruct((width, 2 * length), jnp.bfloat16),
        ],
        input_output_aliases={4 + at: at for at in range(len(so_far))},
        compiler_params=pltpu.CompilerParams(vmem_limit_bytes=60 << 20),
        cost_estimate=pl.CostEstimate(flops=2 * length * width * columns, bytes_accessed=12 << 20, transcendentals=length),
        name="before",
    )(place, x, gain, w, *so_far)


def middle_kernel(place, x_kept, x_other, o_ref, gy_kept, gy_other, w_out_ref, gain_ref, w_up_ref, w_down_ref,
                  out_kept, out_other, gx_ref, go_ref, keep_up, send_up, keep_down, send_down, keep_out, send_out,
                  gy, x1, low, low_t, total, back, whole, part, *, shards, block):
    c = pl.program_id(0)
    length, width = o_ref.shape
    chunk = w_down_ref.shape[0]
    pieces = [slice(at, at + block) for at in range(0, length, block)]
    rows = width // shards
    half, window = width // 2, length // 2
    kept = pl.ds(pl.multiple_of(place[2] * window, window), window)
    other = pl.ds(pl.multiple_of((1 - place[2]) * window, window), window)

    @pl.when(c == 0)
    def _():
        gy[kept, :] = gy_kept[...]
        gy[other, :] = gy_other[...]
        x1[kept, :] = x_kept[...].astype(jnp.float32)
        x1[other, :] = x_other[...].astype(jnp.float32)
        for at in pieces:
            values = x1[at, :] + mm(o_ref[at, :], w_out_ref[...])
            x1[at, :] = values
            mean, rate = row_stats(values)
            normed = ((values - mean) * rate * gain_ref[...]).astype(jnp.bfloat16)
            low[at, :] = normed
            low_t[:, at] = jnp.transpose(normed)
            total[at, :] = values
            back[at, :] = jnp.zeros_like(values)

    lifted, slopes = [], []
    for at in pieces:
        a, slope = gelu_pair(mm(low[at, :], w_up_ref[...]))
        a = a.astype(jnp.bfloat16)
        gu = (mm(gy[at, :], w_down_ref[...], NT) * slope).astype(jnp.bfloat16)
        total[at, :] += mm(a, w_down_ref[...])
        back[at, :] += mm(gu, w_up_ref[...], NT)
        lifted.append(jnp.transpose(a))
        slopes.append(gu)
    whole[...] = mm(low_t[...], jnp.concatenate(slopes, axis=0))
    cut(place, whole, keep_up, send_up, 0)
    grad_down = mm(jnp.concatenate(lifted, axis=1), gy[...])
    if rows % 8:
        for at in range(width // PART):
            for target, begin in ((keep_down, 0), (send_down, chunk // 2)):
                piece = grad_down[begin:begin + chunk // 2, at * PART:(at + 1) * PART]
                target[at] = piece.astype(jnp.bfloat16)
    else:
        part[...] = grad_down
        for rel, target in enumerate((keep_down, send_down)):
            for q_rel in range(4):
                q = (place[1] ^ q_rel) & 3
                source = (((q >> 1) * 2 + (place[0] ^ rel)) * 2 + (q & 1)) * 4 * rows
                for sub in range(4):
                    source_rows = pl.ds(pl.multiple_of(source + sub * rows, 8), rows)
                    for at in range(width // PART):
                        piece = part[source_rows, at * PART:(at + 1) * PART]
                        target[4 * at + sub, q_rel] = piece.astype(jnp.bfloat16)

    @pl.when(c == pl.num_programs(0) - 1)
    def _():
        branch = []
        out_kept[...] = total[kept, :].astype(jnp.bfloat16)
        out_other[...] = total[other, :].astype(jnp.bfloat16)
        for at in pieces:
            grad = gy[at, :].astype(jnp.float32) + norm_back(x1[at, :], gain_ref[...], back[at, :])
            grad = grad.astype(jnp.bfloat16)
            gx_ref[at, :] = grad
            branch.append(grad)
            go_ref[at, :] = mm(grad, w_out_ref[...], NT).astype(jnp.bfloat16)
            low_t[:, at] = jnp.transpose(o_ref[at, :])
        whole[...] = mm(low_t[...], jnp.concatenate(branch, axis=0))
        cut(place, whole, keep_out, send_out, 0)


def middle(place, x, o, gy, w_out, gain, w_up, w_down, shards, block=512):
    length, width = o.shape
    lift = w_up.shape[1]
    steps = 4
    chunk = lift // steps
    half, window = width // 2, length // 2
    at = (lambda c, place: c) if (width // shards) % 8 else (lambda c, place: c ^ (place[1] >> 2))
    whole = lambda *shape: pl.BlockSpec(shape, lambda c, *_: (0, 0), pipeline_mode=pl.Buffered(1))
    out = lambda *shape: pl.BlockSpec(shape, lambda c, *_: (0,) * len(shape), pipeline_mode=pl.Buffered(1))
    shape = jax.ShapeDtypeStruct
    rows = width // shards
    if rows % 8:
        up_shape, down_shape, out_shape = (lift // PART, half, PART), (width // PART, lift // 2, PART), (width // PART, half, PART)
        up = pl.BlockSpec((chunk // PART, half, PART), lambda c, place: (at(c, place), 0, 0))
        down = pl.BlockSpec((width // PART, chunk // 2, PART), lambda c, place: (0, c, 0))
    else:
        piece = (shards // 2, rows, PART)
        up_shape, down_shape, out_shape = (lift // PART, *piece), (lift // PART, *piece), (width // PART, *piece)
        up = pl.BlockSpec((chunk // PART, *piece), lambda c, place: (at(c, place), 0, 0, 0))
        down = pl.BlockSpec((lift // PART, 4, rows, PART), lambda c, place: (0, c, 0, 0))
    bf16 = jnp.bfloat16
    grid_spec = pltpu.PrefetchScalarGridSpec(
        num_scalar_prefetch=1,
        grid=(steps,),
        in_specs=[
            whole(window, width), whole(window, width), whole(length, width), whole(window, width),
            whole(window, width), whole(width, width), whole(1, width),
            pl.BlockSpec((width, chunk), lambda c, place: (0, at(c, place))),
            pl.BlockSpec((chunk, width), lambda c, place: (at(c, place), 0)),
        ],
        out_specs=[
            out(window, width), out(window, width), out(length, width), out(length, width), up, up, down, down,
            out(*out_shape), out(*out_shape),
        ],
        scratch_shapes=[
            pltpu.VMEM((length, width), bf16),
            pltpu.VMEM((length, width), jnp.float32),
            pltpu.VMEM((length, width), bf16),
            pltpu.VMEM((width, length), bf16),
            pltpu.VMEM((length, width), jnp.float32),
            pltpu.VMEM((length, width), jnp.float32),
            pltpu.VMEM((width, width), jnp.float32),
            pltpu.VMEM((chunk, width), jnp.float32),
        ],
    )
    return pl.pallas_call(
        functools.partial(middle_kernel, shards=shards, block=block),
        grid_spec=grid_spec,
        out_shape=[
            shape((window, width), bf16), shape((window, width), bf16),
            shape((length, width), bf16), shape((length, width), bf16),
            *[shape(size, bf16) for size in (up_shape, up_shape, down_shape, down_shape, out_shape, out_shape)],
        ],
        compiler_params=pltpu.CompilerParams(vmem_limit_bytes=60 << 20),
        cost_estimate=pl.CostEstimate(flops=12 * length * width * lift, bytes_accessed=40 << 20, transcendentals=length * lift),
        name="middle",
    )(place, *x, o, *gy, w_out, gain, w_up, w_down)


def after_kernel(place, x_ref, gain_ref, gx_ref, w_ref, *refs):
    out_ref = refs[-1]
    grads = jnp.concatenate([ref[...] for third in range(3) for ref in refs[third:-1:3]], axis=1)
    back = mm(grads, w_ref[...], NT)
    values = x_ref[...].astype(jnp.float32)
    out_ref[...] = (gx_ref[...].astype(jnp.float32) + norm_back(values, gain_ref[...], back)).astype(out_ref.dtype)


def after(place, x, gain, gx, w, pieces, block=256):
    length, width = x.shape
    steps = length // block
    rows = lambda columns: pl.BlockSpec((block, columns), lambda i, place: (place[2] * steps + i, 0))
    own = pl.BlockSpec((block, width), lambda i, place: (i, 0))
    whole = lambda *shape: pl.BlockSpec(shape, lambda i, place: (0, 0), pipeline_mode=pl.Buffered(1))
    grid_spec = pltpu.PrefetchScalarGridSpec(
        num_scalar_prefetch=1,
        grid=(steps,),
        in_specs=[own, whole(1, width), rows(width), whole(width, w.shape[1])] + [rows(piece.shape[1]) for piece in pieces],
        out_specs=own,
    )
    return pl.pallas_call(
        after_kernel,
        grid_spec=grid_spec,
        out_shape=jax.ShapeDtypeStruct((length, width), jnp.bfloat16),
        compiler_params=pltpu.CompilerParams(vmem_limit_bytes=60 << 20),
        cost_estimate=pl.CostEstimate(flops=6 * length * width * width, bytes_accessed=16 << 20, transcendentals=length),
        name="after",
    )(place, x, gain, gx, w, *pieces)


def swapped(block):
    return lax.ppermute(block, "seq", [(0, 1), (1, 0)])


def split_window(block):
    place = lax.axis_index("seq")
    take = lambda at: lax.dynamic_index_in_dim(block, at, 0, keepdims=False)
    return take(place), take(1 - place)


def joined(kept, other):
    place = lax.axis_index("seq")
    return jnp.where(place == 0, jnp.stack([kept, other]), jnp.stack([other, kept]))


def crossed(block, bits):
    step = sum(1 if bit == 0 else 2 if bit == -1 else 2 << bit for bit in bits)
    count = 2 * lax.axis_size("dp")
    return lax.ppermute(block, ("dp", "seq"), [(i, i ^ step) for i in range(count)])


def masks_of(bits):
    return [tuple(bit for e, bit in enumerate(bits) if number >> e & 1) for number in range(1, 1 << len(bits))]


def combine_kernel(*refs, work, steps):
    for lead, cut_up, targets in work:
        def one(index, carry):
            for target, offset, count, sources in targets:
                for at, terms in enumerate(sources):
                    total = None
                    for ref, begin, per, place in terms:
                        where = (index, *place) if per is None else (begin + index * per + place,)
                        value = refs[ref][where].astype(jnp.float32)
                        total = value if total is None else total + value
                    refs[target][offset + index * count + at] = total.astype(refs[target].dtype)
            return carry

        count = lead // steps if cut_up else lead

        def all_of(count=count, one=one):
            if sum(len(sources) for _, _, _, sources in targets) > 32:
                lax.fori_loop(0, count, one, 0)
            else:
                for index in range(count):
                    one(index, 0)

        if cut_up:
            all_of()
        elif steps > 1:
            @pl.when(pl.program_id(0) == 0)
            def _():
                all_of()
        else:
            all_of()


class Flow:
    def __init__(self, place, keep, send, chips, plan, blocks=0):
        if keep.ndim == 3:
            index = jnp.stack([shard_at(place, rel, q) for rel in range(2) for q in range(chips)])
            lead, half, columns = keep.shape
            both = jnp.stack([array.reshape(lead, max(blocks, 1), -1, columns) for array in (keep, send)], axis=2)
            parts = max(blocks, 1)
            both = both.reshape(lead, 2 * chips, parts, -1, columns)[:, index].transpose(0, 2, 1, 3, 4)
            both = both.reshape(lead * parts, 2 * chips, -1, columns)
            keep, send = both[:, :chips], both[:, chips:]
        self.lead, _, self.rows, self.columns = keep.shape
        self.left = list(reversed(range(chips.bit_length() - 1)))
        self.plan = list(plan)
        self.terms = [(keep.reshape(-1, self.rows, self.columns), list(self.left), None)]
        self.first = send.reshape(-1, self.rows, self.columns)


class Operands:
    def __init__(self):
        self.arrays, self.specs, self.seen = [], [], {}

    def add(self, array, spec):
        self.arrays.append(array)
        self.specs.append(spec)
        return len(self.arrays) - 1

    def finder(self, flow, term, fixed, cut_up):
        array, bits, offset = term
        if offset is not None:
            if id(array) not in self.seen:
                self.seen[id(array)] = self.add(array, pl.BlockSpec(array.shape, lambda i: (0, 0, 0), pipeline_mode=pl.Buffered(1)))
            ref, per = self.seen[id(array)], 1 << len(bits)
            return lambda value: (ref, offset, per, sum(value[bit] << (len(bits) - 1 - at) for at, bit in enumerate(bits)))
        view = array.reshape(flow.lead, *(2,) * len(bits), flow.rows, flow.columns)
        block = (flow.lead // cut_up if cut_up else flow.lead, *[1 if bit in fixed else 2 for bit in bits], flow.rows, flow.columns)
        index = tuple(fixed.get(bit, 0) for bit in bits)
        mode = {} if cut_up else dict(pipeline_mode=pl.Buffered(1))
        ref = self.add(view, pl.BlockSpec(block, lambda i: (i if cut_up else 0, *index, 0, 0), **mode))
        return lambda value: (ref, 0, None, tuple(0 if bit in fixed else value[bit] for bit in bits))


def combine(flows, steps):
    operands, plans, sizes = Operands(), [], {}
    for flow in flows:
        bits = flow.plan.pop(0)
        rest = [bit for bit in flow.left if bit not in bits]
        cut_up = steps if steps > 1 and flow.lead % steps == 0 else 0
        gone = {bit: 0 for bit in range(64) if bit not in flow.left}
        fixed = {**gone, bits[0]: 1} if len(bits) == 1 else gone
        finders = [operands.finder(flow, term, fixed, cut_up) for term in flow.terms]
        plans.append((flow, bits, rest, cut_up, gone, finders))
        for mask in masks_of(bits):
            size = flow.lead << len(rest)
            key = mask if steps == 1 else (mask, id(flow))
            sizes.setdefault(key, []).append((flow, size, cut_up and size // cut_up, mask))
    outputs, out_specs = [], []
    for members in sizes.values():
        shape = (sum(size for _, size, _, _ in members), members[0][0].rows, members[0][0].columns)
        outputs.append(jax.ShapeDtypeStruct(shape, jnp.bfloat16))
        cut = members[0][2]
        out_specs.append(
            pl.BlockSpec((cut, *shape[1:]), lambda i: (i, 0, 0)) if cut
            else pl.BlockSpec(shape, lambda i: (0, 0, 0), pipeline_mode=pl.Buffered(1))
        )
    work = []
    for flow, bits, rest, cut_up, gone, finders in plans:
        targets = []
        for number, members in enumerate(sizes.values()):
            offset = 0
            for member, size, _, mask in members:
                if member is flow:
                    sources = []
                    for at in range(1 << len(rest)):
                        value = {bit: (at >> (len(rest) - 1 - e)) & 1 for e, bit in enumerate(rest)}
                        value.update(gone)
                        value.update({bit: int(bit in mask) for bit in bits})
                        sources.append([find(value) for find in finders])
                    targets.append((len(operands.arrays) + number, offset, 1 << len(rest), sources))
                offset += size
        work.append((flow.lead, cut_up, targets))
        flow.left = rest
    results = pl.pallas_call(
        functools.partial(combine_kernel, work=work, steps=steps),
        grid=(steps,),
        in_specs=operands.specs,
        out_specs=out_specs,
        out_shape=outputs,
        compiler_params=pltpu.CompilerParams(vmem_limit_bytes=60 << 20),
        cost_estimate=pl.CostEstimate(flops=1 << 20, bytes_accessed=8 << 20, transcendentals=0),
        name="combine",
    )(*operands.arrays)
    return [
        (members[0][3], array, [(flow, size) for flow, size, _, _ in members])
        for members, array in zip(sizes.values(), results)
    ]


def leave(flows, value=None, steps=1):
    flows = [flow for flow in flows if flow.plan]
    starting = [flow for flow in flows if flow.plan[0] == (-1,)]
    waiting = [flow for flow in flows if flow.plan[0] == ()]
    going = [flow for flow in flows if flow not in starting and flow not in waiting]
    for flow in starting + waiting:
        flow.plan.pop(0)
    sent = combine(going, steps) if going else []
    sent += [((-1,), flow.first, [(flow, flow.first.shape[0])]) for flow in starting]
    value, arrays = lax.optimization_barrier((value, [array for _, array, _ in sent]))
    return value, [(crossed(array, mask), members) for array, (mask, _, members) in zip(arrays, sent)]


def arrive(transfers, value=None):
    moved, value = lax.optimization_barrier(([array for array, _ in transfers], value))
    for array, (_, members) in zip(moved, transfers):
        at = 0
        for flow, size in members:
            flow.terms.append((array, list(flow.left), at if len(members) > 1 else None))
            at += size
    return value


def finish_kernel(*refs, work, gains, count):
    inputs, outputs = refs[:count], refs[count:]
    for terms, targets in work:
        for lead, (target, row, column, width, parts) in enumerate(targets):
            total = None
            for ref, begin, per, place in terms:
                where = (lead, *place) if per is None else (begin + lead * per + place,)
                value = inputs[ref][where].astype(jnp.float32)
                total = value if total is None else total + value
            for part in range(parts):
                piece = slice(part * width, (part + 1) * width)
                begin = column + part * (outputs[target].shape[1] // parts if parts > 1 else 0)
                outputs[target][row:row + total.shape[0], begin:begin + width] = total[:, piece]
    for source, weight, gain, target in gains:
        product = inputs[weight][...] * outputs[source][...]
        sums = lax.dot_general(jnp.ones((8, product.shape[1]), jnp.float32), product, NT,
                               precision=lax.Precision.HIGHEST, preferred_element_type=jnp.float32)
        outputs[target][...] = sums[:1] / inputs[gain][...]


def finish(plans, sizes, gained):
    operands, work, gains = Operands(), [], []
    gone = {bit: 0 for bit in range(64)}
    for flow, targets in plans:
        finders = [operands.finder(flow, term, gone, False) for term in flow.terms]
        work.append(([find(gone) for find in finders], targets))
    sizes = list(sizes)
    for source, *arrays in gained:
        at = [operands.add(array, pl.BlockSpec(array.shape, lambda i: (0, 0), pipeline_mode=pl.Buffered(1))) for array in arrays]
        gains.append((source, *at, len(sizes)))
        sizes.append((1, sizes[source][0]))
    return pl.pallas_call(
        functools.partial(finish_kernel, work=work, gains=gains, count=len(operands.arrays)),
        grid=(1,),
        in_specs=operands.specs,
        out_specs=[pl.BlockSpec(size, lambda i: (0, 0), pipeline_mode=pl.Buffered(1)) for size in sizes],
        out_shape=[jax.ShapeDtypeStruct(size, jnp.float32) for size in sizes],
        compiler_params=pltpu.CompilerParams(vmem_limit_bytes=60 << 20),
        cost_estimate=pl.CostEstimate(flops=1 << 20, bytes_accessed=4 << 20, transcendentals=0),
        name="finish",
    )(*operands.arrays)


def body(tokens, segments, cotangent, gain_attn, w_qkv, w_out, gain_ffn, w_up, w_down):
    chips = lax.axis_size("dp")
    shards = 2 * chips
    dp, seq = lax.axis_index("dp"), lax.axis_index("seq")
    here = jnp.stack([dp & 1, (dp >> 1) * 2 + seq, seq]).astype(jnp.int32)
    there = jnp.stack([dp & 1, (dp >> 1) * 2 + seq, 1 - seq]).astype(jnp.int32)
    far = tuple(range(2, chips.bit_length() - 1))
    rest = [far[at:at + 2] for at in range(2, len(far), 2)]

    x_kept, x_sent = split_window(tokens)
    segments, cotangent, x_sent = lax.optimization_barrier((segments, cotangent, x_sent))
    seg_kept, seg_sent = split_window(segments)
    gy_kept, gy_sent = split_window(cotangent)
    x_other, seg_other, gy_other = swapped(x_sent), swapped(seg_sent), swapped(gy_sent)
    seg = jnp.where(seq == 0, jnp.concatenate([seg_kept, seg_other]), jnp.concatenate([seg_other, seg_kept]))[None]
    first, last = bounds(seg, 256, 256)
    gain_one, gain_two = gain_attn[None], gain_ffn[None]
    begin = shard_at(here, 0, 0) * (w_out.shape[0] // shards)
    shard_of = lambda array: lax.dynamic_slice_in_dim(array, begin, w_out.shape[0] // shards, 0).astype(jnp.float32)
    weights = [shard_of(w_qkv), shard_of(gain_attn)[None], shard_of(w_up), shard_of(gain_ffn)[None]]
    x_other, weights = lax.optimization_barrier((x_other, weights))
    early = before(here, x_kept, gain_one, w_qkv, shards)
    proj, low_t = before(there, x_other, gain_one, w_qkv, shards, early)
    mixture, lse = attend(first, seg, proj)
    out_kept, out_sent, gx, go, keep_up, send_up, keep_down, send_down, keep_out, send_out = middle(
        here, (x_kept, x_other), mixture, (gy_kept, gy_other), w_out, gain_two, w_up, w_down, shards
    )

    core, near = (-1,), [(bit,) for bit in far]
    up = Flow(here, keep_up, send_up, chips, [core, (1,), (0,), *near])
    down = Flow(here, keep_down, send_down, chips, [core, *near[:1], (1,), *near[1:2], (), (0,), *near[2:]], 4)
    heads = []

    def heads_back(begin, count, plan, riders=()):
        *grads, keep, send = attend_back(begin, count, last, here, seg, proj, go, mixture, lse, low_t, shards, riders)
        heads.append(grads)
        return Flow(here, keep, send, chips, [core, *plan])

    (go, out_sent), moving = leave([up, down], (go, out_sent))
    out_other = swapped(out_sent)
    one = heads_back(0, 2, [*near[:1], (0,), (1,), *near[1:]], (keep_out, send_out))
    out_other = arrive(moving, out_other)
    (go, out_other), moving = leave([up, down, one], (go, out_other), 2)
    two = heads_back(2, 3, [(1,), *near[:1], (0, *far[1:2]), *rest])
    arrive(moving)
    go, moving = leave([up, down, one, two], go, 2)
    three = heads_back(5, 1, [(1, *far[:1]), (0, *far[1:2]), *rest])
    arrive(moving)
    flows = [up, down, one, two, three]
    gx, moving = leave(flows, gx)
    pieces = [piece for grads in heads for piece in grads]
    other_rows = after(there, x_other, gain_one, gx, w_qkv, pieces)
    other_rows = arrive(moving, other_rows)
    rows_back = swapped(other_rows)
    gx, moving = leave(flows, gx)
    kept_rows = after(here, x_kept, gain_one, gx, w_qkv, pieces)
    kept_rows = arrive(moving, kept_rows)
    rows, width = up.rows, w_out.shape[1]
    w_qkv_rows, gain_one_rows, w_up_rows, gain_two_rows = weights

    def finish_up(w_rows):
        whole = [(0, 0, lead * PART, PART, 1) for lead in range(up.lead)]
        return finish([(up, whole)], [(rows, up.lead * PART)], [(0, w_rows, gain_two_rows)])

    soon = not up.plan
    (kept_rows, out_other, w_up_rows), moving = leave(flows, (kept_rows, out_other, w_up_rows))
    up_grads = finish_up(w_up_rows) if soon else None
    grad_tokens, outputs = joined(kept_rows, rows_back), joined(out_kept, out_other)
    while True:
        up_grads, grad_tokens, outputs = arrive(moving, (up_grads, grad_tokens, outputs))
        if not any(flow.plan for flow in flows):
            break
        _, moving = leave(flows)
    grad_up, grad_gain_ffn = up_grads or finish_up(w_up_rows)
    out_lead, group = width // PART, iter(range(64))
    of_group = lambda flow, extra=0: [(0, 0, next(group) * SMALL, SMALL, 3) for _ in range(flow.lead - extra)]
    grad_qkv, grad_out, grad_down, grad_gain_attn = finish([
        (one, of_group(one, out_lead) + [(1, 0, lead * PART, PART, 1) for lead in range(out_lead)]),
        (two, of_group(two)),
        (three, of_group(three)),
        (down, [(2, (lead % 4) * rows, (lead // 4) * PART, PART, 1) for lead in range(down.lead)]),
    ], [(rows, 3 * width), (rows, width), (4 * rows, width)], [(0, w_qkv_rows, gain_one_rows)])
    return (
        outputs,
        grad_tokens,
        grad_qkv,
        grad_out,
        grad_up,
        grad_down,
        grad_gain_attn[0],
        grad_gain_ffn[0],
    )


def solution(mesh):
    placed = (
        P("dp", "seq", None),
        P("dp", "seq"),
        P("dp", "seq", None),
        P(),
        P(),
        P(),
        P(),
        P(),
        P(),
    )
    return jax.shard_map(
        body,
        mesh=mesh,
        in_specs=placed,
        out_specs=(
            P("dp", "seq", None),
            P("dp", "seq", None),
            P(("dp", "seq"), None),
            P(("dp", "seq"), None),
            P(("dp", "seq"), None),
            P(("dp", "seq"), None),
            P(("dp", "seq")),
            P(("dp", "seq")),
        ),
        check_vma=False,
    )
```

```python
import functools

import jax
import jax.numpy as jnp
from jax import lax
from jax.experimental import pallas as pl
from jax.experimental.pallas import tpu as pltpu
from jax.sharding import PartitionSpec as P

HEAD_DIM = 32
GROUP = 8
LANES = GROUP * HEAD_DIM
SMALL = 128
PART = 3 * SMALL
GRAIN = 128
masked_score = -1e30
epsilon = 1e-05
SCALE = HEAD_DIM ** (-0.5)
SCALE2 = SCALE * 1.4426950408889634
NT = (((1,), (1,)), ((), ()))
NN = (((1,), (0,)), ((), ()))


def mm(a, b, dims=NN):
    return lax.dot_general(a, b, dims, preferred_element_type=jnp.float32)


def attend_kernel(first, seg_ref, q_ref, k_ref, v_ref, o_ref, lse_ref, bias, total, *, bq, unroll):
    i, g = pl.program_id(0), pl.program_id(1)
    length = k_ref.shape[0]
    start = first[i]
    lane = lax.div(lax.broadcasted_iota(jnp.int32, (1, LANES), 1), HEAD_DIM)
    lane_head = lax.broadcasted_iota(jnp.int32, (1, 128), 1)

    def span(width):
        begin = pl.multiple_of(start * GRAIN, GRAIN)

        @pl.when(g == 0)
        def _():
            seg_q = jnp.transpose(jnp.broadcast_to(seg_ref[0:1, pl.ds(pl.multiple_of(i * bq, bq), bq)], (128, bq)))[:, 0:1]
            place_q = i * bq + lax.broadcasted_iota(jnp.int32, (bq, width), 0)
            place_k = begin + lax.broadcasted_iota(jnp.int32, (bq, width), 1)
            allowed = (place_k <= place_q) & (seg_q == seg_ref[0:1, pl.ds(begin, width)])
            bias[:, :width] = jnp.where(allowed, 0.0, masked_score)

        total[...] = jnp.zeros_like(total)

        def head(h, logs):
            query = jnp.where(lane == h, q_ref[...], jnp.zeros((), jnp.bfloat16))
            s = mm(query, k_ref[pl.ds(begin, width), :], NT) * SCALE2 + bias[:, :width]
            top = jnp.max(s, axis=-1, keepdims=True)
            e = jnp.exp2(s - top)
            row = jnp.sum(e, axis=-1, keepdims=True)
            out = mm(e.astype(jnp.bfloat16), v_ref[pl.ds(begin, width), :])
            total[...] = jnp.where(lane == h, out * (1.0 / row), total[...])
            place = jnp.where(h < GROUP // 2, h, h + GROUP // 2)
            return jnp.where(lane_head == place, top + jnp.log2(row), logs)

        logs = lax.fori_loop(0, GROUP, head, jnp.zeros((bq, 128), jnp.float32), unroll=unroll)
        o_ref[...] = total[...].astype(o_ref.dtype)
        lse_ref[...] = jnp.transpose(logs)[:2 * GROUP]

    blocks = (i + 1) * (bq // GRAIN) - start
    for count in range(bq // GRAIN, length // GRAIN + 1):
        pl.when(blocks == count)(functools.partial(span, count * GRAIN))


def attend(first, seg, proj, bq=256, unroll=8):
    length, width = proj.shape
    groups = width // 3 // LANES
    grid_spec = pltpu.PrefetchScalarGridSpec(
        num_scalar_prefetch=1,
        grid=(length // bq, groups),
        in_specs=[
            pl.BlockSpec((1, length), lambda i, g, *_: (0, 0)),
            pl.BlockSpec((bq, LANES), lambda i, g, *_: (i, g)),
            pl.BlockSpec((length, LANES), lambda i, g, *_: (0, groups + g)),
            pl.BlockSpec((length, LANES), lambda i, g, *_: (0, 2 * groups + g)),
        ],
        out_specs=[
            pl.BlockSpec((bq, LANES), lambda i, g, *_: (i, g)),
            pl.BlockSpec((2 * GROUP, bq), lambda i, g, *_: (g, i)),
        ],
        scratch_shapes=[pltpu.VMEM((bq, length), jnp.float32), pltpu.VMEM((bq, LANES), jnp.float32)],
    )
    return pl.pallas_call(
        functools.partial(attend_kernel, bq=bq, unroll=unroll),
        grid_spec=grid_spec,
        out_shape=[
            jax.ShapeDtypeStruct((length, width // 3), jnp.bfloat16),
            jax.ShapeDtypeStruct((groups * 2 * GROUP, length), jnp.float32),
        ],
        compiler_params=pltpu.CompilerParams(vmem_limit_bytes=54 << 20),
        cost_estimate=pl.CostEstimate(flops=28 << 30, bytes_accessed=8 << 20, transcendentals=24 * length * length),
        name="attend",
    )(first, seg, proj, proj, proj)


def attend_back_kernel(last, place, seg_ref, q_ref, k_ref, v_ref, up_ref, o_ref, lse_ref, low_t_ref, *refs, bk):
    *riders, gq_ref, gk_ref, gv_ref, keep_ref, send_ref, bias, inner, key_t, value_t, q_t, up_t, gq_t, gk, gv, grad = refs
    g, j = pl.program_id(0), pl.program_id(1)
    length, lanes = q_ref.shape
    heads = lanes // HEAD_DIM
    lane = lax.div(lax.broadcasted_iota(jnp.int32, (1, lanes), 1), HEAD_DIM)

    @pl.when(j == 0)
    def _():
        gq_t[...] = jnp.zeros_like(gq_t)
        q_t[...] = jnp.transpose(q_ref[...])
        up_t[...] = jnp.transpose(up_ref[...])
        product = up_t[...].astype(jnp.float32) * jnp.transpose(o_ref[...]).astype(jnp.float32)
        for h in range(heads):
            rows = slice(h * HEAD_DIM, (h + 1) * HEAD_DIM)
            inner[h:h + 1, :] = jnp.sum(product[rows], axis=0, keepdims=True)

    key_t[...] = jnp.transpose(k_ref[...])
    value_t[...] = jnp.transpose(v_ref[...])

    def span(width):
        begin = pl.multiple_of(j * bk, bk)
        here = pl.ds(begin, width)

        @pl.when(g == 0)
        def _():
            seg_k = jnp.transpose(jnp.broadcast_to(seg_ref[0:1, pl.ds(begin, bk)], (128, bk)))[:, 0:1]
            place_k = lax.broadcasted_iota(jnp.int32, (bk, width), 0)
            place_q = lax.broadcasted_iota(jnp.int32, (bk, width), 1)
            allowed = (place_k <= place_q) & (seg_k == seg_ref[0:1, here])
            bias[j, :, :width] = jnp.where(allowed, 0.0, masked_score)

        for h in range(heads):
            rows = slice(h * HEAD_DIM, (h + 1) * HEAD_DIM)
            key, value = jnp.transpose(key_t[rows, :]), jnp.transpose(value_t[rows, :])
            s = mm(key, q_t[rows, here]) * SCALE2 + (bias[j, :, :width] - lse_ref[h:h + 1, here])
            p = jnp.exp2(s)
            dp = mm(value, up_t[rows, here])
            ds = (p * (dp - inner[h:h + 1, here])).astype(jnp.bfloat16)
            grad_v = mm(p.astype(jnp.bfloat16), up_ref[here, :])
            grad_k = mm(ds, q_ref[here, :])
            gv[...] = jnp.where(lane == h, grad_v, gv[...]) if h else grad_v
            gk[...] = jnp.where(lane == h, grad_k, gk[...]) if h else grad_k
            gq_t[rows, here] += mm(key_t[rows, :], ds)

    blocks = last[j] - j * (bk // GRAIN)
    for count in range(bk // GRAIN, length // GRAIN + 1):
        pl.when(blocks == count)(functools.partial(span, count * GRAIN))

    here = pl.ds(pl.multiple_of(j * bk, bk), bk)
    gk_ref[here, :] = (gk[...] * SCALE).astype(gk_ref.dtype)
    gv_ref[here, :] = gv[...].astype(gv_ref.dtype)

    @pl.when(j == pl.num_programs(1) - 1)
    def _():
        gq_ref[...] = jnp.transpose((gq_t[...] * SCALE).astype(gq_ref.dtype))
        joined = jnp.concatenate([gq_ref[...], gk_ref[...], gv_ref[...]], axis=1)
        grad[...] = mm(low_t_ref[...], joined)
        cut(place, grad, keep_ref, send_ref, g)

    if riders:
        @pl.when((g == 0) & (j == 0))
        def _():
            extra = riders[0].shape[0]
            for rider, target in zip(riders, (keep_ref, send_ref)):
                target[-extra:] = rider[...]


def attend_back(begin, count, last, place, seg, proj, up, o, lse, low_t, shards, riders=(), bk=256):
    length, width = proj.shape
    groups = width // 3 // SMALL
    half = width // 6
    group = lambda g: g + begin
    whole = lambda offset: pl.BlockSpec((length, SMALL), lambda g, j, *_: (0, offset + group(g)))
    block = lambda offset: pl.BlockSpec((bk, SMALL), lambda g, j, *_: (j, offset + group(g)))
    fixed = lambda *shape: pl.BlockSpec(shape, lambda g, j, *_: (0, 0), pipeline_mode=pl.Buffered(1))
    out = pl.BlockSpec((length, SMALL), lambda g, j, *_: (0, g))
    rows = 2 * half // shards
    piece = (half, PART) if rows % 8 else (shards // 2, rows, PART)
    lead = count + (riders[0].shape[0] if riders else 0)
    all_of = lambda *size: pl.BlockSpec(size, lambda g, j, *_: (0,) * len(size), pipeline_mode=pl.Buffered(1))
    split = all_of(lead, *piece)
    grid_spec = pltpu.PrefetchScalarGridSpec(
        num_scalar_prefetch=2,
        grid=(count, length // bk),
        in_specs=[
            fixed(1, length),
            whole(0),
            block(groups),
            block(2 * groups),
            whole(0),
            whole(0),
            pl.BlockSpec((8, length), lambda g, j, *_: (group(g), 0)),
            fixed(2 * half, length),
            *[all_of(*rider.shape) for rider in riders],
        ],
        out_specs=[out, out, out, split, split],
        scratch_shapes=[
            pltpu.VMEM((length // bk, bk, length), jnp.float32),
            pltpu.VMEM((8, length), jnp.float32),
            pltpu.VMEM((SMALL, bk), jnp.bfloat16),
            pltpu.VMEM((SMALL, bk), jnp.bfloat16),
            pltpu.VMEM((SMALL, length), jnp.bfloat16),
            pltpu.VMEM((SMALL, length), jnp.bfloat16),
            pltpu.VMEM((SMALL, length), jnp.float32),
            pltpu.VMEM((bk, SMALL), jnp.float32),
            pltpu.VMEM((bk, SMALL), jnp.float32),
            pltpu.VMEM((2 * half, PART), jnp.float32),
        ],
    )
    heads = jax.ShapeDtypeStruct((length, count * SMALL), jnp.bfloat16)
    parts = jax.ShapeDtypeStruct((lead, *piece), jnp.bfloat16)
    return pl.pallas_call(
        functools.partial(attend_back_kernel, bk=bk),
        grid_spec=grid_spec,
        out_shape=[heads, heads, heads, parts, parts],
        compiler_params=pltpu.CompilerParams(vmem_limit_bytes=60 << 20),
        cost_estimate=pl.CostEstimate(flops=(count * 10) << 30, bytes_accessed=8 << 20, transcendentals=count * 4 * length * length),
        name="attend_back",
    )(last, place, seg, proj, proj, proj, up, o, lse, low_t, *riders)


def bounds(seg, bq, bk):
    row = seg[0]
    first = jnp.sum(row[None, :] < row[::bq][:, None], axis=1) // GRAIN
    last = (jnp.sum(row[None, :] <= row[bk - 1::bk][:, None], axis=1) + GRAIN - 1) // GRAIN
    return first.astype(jnp.int32), last.astype(jnp.int32)


def gelu_pair(u):
    c = 0.7978845608028654
    square = u * u
    t = jnp.tanh(u * (c + (c * 0.044715) * square))
    half = 0.5 * t + 0.5
    slope = half + (0.5 * u) * (1.0 - t * t) * (c + (3 * c * 0.044715) * square)
    return u * half, slope


def row_stats(values):
    mean = jnp.mean(values, axis=-1, keepdims=True)
    centred = values - mean
    return mean, lax.rsqrt(jnp.mean(centred * centred, axis=-1, keepdims=True) + epsilon)


def norm_back(values, gain, upstream):
    mean, rate = row_stats(values)
    unit = (values - mean) * rate
    inner = upstream * gain
    level = jnp.mean(inner, axis=-1, keepdims=True)
    along = jnp.mean(inner * unit, axis=-1, keepdims=True)
    return rate * (inner - level - unit * along)


def shard_at(place, core_rel, q_rel):
    core, q = place[0] ^ core_rel, place[1] ^ q_rel
    return ((q >> 1) * 2 + core) * 2 + (q & 1)


def cut(place, grad, keep, send, first):
    half = grad.shape[0] // 2
    for at in range(grad.shape[1] // PART):
        columns = slice(at * PART, (at + 1) * PART)
        if len(keep.shape) == 3:
            keep[first + at] = grad[:half, columns].astype(keep.dtype)
            send[first + at] = grad[half:, columns].astype(send.dtype)
        else:
            chips, rows = keep.shape[1:3]
            for rel, target in enumerate((keep, send)):
                for q in range(chips):
                    source = pl.ds(pl.multiple_of(shard_at(place, rel, q) * rows, 8), rows)
                    target[first + at, q] = grad[source, columns].astype(target.dtype)


def before_kernel(place, x_ref, gain_ref, w_ref, *refs, shards, block):
    proj_ref, low_t_ref, low = refs[-3:]
    length, width = x_ref.shape

    @pl.when(pl.program_id(0) == 0)
    def _():
        for at in range(0, length, block):
            at = slice(at, at + block)
            values = x_ref[at, :].astype(jnp.float32)
            mean, rate = row_stats(values)
            normed = ((values - mean) * rate * gain_ref[...]).astype(jnp.bfloat16)
            low[at, :] = normed
            low_t_ref[:, at] = jnp.transpose(normed)

    proj_ref[...] = mm(low[...], w_ref[...]).astype(jnp.bfloat16)


def before(place, x, gain, w, shards, so_far=(), chunk=768, block=256):
    length, width = x.shape
    columns = w.shape[1]
    whole = lambda *shape: pl.BlockSpec(shape, lambda c, *_: (0, 0), pipeline_mode=pl.Buffered(1))
    grid_spec = pltpu.PrefetchScalarGridSpec(
        num_scalar_prefetch=1,
        grid=(columns // chunk,),
        in_specs=[whole(length, width), whole(1, width), pl.BlockSpec((width, chunk), lambda c, *_: (0, c))]
        + [pl.BlockSpec(memory_space=pl.ANY)] * len(so_far),
        out_specs=[
            pl.BlockSpec((length, chunk), lambda c, place: (place[2], c)),
            pl.BlockSpec((width, length), lambda c, place: (0, place[2])),
        ],
        scratch_shapes=[pltpu.VMEM((length, width), jnp.bfloat16)],
    )
    return pl.pallas_call(
        functools.partial(before_kernel, shards=shards, block=block),
        grid_spec=grid_spec,
        out_shape=[
            jax.ShapeDtypeStruct((2 * length, columns), jnp.bfloat16),
            jax.ShapeDtypeStruct((width, 2 * length), jnp.bfloat16),
        ],
        input_output_aliases={4 + at: at for at in range(len(so_far))},
        compiler_params=pltpu.CompilerParams(vmem_limit_bytes=60 << 20),
        cost_estimate=pl.CostEstimate(flops=2 * length * width * columns, bytes_accessed=12 << 20, transcendentals=length),
        name="before",
    )(place, x, gain, w, *so_far)


def middle_kernel(place, x_kept, x_other, o_ref, gy_kept, gy_other, w_out_ref, gain_ref, w_up_ref, w_down_ref,
                  out_kept, out_other, gx_ref, go_ref, keep_up, send_up, keep_down, send_down, keep_out, send_out,
                  gy, x1, low, low_t, total, back, whole, part, *, shards, block):
    c = pl.program_id(0)
    length, width = o_ref.shape
    chunk = w_down_ref.shape[0]
    pieces = [slice(at, at + block) for at in range(0, length, block)]
    rows = width // shards
    half, window = width // 2, length // 2
    kept = pl.ds(pl.multiple_of(place[2] * window, window), window)
    other = pl.ds(pl.multiple_of((1 - place[2]) * window, window), window)

    @pl.when(c == 0)
    def _():
        gy[kept, :] = gy_kept[...]
        gy[other, :] = gy_other[...]
        x1[kept, :] = x_kept[...].astype(jnp.float32)
        x1[other, :] = x_other[...].astype(jnp.float32)
        for at in pieces:
            values = x1[at, :] + mm(o_ref[at, :], w_out_ref[...])
            x1[at, :] = values
            mean, rate = row_stats(values)
            normed = ((values - mean) * rate * gain_ref[...]).astype(jnp.bfloat16)
            low[at, :] = normed
            low_t[:, at] = jnp.transpose(normed)
            total[at, :] = values
            back[at, :] = jnp.zeros_like(values)

    lifted, slopes = [], []
    for at in pieces:
        a, slope = gelu_pair(mm(low[at, :], w_up_ref[...]))
        a = a.astype(jnp.bfloat16)
        gu = (mm(gy[at, :], w_down_ref[...], NT) * slope).astype(jnp.bfloat16)
        total[at, :] += mm(a, w_down_ref[...])
        back[at, :] += mm(gu, w_up_ref[...], NT)
        lifted.append(jnp.transpose(a))
        slopes.append(gu)
    whole[...] = mm(low_t[...], jnp.concatenate(slopes, axis=0))
    cut(place, whole, keep_up, send_up, 0)
    grad_down = mm(jnp.concatenate(lifted, axis=1), gy[...])
    if rows % 8:
        for at in range(width // PART):
            for target, begin in ((keep_down, 0), (send_down, chunk // 2)):
                piece = grad_down[begin:begin + chunk // 2, at * PART:(at + 1) * PART]
                target[at] = piece.astype(jnp.bfloat16)
    else:
        part[...] = grad_down
        for rel, target in enumerate((keep_down, send_down)):
            for q_rel in range(4):
                q = (place[1] ^ q_rel) & 3
                source = (((q >> 1) * 2 + (place[0] ^ rel)) * 2 + (q & 1)) * 4 * rows
                for sub in range(4):
                    source_rows = pl.ds(pl.multiple_of(source + sub * rows, 8), rows)
                    for at in range(width // PART):
                        piece = part[source_rows, at * PART:(at + 1) * PART]
                        target[4 * at + sub, q_rel] = piece.astype(jnp.bfloat16)

    @pl.when(c == pl.num_programs(0) - 1)
    def _():
        branch = []
        out_kept[...] = total[kept, :].astype(jnp.bfloat16)
        out_other[...] = total[other, :].astype(jnp.bfloat16)
        for at in pieces:
            grad = gy[at, :].astype(jnp.float32) + norm_back(x1[at, :], gain_ref[...], back[at, :])
            grad = grad.astype(jnp.bfloat16)
            gx_ref[at, :] = grad
            branch.append(grad)
            go_ref[at, :] = mm(grad, w_out_ref[...], NT).astype(jnp.bfloat16)
            low_t[:, at] = jnp.transpose(o_ref[at, :])
        whole[...] = mm(low_t[...], jnp.concatenate(branch, axis=0))
        cut(place, whole, keep_out, send_out, 0)


def middle(place, x, o, gy, w_out, gain, w_up, w_down, shards, block=512):
    length, width = o.shape
    lift = w_up.shape[1]
    steps = 4
    chunk = lift // steps
    half, window = width // 2, length // 2
    at = (lambda c, place: c) if (width // shards) % 8 else (lambda c, place: c ^ (place[1] >> 2))
    whole = lambda *shape: pl.BlockSpec(shape, lambda c, *_: (0, 0), pipeline_mode=pl.Buffered(1))
    out = lambda *shape: pl.BlockSpec(shape, lambda c, *_: (0,) * len(shape), pipeline_mode=pl.Buffered(1))
    shape = jax.ShapeDtypeStruct
    rows = width // shards
    if rows % 8:
        up_shape, down_shape, out_shape = (lift // PART, half, PART), (width // PART, lift // 2, PART), (width // PART, half, PART)
        up = pl.BlockSpec((chunk // PART, half, PART), lambda c, place: (at(c, place), 0, 0))
        down = pl.BlockSpec((width // PART, chunk // 2, PART), lambda c, place: (0, c, 0))
    else:
        piece = (shards // 2, rows, PART)
        up_shape, down_shape, out_shape = (lift // PART, *piece), (lift // PART, *piece), (width // PART, *piece)
        up = pl.BlockSpec((chunk // PART, *piece), lambda c, place: (at(c, place), 0, 0, 0))
        down = pl.BlockSpec((lift // PART, 4, rows, PART), lambda c, place: (0, c, 0, 0))
    bf16 = jnp.bfloat16
    grid_spec = pltpu.PrefetchScalarGridSpec(
        num_scalar_prefetch=1,
        grid=(steps,),
        in_specs=[
            whole(window, width), whole(window, width), whole(length, width), whole(window, width),
            whole(window, width), whole(width, width), whole(1, width),
            pl.BlockSpec((width, chunk), lambda c, place: (0, at(c, place))),
            pl.BlockSpec((chunk, width), lambda c, place: (at(c, place), 0)),
        ],
        out_specs=[
            out(window, width), out(window, width), out(length, width), out(length, width), up, up, down, down,
            out(*out_shape), out(*out_shape),
        ],
        scratch_shapes=[
            pltpu.VMEM((length, width), bf16),
            pltpu.VMEM((length, width), jnp.float32),
            pltpu.VMEM((length, width), bf16),
            pltpu.VMEM((width, length), bf16),
            pltpu.VMEM((length, width), jnp.float32),
            pltpu.VMEM((length, width), jnp.float32),
            pltpu.VMEM((width, width), jnp.float32),
            pltpu.VMEM((chunk, width), jnp.float32),
        ],
    )
    return pl.pallas_call(
        functools.partial(middle_kernel, shards=shards, block=block),
        grid_spec=grid_spec,
        out_shape=[
            shape((window, width), bf16), shape((window, width), bf16),
            shape((length, width), bf16), shape((length, width), bf16),
            *[shape(size, bf16) for size in (up_shape, up_shape, down_shape, down_shape, out_shape, out_shape)],
        ],
        compiler_params=pltpu.CompilerParams(vmem_limit_bytes=60 << 20),
        cost_estimate=pl.CostEstimate(flops=12 * length * width * lift, bytes_accessed=40 << 20, transcendentals=length * lift),
        name="middle",
    )(place, *x, o, *gy, w_out, gain, w_up, w_down)


def after_kernel(place, x_ref, gain_ref, gx_ref, w_ref, *refs):
    out_ref = refs[-1]
    grads = jnp.concatenate([ref[...] for third in range(3) for ref in refs[third:-1:3]], axis=1)
    back = mm(grads, w_ref[...], NT)
    values = x_ref[...].astype(jnp.float32)
    out_ref[...] = (gx_ref[...].astype(jnp.float32) + norm_back(values, gain_ref[...], back)).astype(out_ref.dtype)


def after(place, x, gain, gx, w, pieces, block=256):
    length, width = x.shape
    steps = length // block
    rows = lambda columns: pl.BlockSpec((block, columns), lambda i, place: (place[2] * steps + i, 0))
    own = pl.BlockSpec((block, width), lambda i, place: (i, 0))
    whole = lambda *shape: pl.BlockSpec(shape, lambda i, place: (0, 0), pipeline_mode=pl.Buffered(1))
    grid_spec = pltpu.PrefetchScalarGridSpec(
        num_scalar_prefetch=1,
        grid=(steps,),
        in_specs=[own, whole(1, width), rows(width), whole(width, w.shape[1])] + [rows(piece.shape[1]) for piece in pieces],
        out_specs=own,
    )
    return pl.pallas_call(
        after_kernel,
        grid_spec=grid_spec,
        out_shape=jax.ShapeDtypeStruct((length, width), jnp.bfloat16),
        compiler_params=pltpu.CompilerParams(vmem_limit_bytes=60 << 20),
        cost_estimate=pl.CostEstimate(flops=6 * length * width * width, bytes_accessed=16 << 20, transcendentals=length),
        name="after",
    )(place, x, gain, gx, w, *pieces)


def swapped(block):
    return lax.ppermute(block, "seq", [(0, 1), (1, 0)])


def split_window(block):
    place = lax.axis_index("seq")
    take = lambda at: lax.dynamic_index_in_dim(block, at, 0, keepdims=False)
    return take(place), take(1 - place)


def joined(kept, other):
    place = lax.axis_index("seq")
    return jnp.where(place == 0, jnp.stack([kept, other]), jnp.stack([other, kept]))


def crossed(block, bits):
    step = sum(1 if bit == 0 else 2 if bit == -1 else 2 << bit for bit in bits)
    count = 2 * lax.axis_size("dp")
    return lax.ppermute(block, ("dp", "seq"), [(i, i ^ step) for i in range(count)])


def masks_of(bits):
    return [tuple(bit for e, bit in enumerate(bits) if number >> e & 1) for number in range(1, 1 << len(bits))]


def combine_kernel(*refs, work, steps):
    for lead, cut_up, targets in work:
        def one(index, carry):
            for target, offset, count, sources in targets:
                for at, terms in enumerate(sources):
                    total = None
                    for ref, begin, per, place in terms:
                        where = (index, *place) if per is None else (begin + index * per + place,)
                        value = refs[ref][where].astype(jnp.float32)
                        total = value if total is None else total + value
                    refs[target][offset + index * count + at] = total.astype(refs[target].dtype)
            return carry

        count = lead // steps if cut_up else lead

        def all_of(count=count, one=one):
            if sum(len(sources) for _, _, _, sources in targets) > 32:
                lax.fori_loop(0, count, one, 0)
            else:
                for index in range(count):
                    one(index, 0)

        if cut_up:
            all_of()
        elif steps > 1:
            @pl.when(pl.program_id(0) == 0)
            def _():
                all_of()
        else:
            all_of()


class Flow:
    def __init__(self, place, keep, send, chips, plan, blocks=0):
        if keep.ndim == 3:
            index = jnp.stack([shard_at(place, rel, q) for rel in range(2) for q in range(chips)])
            lead, half, columns = keep.shape
            both = jnp.stack([array.reshape(lead, max(blocks, 1), -1, columns) for array in (keep, send)], axis=2)
            parts = max(blocks, 1)
            both = both.reshape(lead, 2 * chips, parts, -1, columns)[:, index].transpose(0, 2, 1, 3, 4)
            both = both.reshape(lead * parts, 2 * chips, -1, columns)
            keep, send = both[:, :chips], both[:, chips:]
        self.lead, _, self.rows, self.columns = keep.shape
        self.left = list(reversed(range(chips.bit_length() - 1)))
        self.plan = list(plan)
        self.terms = [(keep.reshape(-1, self.rows, self.columns), list(self.left), None)]
        self.first = send.reshape(-1, self.rows, self.columns)


class Operands:
    def __init__(self):
        self.arrays, self.specs, self.seen = [], [], {}

    def add(self, array, spec):
        self.arrays.append(array)
        self.specs.append(spec)
        return len(self.arrays) - 1

    def finder(self, flow, term, fixed, cut_up):
        array, bits, offset = term
        if offset is not None:
            if id(array) not in self.seen:
                self.seen[id(array)] = self.add(array, pl.BlockSpec(array.shape, lambda i: (0, 0, 0), pipeline_mode=pl.Buffered(1)))
            ref, per = self.seen[id(array)], 1 << len(bits)
            return lambda value: (ref, offset, per, sum(value[bit] << (len(bits) - 1 - at) for at, bit in enumerate(bits)))
        view = array.reshape(flow.lead, *(2,) * len(bits), flow.rows, flow.columns)
        block = (flow.lead // cut_up if cut_up else flow.lead, *[1 if bit in fixed else 2 for bit in bits], flow.rows, flow.columns)
        index = tuple(fixed.get(bit, 0) for bit in bits)
        mode = {} if cut_up else dict(pipeline_mode=pl.Buffered(1))
        ref = self.add(view, pl.BlockSpec(block, lambda i: (i if cut_up else 0, *index, 0, 0), **mode))
        return lambda value: (ref, 0, None, tuple(0 if bit in fixed else value[bit] for bit in bits))


def combine(flows, steps):
    operands, plans, sizes = Operands(), [], {}
    for flow in flows:
        bits = flow.plan.pop(0)
        rest = [bit for bit in flow.left if bit not in bits]
        cut_up = steps if steps > 1 and flow.lead % steps == 0 else 0
        gone = {bit: 0 for bit in range(64) if bit not in flow.left}
        fixed = {**gone, bits[0]: 1} if len(bits) == 1 else gone
        finders = [operands.finder(flow, term, fixed, cut_up) for term in flow.terms]
        plans.append((flow, bits, rest, cut_up, gone, finders))
        for mask in masks_of(bits):
            size = flow.lead << len(rest)
            key = mask if steps == 1 else (mask, id(flow))
            sizes.setdefault(key, []).append((flow, size, cut_up and size // cut_up, mask))
    outputs, out_specs = [], []
    for members in sizes.values():
        shape = (sum(size for _, size, _, _ in members), members[0][0].rows, members[0][0].columns)
        outputs.append(jax.ShapeDtypeStruct(shape, jnp.bfloat16))
        cut = members[0][2]
        out_specs.append(
            pl.BlockSpec((cut, *shape[1:]), lambda i: (i, 0, 0)) if cut
            else pl.BlockSpec(shape, lambda i: (0, 0, 0), pipeline_mode=pl.Buffered(1))
        )
    work = []
    for flow, bits, rest, cut_up, gone, finders in plans:
        targets = []
        for number, members in enumerate(sizes.values()):
            offset = 0
            for member, size, _, mask in members:
                if member is flow:
                    sources = []
                    for at in range(1 << len(rest)):
                        value = {bit: (at >> (len(rest) - 1 - e)) & 1 for e, bit in enumerate(rest)}
                        value.update(gone)
                        value.update({bit: int(bit in mask) for bit in bits})
                        sources.append([find(value) for find in finders])
                    targets.append((len(operands.arrays) + number, offset, 1 << len(rest), sources))
                offset += size
        work.append((flow.lead, cut_up, targets))
        flow.left = rest
    results = pl.pallas_call(
        functools.partial(combine_kernel, work=work, steps=steps),
        grid=(steps,),
        in_specs=operands.specs,
        out_specs=out_specs,
        out_shape=outputs,
        compiler_params=pltpu.CompilerParams(vmem_limit_bytes=60 << 20),
        cost_estimate=pl.CostEstimate(flops=1 << 20, bytes_accessed=8 << 20, transcendentals=0),
        name="combine",
    )(*operands.arrays)
    return [
        (members[0][3], array, [(flow, size) for flow, size, _, _ in members])
        for members, array in zip(sizes.values(), results)
    ]


def leave(flows, value=None, steps=1):
    flows = [flow for flow in flows if flow.plan]
    starting = [flow for flow in flows if flow.plan[0] == (-1,)]
    waiting = [flow for flow in flows if flow.plan[0] == ()]
    going = [flow for flow in flows if flow not in starting and flow not in waiting]
    for flow in starting + waiting:
        flow.plan.pop(0)
    sent = combine(going, steps) if going else []
    sent += [((-1,), flow.first, [(flow, flow.first.shape[0])]) for flow in starting]
    value, arrays = lax.optimization_barrier((value, [array for _, array, _ in sent]))
    return value, [(crossed(array, mask), members) for array, (mask, _, members) in zip(arrays, sent)]


def arrive(transfers, value=None):
    moved, value = lax.optimization_barrier(([array for array, _ in transfers], value))
    for array, (_, members) in zip(moved, transfers):
        at = 0
        for flow, size in members:
            flow.terms.append((array, list(flow.left), at if len(members) > 1 else None))
            at += size
    return value


def finish_kernel(*refs, work, gains, count):
    inputs, outputs = refs[:count], refs[count:]
    for terms, targets in work:
        for lead, (target, row, column, width, parts) in enumerate(targets):
            total = None
            for ref, begin, per, place in terms:
                where = (lead, *place) if per is None else (begin + lead * per + place,)
                value = inputs[ref][where].astype(jnp.float32)
                total = value if total is None else total + value
            for part in range(parts):
                piece = slice(part * width, (part + 1) * width)
                begin = column + part * (outputs[target].shape[1] // parts if parts > 1 else 0)
                outputs[target][row:row + total.shape[0], begin:begin + width] = total[:, piece]
    for source, weight, gain, target in gains:
        product = inputs[weight][...] * outputs[source][...]
        sums = lax.dot_general(jnp.ones((8, product.shape[1]), jnp.float32), product, NT,
                               precision=lax.Precision.HIGHEST, preferred_element_type=jnp.float32)
        outputs[target][...] = sums[:1] / inputs[gain][...]


def finish(plans, sizes, gained):
    operands, work, gains = Operands(), [], []
    gone = {bit: 0 for bit in range(64)}
    for flow, targets in plans:
        finders = [operands.finder(flow, term, gone, False) for term in flow.terms]
        work.append(([find(gone) for find in finders], targets))
    sizes = list(sizes)
    for source, *arrays in gained:
        at = [operands.add(array, pl.BlockSpec(array.shape, lambda i: (0, 0), pipeline_mode=pl.Buffered(1))) for array in arrays]
        gains.append((source, *at, len(sizes)))
        sizes.append((1, sizes[source][0]))
    return pl.pallas_call(
        functools.partial(finish_kernel, work=work, gains=gains, count=len(operands.arrays)),
        grid=(1,),
        in_specs=operands.specs,
        out_specs=[pl.BlockSpec(size, lambda i: (0, 0), pipeline_mode=pl.Buffered(1)) for size in sizes],
        out_shape=[jax.ShapeDtypeStruct(size, jnp.float32) for size in sizes],
        compiler_params=pltpu.CompilerParams(vmem_limit_bytes=60 << 20),
        cost_estimate=pl.CostEstimate(flops=1 << 20, bytes_accessed=4 << 20, transcendentals=0),
        name="finish",
    )(*operands.arrays)


def body(tokens, segments, cotangent, gain_attn, w_qkv, w_out, gain_ffn, w_up, w_down):
    chips = lax.axis_size("dp")
    shards = 2 * chips
    dp, seq = lax.axis_index("dp"), lax.axis_index("seq")
    here = jnp.stack([dp & 1, (dp >> 1) * 2 + seq, seq]).astype(jnp.int32)
    there = jnp.stack([dp & 1, (dp >> 1) * 2 + seq, 1 - seq]).astype(jnp.int32)
    far = tuple(range(2, chips.bit_length() - 1))
    rest = [far[at:at + 2] for at in range(2, len(far), 2)]

    x_kept, x_sent = split_window(tokens)
    segments, cotangent, x_sent = lax.optimization_barrier((segments, cotangent, x_sent))
    seg_kept, seg_sent = split_window(segments)
    gy_kept, gy_sent = split_window(cotangent)
    x_other, seg_other, gy_other = swapped(x_sent), swapped(seg_sent), swapped(gy_sent)
    seg = jnp.where(seq == 0, jnp.concatenate([seg_kept, seg_other]), jnp.concatenate([seg_other, seg_kept]))[None]
    first, last = bounds(seg, 256, 256)
    gain_one, gain_two = gain_attn[None], gain_ffn[None]
    begin = shard_at(here, 0, 0) * (w_out.shape[0] // shards)
    shard_of = lambda array: lax.dynamic_slice_in_dim(array, begin, w_out.shape[0] // shards, 0).astype(jnp.float32)
    weights = [shard_of(w_qkv), shard_of(gain_attn)[None], shard_of(w_up), shard_of(gain_ffn)[None]]
    x_other, weights = lax.optimization_barrier((x_other, weights))
    early = before(here, x_kept, gain_one, w_qkv, shards)
    proj, low_t = before(there, x_other, gain_one, w_qkv, shards, early)
    mixture, lse = attend(first, seg, proj)
    out_kept, out_sent, gx, go, keep_up, send_up, keep_down, send_down, keep_out, send_out = middle(
        here, (x_kept, x_other), mixture, (gy_kept, gy_other), w_out, gain_two, w_up, w_down, shards
    )

    core, near = (-1,), [(bit,) for bit in far]
    up = Flow(here, keep_up, send_up, chips, [core, (1,), (0,), *near])
    down = Flow(here, keep_down, send_down, chips, [core, *near[:1], (1,), *near[1:2], (), (0,), *near[2:]], 4)
    heads = []

    def heads_back(begin, count, plan, riders=()):
        *grads, keep, send = attend_back(begin, count, last, here, seg, proj, go, mixture, lse, low_t, shards, riders)
        heads.append(grads)
        return Flow(here, keep, send, chips, [core, *plan])

    (go, out_sent), moving = leave([up, down], (go, out_sent))
    out_other = swapped(out_sent)
    one = heads_back(0, 2, [*near[:1], (0,), (1,), *near[1:]], (keep_out, send_out))
    out_other = arrive(moving, out_other)
    (go, out_other), moving = leave([up, down, one], (go, out_other), 2)
    two = heads_back(2, 3, [(1,), *near[:1], (0, *far[1:2]), *rest])
    arrive(moving)
    go, moving = leave([up, down, one, two], go, 2)
    three = heads_back(5, 1, [(1, *far[:1]), (0, *far[1:2]), *rest])
    arrive(moving)
    flows = [up, down, one, two, three]
    gx, moving = leave(flows, gx)
    pieces = [piece for grads in heads for piece in grads]
    other_rows = after(there, x_other, gain_one, gx, w_qkv, pieces)
    other_rows = arrive(moving, other_rows)
    rows_back = swapped(other_rows)
    gx, moving = leave(flows, gx)
    kept_rows = after(here, x_kept, gain_one, gx, w_qkv, pieces)
    kept_rows = arrive(moving, kept_rows)
    rows, width = up.rows, w_out.shape[1]
    w_qkv_rows, gain_one_rows, w_up_rows, gain_two_rows = weights

    def finish_up(w_rows):
        whole = [(0, 0, lead * PART, PART, 1) for lead in range(up.lead)]
        return finish([(up, whole)], [(rows, up.lead * PART)], [(0, w_rows, gain_two_rows)])

    soon = not up.plan
    (kept_rows, out_other, w_up_rows), moving = leave(flows, (kept_rows, out_other, w_up_rows))
    up_grads = finish_up(w_up_rows) if soon else None
    grad_tokens, outputs = joined(kept_rows, rows_back), joined(out_kept, out_other)
    while True:
        up_grads, grad_tokens, outputs = arrive(moving, (up_grads, grad_tokens, outputs))
        if not any(flow.plan for flow in flows):
            break
        _, moving = leave(flows)
    grad_up, grad_gain_ffn = up_grads or finish_up(w_up_rows)
    out_lead, group = width // PART, iter(range(64))
    of_group = lambda flow, extra=0: [(0, 0, next(group) * SMALL, SMALL, 3) for _ in range(flow.lead - extra)]
    grad_qkv, grad_out, grad_down, grad_gain_attn = finish([
        (one, of_group(one, out_lead) + [(1, 0, lead * PART, PART, 1) for lead in range(out_lead)]),
        (two, of_group(two)),
        (three, of_group(three)),
        (down, [(2, (lead % 4) * rows, (lead // 4) * PART, PART, 1) for lead in range(down.lead)]),
    ], [(rows, 3 * width), (rows, width), (4 * rows, width)], [(0, w_qkv_rows, gain_one_rows)])
    return (
        outputs,
        grad_tokens,
        grad_qkv,
        grad_out,
        grad_up,
        grad_down,
        grad_gain_attn[0],
        grad_gain_ffn[0],
    )


def solution(mesh):
    placed = (
        P("dp", "seq", None),
        P("dp", "seq"),
        P("dp", "seq", None),
        P(),
        P(),
        P(),
        P(),
        P(),
        P(),
    )
    return jax.shard_map(
        body,
        mesh=mesh,
        in_specs=placed,
        out_specs=(
            P("dp", "seq", None),
            P("dp", "seq", None),
            P(("dp", "seq"), None),
            P(("dp", "seq"), None),
            P(("dp", "seq"), None),
            P(("dp", "seq"), None),
            P(("dp", "seq")),
            P(("dp", "seq")),
        ),
        check_vma=False,
    )
```
